32 devices in a mesh: dp: 2 (over x), ctx: 16 (over z, y, core).
Axes of the slice: x: 2, y: 2, z: 4, core: 2. Of those that a mesh axis runs over, the one named last changes fastest.
Arguments:
- positions: int32 [2, 2048], P('dp', 'ctx'), may hold values from 0 to 2047, as said below
- queries: bfloat16 [2, 2048, 2, 576], P('dp', 'ctx'), may hold values from -12 to 12
- latent: bfloat16 [2, 2048, 576], P('dp', 'ctx'), may hold values from -6 to 6
- out_grad: bfloat16 [2, 2048, 2, 128], P('dp', 'ctx'), may hold values from -6 to 6
- attn_out: bfloat16 [2, 2048, 2, 512], P('dp', 'ctx'), may hold values from -2 to 2
- wuv: bfloat16 [2, 512, 128], replicated, may hold values from -0.25 to 0.25
Outputs:
- grad_queries: bfloat16 [2, 2048, 2, 576], P('dp', 'ctx')
- grad_latent: bfloat16 [2, 2048, 576], P('dp', 'ctx')
- grad_wuv: float32 [2, 512, 128], replicated
The draws below stay inside these ranges and needn't reach their ends.
Inputs may be any that keep to these rules, and one draw needn't show every extreme that they name: Each sequence's rows hold every position 0 to 2047 once. The rows of one index of ctx are 16 blocks of 8 consecutive positions in rising order; block s lies in positions s * 128 to (s + 1) * 128 - 1.
All inputs are finite; a program needn't handle non-finite values.
Results may differ from the reference program's by a relative error of at most 0.0085.
Values may be sent and summed in bfloat16 or wider, within the bound.
No kernel may reach another device: no remote copies, remote signals or barrier semaphores. Data moves between devices by JAX's collectives and lax.ppermute only.
A program may use at most 256 MiB of HBM per device.

```python
import jax
import jax.numpy as jnp
from jax import lax

LATENT = 512
ROPE = 64
HEAD_DIM = 128
HEADS = 2
STRIPES = 16
TOK_DEV = 128
STRETCH = 8
KV = 576
TOKENS = 2048
SEQS = 2
ALL_TOKENS = 4096
N_CTX = 16


def common_latent(key):
    return jax.random.normal(key, (SEQS, TOKENS, KV), jnp.float32)


def draw_positions(key, part):
    key = jax.random.fold_in(key, 7)
    groups = TOKENS // (STRIPES * STRETCH)
    keys = jax.random.split(key, SEQS * STRIPES)
    orders = jax.vmap(lambda k: jax.random.permutation(k, groups))(keys).reshape(SEQS, STRIPES, groups)
    orders = jnp.transpose(orders, (0, 2, 1))
    stripe = jnp.arange(STRIPES, dtype=jnp.int32)[None, None, :, None]
    inner = jnp.arange(STRETCH, dtype=jnp.int32)[None, None, None, :]
    values = (stripe * groups + orders[:, :, :, None].astype(jnp.int32)) * STRETCH + inner
    return values.reshape(SEQS, TOKENS).astype(jnp.int32)


def draw_latent(key, part):
    base = common_latent(key)
    values = jnp.clip(base, -6.0, 6.0)
    return values.astype(jnp.bfloat16)


def draw_queries(key, part):
    key = jax.random.fold_in(key, 5)
    shape = (SEQS, TOKENS, HEADS, KV)
    values = jnp.clip(jax.random.normal(key, shape, jnp.float32), -6.0, 6.0)
    return values.astype(jnp.bfloat16)


def shard_levels(key, shape, pieces, low, largest):
    factor_of = 1.0
    for position, shards_of in pieces:
        draws = jax.random.uniform(jax.random.fold_in(jax.random.fold_in(key, 6), position), (shards_of,), jnp.float32, low / len(pieces), largest / len(pieces))
        factor_of = factor_of * jnp.repeat(jnp.exp(draws), shape[position] // shards_of).reshape((-1,) + (1,) * (len(shape) - 1 - position))
    return factor_of


def gaussian(rng, dims, scale, most, shards=(), held_as=jnp.bfloat16):
    result = scale * jax.random.normal(rng, dims, jnp.float32)
    if shards:
        result = result * shard_levels(rng, dims, shards, -0.22, 0.18)
    return jnp.clip(result, -most, most).astype(held_as)


def setup_inputs(seed: int = 0) -> dict:
    streams_of = jax.random.split(jax.random.key(seed), 7)
    return {
        "positions": draw_positions(jax.random.fold_in(streams_of[6], 71), 0),
        "queries": draw_queries(jax.random.fold_in(streams_of[6], 71), 0),
        "latent": draw_latent(jax.random.fold_in(streams_of[6], 71), 0),
        "out_grad": gaussian(streams_of[3], (SEQS, TOKENS, HEADS, HEAD_DIM), 1.0, 6.0, ((0, 2), (1, 16))),
        "attn_out": gaussian(streams_of[4], (SEQS, TOKENS, HEADS, LATENT), 0.3, 2.0, ((0, 2), (1, 16))),
        "wuv": gaussian(streams_of[5], (HEADS, LATENT, HEAD_DIM), LATENT ** -0.5, 0.25),
    }


def masked_scores(query_rows, key_rows, key_pos, query_pos, factor):
    scores = factor * jnp.dot(query_rows, key_rows.T, preferred_element_type=jnp.float32)
    return jnp.where(key_pos[None, :] <= query_pos[:, None], scores, -1e30)


def reference(positions, queries, latent, out_grad, attn_out, wuv):
    factor = (HEAD_DIM + ROPE) ** -0.5
    rows = STRETCH * HEADS
    span = N_CTX * STRETCH

    def one_sequence(inputs):
        pos, qseq, lat, dout, olat = inputs
        grad_context = jnp.einsum('thd,hld->thl', dout.astype(jnp.float32), wuv.astype(jnp.float32)).astype(jnp.bfloat16)
        delta = jnp.sum(grad_context.astype(jnp.float32) * olat.astype(jnp.float32), axis=-1)
        keys = lat.reshape(N_CTX, STRIPES, STRETCH, KV).transpose(1, 0, 2, 3).reshape(STRIPES, span, KV)
        key_pos = pos.reshape(N_CTX, STRIPES, STRETCH).transpose(1, 0, 2).reshape(STRIPES, span)

        def per_device(total, index):
            start = (index * TOK_DEV).astype(jnp.int32)
            q_rows = lax.dynamic_slice_in_dim(qseq, start, TOK_DEV, 0).reshape(STRIPES, rows, KV)
            g_rows = lax.dynamic_slice_in_dim(grad_context, start, TOK_DEV, 0).reshape(STRIPES, rows, LATENT)
            d_rows = lax.dynamic_slice_in_dim(delta, start, TOK_DEV, 0).reshape(STRIPES, rows)
            p_rows = jnp.repeat(lax.dynamic_slice_in_dim(pos, start, TOK_DEV, 0).reshape(STRIPES, STRETCH), HEADS, axis=1)
            partial_value = jnp.zeros((STRIPES, span, KV), jnp.float32)
            grads = []
            for stripe in range(STRIPES):
                key_rows = keys[:stripe + 1].reshape(-1, KV)
                kpos = key_pos[:stripe + 1].reshape(-1)
                scores = masked_scores(q_rows[stripe], key_rows, kpos, p_rows[stripe], factor)
                top = jnp.max(scores, axis=1, keepdims=True)
                lse = top + jnp.log(jnp.sum(jnp.exp(scores - top), axis=1, keepdims=True))
                prob = jnp.exp(scores - lse)
                grad_prob = jnp.dot(g_rows[stripe], key_rows[:, :LATENT].T, preferred_element_type=jnp.float32)
                grad_score = (prob * (grad_prob - d_rows[stripe][:, None])).astype(jnp.bfloat16)
                grads.append((factor * jnp.dot(grad_score, key_rows, preferred_element_type=jnp.float32)).astype(jnp.bfloat16))
                term = factor * jnp.dot(grad_score.T, q_rows[stripe], preferred_element_type=jnp.float32)
                term = term.at[:, :LATENT].add(jnp.dot(prob.astype(jnp.bfloat16).T, g_rows[stripe], preferred_element_type=jnp.float32))
                partial_value = partial_value.at[:stripe + 1].add(term.reshape(stripe + 1, span, KV))
            rounded = lax.optimization_barrier(partial_value.astype(jnp.bfloat16))
            return total + rounded.astype(jnp.float32), jnp.stack(grads).reshape(TOK_DEV, HEADS, KV)

        total, grad_q = lax.scan(per_device, jnp.zeros((STRIPES, span, KV), jnp.float32), jnp.arange(N_CTX, dtype=jnp.int32))
        grad_lat = total.reshape(STRIPES, N_CTX, STRETCH, KV).transpose(1, 0, 2, 3).reshape(TOKENS, KV)
        return grad_q.reshape(TOKENS, HEADS, KV), grad_lat.astype(jnp.bfloat16)

    grad_queries, grad_latent = lax.map(one_sequence, (positions, queries, latent, out_grad, attn_out))
    grad_wuv = jnp.einsum('sthl,sthd->hld', attn_out.astype(jnp.float32), out_grad.astype(jnp.float32), precision=lax.Precision.HIGHEST) * (ALL_TOKENS ** -0.5)
    return grad_queries, grad_latent, grad_wuv
```

```python
import functools
import math

import jax
import jax.numpy as jnp
from jax import lax
from jax.experimental import pallas as pl
from jax.experimental.pallas import tpu as pltpu
from jax.sharding import PartitionSpec as P

ROPE = 64
HEAD_DIM = 128
GROUP = 4
EXTRA = 16
F32 = jnp.float32
BF16 = jnp.bfloat16
VMEM_LIMIT = 56 * 1024 * 1024


def mm(a, b):
    return jnp.dot(a, b, preferred_element_type=F32)


def mm_t(a, b):
    return lax.dot_general(a, b, (((1,), (1,)), ((), ())), preferred_element_type=F32)


def call(kernel, outs, args, scratch=(), flops=0, nbytes=0, name=None, smem=()):
    specs = [
        pl.BlockSpec(memory_space=pltpu.SMEM if i in smem else pltpu.VMEM) for i in range(len(args))
    ]
    return pl.pallas_call(
        kernel,
        out_shape=[jax.ShapeDtypeStruct(s, d) for s, d in outs],
        in_specs=specs,
        out_specs=[pl.BlockSpec(memory_space=pltpu.VMEM) for _ in outs],
        scratch_shapes=list(scratch),
        compiler_params=pltpu.CompilerParams(vmem_limit_bytes=VMEM_LIMIT),
        cost_estimate=pl.CostEstimate(flops=flops, bytes_accessed=nbytes, transcendentals=0),
        name=name,
    )(*args)


def own_kernel(idx_ref, attn_ref, og_ref, wuv_ref, delta_ref, *rest):
    chunks, term = rest[:GROUP], rest[GROUP]
    heads, lat, tok = attn_ref.shape
    delta_ref[...] = jnp.zeros_like(delta_ref)
    for h in range(heads):
        g = mm(wuv_ref[h], og_ref[h]).astype(BF16).astype(F32)
        delta_ref[h : h + 1, :] = jnp.sum(g * attn_ref[h].astype(F32), axis=0, keepdims=True)
        term[h] = mm_t(attn_ref[h], og_ref[h])
    step = lat // GROUP
    me = lax.rem(idx_ref[0], GROUP)
    for k in range(GROUP):
        at = pl.multiple_of(jnp.bitwise_xor(me, k) * step, step)
        chunks[k][...] = term[:, pl.ds(at, step), :].astype(BF16)


def score_kernel(factor, nkey, width, heads, *refs):
    lat_refs = refs[:nkey]
    q_refs = refs[nkey : nkey + GROUP]
    delta_ref = refs[nkey + GROUP]
    s_ref, k_ref, stat_ref, kt, qt = refs[nkey + GROUP + 1 :]
    wide = kt.shape[0]
    tok = lat_refs[0].shape[1]
    rows = heads * tok
    for a in range(nkey):
        kt[: width + EXTRA, a * tok : (a + 1) * tok] = lat_refs[a][...]
    kt[width + EXTRA :, :] = jnp.zeros((wide - width - EXTRA, nkey * tok), BF16)
    k_ref[...] = kt[...].T
    pos = k_ref[:, width : width + 128 - width % 128].astype(F32)
    key_pos = pos[:, 0:1] * 64.0 + pos[:, 1:2]
    qt[width:, :] = jnp.zeros((wide - width, rows), BF16)
    stat_ref[...] = jnp.zeros_like(stat_ref)
    stat_ref[GROUP * heads : GROUP * heads + heads, :] = delta_ref[:heads, :]
    for j in range(GROUP):
        q_ref = q_refs[j]
        for h in range(heads):
            qt[:width, h * tok : (h + 1) * tok] = q_ref[h * width : (h + 1) * width, :]
        base = q_ref.shape[0] - EXTRA
        qp = q_ref[base:, :].astype(F32)
        one = qp[0:1, :] * 64.0 + qp[1:2, :]
        row_pos = jnp.concatenate([one] * heads, axis=1)
        s = mm(k_ref[...], qt[...]) * factor
        s = jnp.where(key_pos <= row_pos, s, -1e30)
        s_ref[:, j * rows : (j + 1) * rows] = s
        top = jnp.max(s, axis=0, keepdims=True)
        lse = top + jnp.log(jnp.sum(jnp.exp(s - top), axis=0, keepdims=True))
        for h in range(heads):
            stat_ref[j * heads + h : j * heads + h + 1, :] = lse[:, h * tok : (h + 1) * tok]


def context_kernel(width, heads, *refs):
    q_refs = refs[:GROUP]
    k_ref, wuv_ref, g_ref, gp_ref = refs[GROUP:]
    lat = wuv_ref.shape[1]
    tok = q_refs[0].shape[1]
    rows = heads * tok
    for j in range(GROUP):
        for h in range(heads):
            at = heads * width + h * HEAD_DIM
            og = q_refs[j][at : at + HEAD_DIM, :]
            g_ref[:, j * rows + h * tok : j * rows + (h + 1) * tok] = mm(wuv_ref[h], og).astype(BF16)
        cols = slice(j * rows, (j + 1) * rows)
        gp_ref[:, cols] = mm(k_ref[:, :lat], g_ref[:, cols])


def grad_kernel(factor, nkey, width, heads, *refs):
    lat_refs = refs[:nkey]
    q_refs = refs[nkey : nkey + GROUP]
    stats = refs[nkey + GROUP : nkey + 2 * GROUP]
    s_ref, gp_ref, g_ref = refs[nkey + 2 * GROUP : nkey + 2 * GROUP + 3]
    rest = refs[nkey + 2 * GROUP + 3 :]
    gq_refs = rest[:GROUP]
    part_refs = rest[GROUP : GROUP + nkey]
    kt, qt, gs_all, p_all = rest[GROUP + nkey :]
    tok = lat_refs[0].shape[1]
    rows = heads * tok
    lat = g_ref.shape[0]
    for a in range(nkey):
        kt[:, a * tok : (a + 1) * tok] = lat_refs[a][:width, :]
    for j in range(GROUP):
        cols = slice(j * rows, (j + 1) * rows)
        lse_parts = []
        for k in range(GROUP):
            at = (j ^ k) * heads
            lse_parts.append(
                jnp.concatenate([stats[k][at + h : at + h + 1, :] for h in range(heads)], axis=1)
            )
        top = functools.reduce(jnp.maximum, lse_parts)
        lse = top + jnp.log(sum(jnp.exp(part - top) for part in lse_parts))
        at = GROUP * heads
        delta = jnp.concatenate([stats[j][at + h : at + h + 1, :] for h in range(heads)], axis=1)
        p = jnp.exp(s_ref[:, cols] - lse)
        gs = (p * (gp_ref[:, cols] - delta)).astype(BF16)
        p_all[:, cols] = p.astype(BF16)
        gs_all[:, cols] = gs
        gq = (mm(kt[...], gs) * factor).astype(BF16)
        for h in range(heads):
            head_cols = slice(j * rows + h * tok, j * rows + (h + 1) * tok)
            qt[:, head_cols] = q_refs[j][h * width : (h + 1) * width, :]
            gq_refs[j][h] = gq[:, h * tok : (h + 1) * tok]
    for a in range(nkey):
        at = slice(a * tok, (a + 1) * tok)
        gs = gs_all[at, :]
        along = mm_t(qt[...], gs) * factor
        value = mm_t(g_ref[...], p_all[at, :])
        part_refs[a][:lat, :] = (along[:lat] + value).astype(BF16)
        part_refs[a][lat:, :] = along[lat:].astype(BF16)


def spread_kernel(idx_ref, *refs):
    chunks, out_ref = refs[:GROUP], refs[GROUP]
    step = chunks[0].shape[1]
    me = lax.rem(idx_ref[0], GROUP)
    for k in range(GROUP):
        at = pl.multiple_of(jnp.bitwise_xor(me, k) * step, step)
        out_ref[:, pl.ds(at, step), :] = chunks[k][...].astype(F32)


def body(n_ctx, n_dp, positions, queries, latent, out_grad, attn_out, wuv):
    tok, heads, width = queries.shape[1:]
    lat = attn_out.shape[3]
    lines = n_ctx // GROUP
    rows = heads * tok
    all_rows = GROUP * rows
    keys = lines * tok
    wide = -(-(width + EXTRA) // 128) * 128
    factor = (HEAD_DIM + ROPE) ** (-0.5)

    def swap(x, mask):
        return lax.ppermute(x, "ctx", [(i, i ^ mask) for i in range(n_ctx)])

    idx = lax.axis_index("ctx").reshape(1)
    pos = positions
    pos_rows = jnp.concatenate(
        [pos // 64, pos % 64, jnp.zeros((EXTRA - 2, tok), pos.dtype)], axis=0
    ).astype(BF16)
    q_t = jnp.transpose(queries[0], (1, 2, 0))
    og_t = jnp.transpose(out_grad[0], (1, 2, 0))
    attn_t = jnp.transpose(attn_out[0], (1, 2, 0))
    lat_msg = jnp.concatenate([latent[0].T, pos_rows], axis=0)
    q_msg = jnp.concatenate(
        [q_t.reshape(heads * width, tok), og_t.reshape(heads * HEAD_DIM, tok), pos_rows], axis=0
    )
    lats = [lat_msg] + [swap(lat_msg, GROUP * k) for k in range(1, lines)]
    qs = [q_msg] + [swap(q_msg, k) for k in range(1, GROUP)]

    step = lat // GROUP
    delta, *chunks = call(
        own_kernel,
        [((8, tok), F32)] + [((heads, step, HEAD_DIM), BF16)] * GROUP,
        [idx, attn_t, og_t, wuv],
        [pltpu.VMEM((heads, lat, HEAD_DIM), F32)],
        flops=4 * rows * lat * HEAD_DIM,
        nbytes=2 * (attn_t.size + og_t.size + 2 * wuv.size),
        name="own_rows",
        smem=(0,),
    )
    got = [chunks[0]] + [swap(chunks[k], k) for k in range(1, GROUP)]
    scale = 1.0 / math.sqrt(tok * n_ctx * n_dp)
    mine = (sum(c.astype(F32) for c in got) * scale).astype(BF16)
    for bit in range((lines - 1).bit_length()):
        mine = (mine.astype(F32) + swap(mine, GROUP << bit).astype(F32)).astype(BF16)
    for bit in range((n_dp - 1).bit_length()):
        other = lax.ppermute(mine, "dp", [(i, i ^ (1 << bit)) for i in range(n_dp)])
        mine = (mine.astype(F32) + other.astype(F32)).astype(BF16)

    s, k_nat, stat = call(
        functools.partial(score_kernel, factor, lines, width, heads),
        [((keys, all_rows), F32), ((keys, wide), BF16), ((EXTRA, tok), F32)],
        lats + qs + [delta],
        [pltpu.VMEM((wide, keys), BF16), pltpu.VMEM((wide, rows), BF16)],
        flops=2 * keys * all_rows * wide,
        nbytes=4 * keys * all_rows + 2 * keys * wide * 2 + 2 * all_rows * wide,
        name="scores",
    )
    stats = [stat] + [swap(stat, k) for k in range(1, GROUP)]
    g, gp = call(
        functools.partial(context_kernel, width, heads),
        [((lat, all_rows), BF16), ((keys, all_rows), F32)],
        qs + [k_nat, wuv],
        flops=2 * keys * all_rows * lat + 2 * all_rows * lat * HEAD_DIM,
        nbytes=4 * keys * all_rows + 2 * keys * wide + 2 * all_rows * (wide + lat),
        name="context_grads",
    )
    outs = call(
        functools.partial(grad_kernel, factor, lines, width, heads),
        [((heads, width, tok), BF16)] * GROUP + [((width, tok), BF16)] * lines,
        lats + qs + stats + [s, gp, g],
        [
            pltpu.VMEM((width, keys), BF16),
            pltpu.VMEM((width, all_rows), BF16),
            pltpu.VMEM((keys, all_rows), BF16),
            pltpu.VMEM((keys, all_rows), BF16),
        ],
        flops=2 * keys * all_rows * (2 * width + lat),
        nbytes=8 * keys * all_rows + 2 * all_rows * (2 * width + lat) + 4 * keys * width,
        name="gradients",
    )
    gqs, parts = outs[:GROUP], outs[GROUP:]
    parts = [parts[0]] + [swap(parts[k], GROUP * k) for k in range(1, lines)]
    gqs = [gqs[0]] + [swap(gqs[k], k) for k in range(1, GROUP)]
    grad_lat = sum(p.astype(F32) for p in parts).astype(BF16)
    grad_q = sum(p.astype(F32) for p in gqs).astype(BF16)
    pieces = [mine] + [swap(mine, k) for k in range(1, GROUP)]
    (grad_w,) = call(
        spread_kernel, [((heads, lat, HEAD_DIM), F32)], [idx] + pieces, name="spread", smem=(0,)
    )
    return (jnp.transpose(grad_q, (2, 0, 1))[None], grad_lat.T[None], grad_w)


def solution(mesh):
    placed = (
        P("dp", "ctx"),
        P("dp", "ctx", None, None),
        P("dp", "ctx", None),
        P("dp", "ctx", None, None),
        P("dp", "ctx", None, None),
        P(),
    )
    return jax.shard_map(
        functools.partial(body, mesh.shape["ctx"], mesh.shape["dp"]),
        mesh=mesh,
        in_specs=placed,
        out_specs=(P("dp", "ctx", None, None), P("dp", "ctx", None), P()),
        check_vma=False,
    )
```

```python
import functools
import math

import jax
import jax.numpy as jnp
from jax import lax
from jax.experimental import pallas as pl
from jax.experimental.pallas import tpu as pltpu
from jax.sharding import PartitionSpec as P

ROPE = 64
HEAD_DIM = 128
GROUP = 4
EXTRA = 16
F32 = jnp.float32
BF16 = jnp.bfloat16


def mm(a, b):
    return jnp.dot(a, b, preferred_element_type=F32)


def mm_t(a, b):
    return lax.dot_general(a, b, (((1,), (1,)), ((), ())), preferred_element_type=F32)


def size_of(shape, dtype):
    return math.prod(shape) * jnp.dtype(dtype).itemsize


def call(kernel, name, outs, args, scratch=(), flops=0, smem=()):
    specs = [
        pl.BlockSpec(memory_space=pltpu.SMEM if i in smem else pltpu.VMEM) for i in range(len(args))
    ]
    moved = sum(size_of(a.shape, a.dtype) for a in args) + sum(size_of(*o) for o in outs)
    held = moved + sum(size_of(*s) for s in scratch)
    return pl.pallas_call(
        kernel,
        out_shape=[jax.ShapeDtypeStruct(s, d) for s, d in outs],
        in_specs=specs,
        out_specs=[pl.BlockSpec(memory_space=pltpu.VMEM) for _ in outs],
        scratch_shapes=[pltpu.VMEM(s, d) for s, d in scratch],
        compiler_params=pltpu.CompilerParams(vmem_limit_bytes=int(1.2 * held) + (8 << 20)),
        cost_estimate=pl.CostEstimate(flops=flops, bytes_accessed=moved, transcendentals=0),
        name=name,
    )(*args)


def pack_kernel(pos_ref, q_ref, og_ref, lat_ref, lat_msg_ref, msg_ref):
    heads, width, tok = q_ref.shape
    lat_msg_ref[:width, :] = lat_ref[...]
    lat_msg_ref[width:, :] = pos_ref[...]
    for h in range(heads):
        msg_ref[h * width : (h + 1) * width, :] = q_ref[h]
        at = heads * width + h * HEAD_DIM
        msg_ref[at : at + HEAD_DIM, :] = og_ref[:, h, :].T
    msg_ref[heads * (width + HEAD_DIM) :, :] = pos_ref[...]


def own_kernel(width, idx_ref, attn_ref, msg_ref, wuv_ref, delta_ref, *rest):
    chunks, term = rest[:GROUP], rest[GROUP]
    heads, lat, _ = wuv_ref.shape
    delta_ref[...] = jnp.zeros_like(delta_ref)
    for h in range(heads):
        at = heads * width + h * HEAD_DIM
        og = msg_ref[at : at + HEAD_DIM, :]
        attn = attn_ref[:, h, :].T
        g = mm(wuv_ref[h], og).astype(BF16).astype(F32)
        delta_ref[h : h + 1, :] = jnp.sum(g * attn.astype(F32), axis=0, keepdims=True)
        term[h] = mm_t(attn, og)
    step = lat // GROUP
    me = lax.rem(idx_ref[0], GROUP)
    for k in range(GROUP):
        at = pl.multiple_of(jnp.bitwise_xor(me, k) * step, step)
        chunks[k][...] = term[:, pl.ds(at, step), :].astype(BF16)


def score_kernel(factor, nkey, width, heads, *refs):
    lat_refs = refs[:nkey]
    q_refs = refs[nkey : nkey + GROUP]
    delta_ref, s_ref, k_ref, stat_ref, kt, qt = refs[nkey + GROUP :]
    wide = kt.shape[0]
    tok = lat_refs[0].shape[1]
    rows = heads * tok
    for a in range(nkey):
        kt[: width + EXTRA, a * tok : (a + 1) * tok] = lat_refs[a][...]
    kt[width + EXTRA :, :] = jnp.zeros((wide - width - EXTRA, nkey * tok), BF16)
    k_ref[...] = kt[...].T
    pos = k_ref[:, wide - 128 :].astype(F32)
    at = width - (wide - 128)
    key_pos = pos[:, at : at + 1] * 64.0 + pos[:, at + 1 : at + 2]
    qt[width:, :] = jnp.zeros((wide - width, rows), BF16)
    stat_ref[...] = jnp.zeros_like(stat_ref)
    stat_ref[GROUP * heads : GROUP * heads + heads, :] = delta_ref[:heads, :]
    for j in range(GROUP):
        q_ref = q_refs[j]
        for h in range(heads):
            qt[:width, h * tok : (h + 1) * tok] = q_ref[h * width : (h + 1) * width, :]
        base = q_ref.shape[0] - EXTRA
        qp = q_ref[base:, :].astype(F32)
        one = qp[0:1, :] * 64.0 + qp[1:2, :]
        row_pos = jnp.concatenate([one] * heads, axis=1)
        s = mm(k_ref[...], qt[...]) * factor
        s = jnp.where(key_pos <= row_pos, s, -1e30)
        s_ref[:, j * rows : (j + 1) * rows] = s
        top = jnp.max(s, axis=0, keepdims=True)
        lse = top + jnp.log(jnp.sum(jnp.exp(s - top), axis=0, keepdims=True))
        for h in range(heads):
            at = j * heads + h
            stat_ref[at : at + 1, :] = lse[:, h * tok : (h + 1) * tok]


def context_kernel(width, heads, *refs):
    q_refs = refs[:GROUP]
    wuv_ref, k_ref, g_ref, gp_ref = refs[GROUP:]
    lat, all_rows = g_ref.shape
    tok = q_refs[0].shape[1]
    rows = heads * tok
    for j in range(GROUP):
        for h in range(heads):
            at = heads * width + h * HEAD_DIM
            og = q_refs[j][at : at + HEAD_DIM, :]
            col = j * rows + h * tok
            g_ref[:, col : col + tok] = mm(wuv_ref[h], og).astype(BF16)
        cols = slice(j * rows, (j + 1) * rows)
        gp_ref[:, cols] = mm(k_ref[:, :lat], g_ref[:, cols])


def grad_kernel(factor, nkey, width, heads, *refs):
    lat_refs, refs = refs[:nkey], refs[nkey:]
    q_refs, refs = refs[:GROUP], refs[GROUP:]
    stats, refs = refs[:GROUP], refs[GROUP:]
    (s_ref, gp_ref, g_ref), refs = refs[:3], refs[3:]
    part_refs, refs = refs[:nkey], refs[nkey:]
    own_ref, core_ref, across_ref, kt, qt, gs_all, p_all = refs
    tok = q_refs[0].shape[1]
    rows = heads * tok
    lat = g_ref.shape[0]
    for a in range(nkey):
        kt[:, a * tok : (a + 1) * tok] = lat_refs[a][:width, :]
    for j in range(GROUP):
        cols = slice(j * rows, (j + 1) * rows)
        lse_parts = []
        for k in range(GROUP):
            at = (j ^ k) * heads
            lse_parts.append(
                jnp.concatenate([stats[k][at + h : at + h + 1, :] for h in range(heads)], axis=1)
            )
        top = functools.reduce(jnp.maximum, lse_parts)
        lse = top + jnp.log(sum(jnp.exp(part - top) for part in lse_parts))
        at = GROUP * heads
        delta = jnp.concatenate([stats[j][at + h : at + h + 1, :] for h in range(heads)], axis=1)
        p = jnp.exp(s_ref[:, cols] - lse)
        gs = (p * (gp_ref[:, cols] - delta)).astype(BF16)
        gs_all[:, cols] = gs
        p_all[:, cols] = p.astype(BF16)
        gq = (mm(kt[...], gs) * factor).astype(BF16)
        for h in range(heads):
            head_cols = slice(j * rows + h * tok, j * rows + (h + 1) * tok)
            qt[:, head_cols] = q_refs[j][h * width : (h + 1) * width, :]
            part = gq[:, h * tok : (h + 1) * tok]
            if j == 0:
                own_ref[h] = part
            elif j == 2:
                across_ref[h] = part
            else:
                core_ref[j // 2 * heads + h] = part
    for a in range(nkey):
        at = slice(a * tok, (a + 1) * tok)
        along = mm_t(qt[...], gs_all[at, :]) * factor
        value = mm_t(g_ref[...], p_all[at, :])
        part_refs[a][:lat, :] = (along[:lat] + value).astype(BF16)
        part_refs[a][lat:, :] = along[lat:].astype(BF16)


def spread_kernel(idx_ref, *refs):
    chunks, out_ref = refs[:GROUP], refs[GROUP]
    step = chunks[0].shape[1]
    me = lax.rem(idx_ref[0], GROUP)
    for k in range(GROUP):
        at = pl.multiple_of(jnp.bitwise_xor(me, k) * step, step)
        out_ref[:, pl.ds(at, step), :] = chunks[k][...].astype(F32)


def body(n_ctx, n_dp, positions, queries, latent, out_grad, attn_out, wuv):
    tok, heads, width = queries.shape[1:]
    lat = attn_out.shape[3]
    lines = n_ctx // GROUP
    line_bits = (lines - 1).bit_length()
    rows = heads * tok
    all_rows = GROUP * rows
    keys = lines * tok
    wide = -(-(width + EXTRA) // 128) * 128
    factor = (HEAD_DIM + ROPE) ** (-0.5)

    def swap(x, mask):
        return lax.ppermute(x, "ctx", [(i, i ^ mask) for i in range(n_ctx)])

    def after(x, *done):
        return lax.optimization_barrier((x, done))[0]

    idx = lax.axis_index("ctx").reshape(1)
    pos_rows = jnp.concatenate(
        [positions // 64, positions % 64, jnp.zeros((EXTRA - 2, tok), positions.dtype)], axis=0
    ).astype(BF16)
    lat_msg, q_msg = call(
        pack_kernel,
        "pack",
        [((width + EXTRA, tok), BF16), ((heads * (width + HEAD_DIM) + EXTRA, tok), BF16)],
        [pos_rows, jnp.transpose(queries[0], (1, 2, 0)), out_grad[0], latent[0].T],
    )
    held, firsts = {0: lat_msg}, []
    for bit in reversed(range(line_bits)):
        first = swap(lat_msg, GROUP << bit)
        ahead = {m: after(x, first) for m, x in held.items() if m}
        held.update({m | 1 << bit: swap(x, GROUP << bit) for m, x in ahead.items()})
        held[1 << bit] = first
        firsts.append(first)
    lats = [held[m] for m in range(lines)]
    q_across = swap(q_msg, 2)
    q_core = swap(q_msg, 1)
    q_far = swap(after(q_across, q_core), 1)
    qs = [q_msg, q_core, q_across, q_far]

    step = lat // GROUP
    delta, *chunks = call(
        functools.partial(own_kernel, width),
        "own_rows",
        [((8, tok), F32)] + [((heads, step, HEAD_DIM), BF16)] * GROUP,
        [idx, attn_out[0], q_msg, wuv],
        [((heads, lat, HEAD_DIM), F32)],
        flops=4 * rows * lat * HEAD_DIM,
        smem=(0,),
    )
    chunks = after(chunks, *firsts, q_core, q_across)
    got = [chunks[0]] + [swap(chunks[k], k) for k in range(1, GROUP)]
    scale = 1.0 / math.sqrt(tok * n_ctx * n_dp)
    mine = (sum(c.astype(F32) for c in got) * scale).astype(BF16)
    hops = [("ctx", n_ctx, GROUP << bit) for bit in range(line_bits)]
    hops += [("dp", n_dp, 1 << bit) for bit in range((n_dp - 1).bit_length())]

    def climb(total, steps, *done):
        for axis, size, mask in steps:
            other = lax.ppermute(total, axis, [(i, i ^ mask) for i in range(size)])
            other = after(other, *done)
            total = (total.astype(F32) + other.astype(F32)).astype(BF16)
        return total

    s, k_nat, stat = call(
        functools.partial(score_kernel, factor, lines, width, heads),
        "scores",
        [((keys, all_rows), F32), ((keys, wide), BF16), ((EXTRA, tok), F32)],
        lats + qs + [after(delta, mine)],
        [((wide, keys), BF16), ((wide, rows), BF16)],
        flops=2 * keys * all_rows * wide,
    )
    stats = [stat] + [swap(stat, k) for k in range(1, GROUP)]
    mine = climb(mine, hops[:1], stat)
    g, gp = call(
        functools.partial(context_kernel, width, heads),
        "context",
        [((lat, all_rows), BF16), ((keys, all_rows), F32)],
        qs + [wuv, after(k_nat, mine)],
        flops=2 * keys * all_rows * lat + 2 * all_rows * lat * HEAD_DIM,
    )
    mine = climb(mine, hops[1:-1], gp)
    outs = call(
        functools.partial(grad_kernel, factor, lines, width, heads),
        "gradients",
        [((width, tok), BF16)] * lines
        + [((heads, width, tok), BF16), ((2 * heads, width, tok), BF16), ((heads, width, tok), BF16)],
        lats + qs + [after(stats[0], mine)] + stats[1:] + [s, gp, g],
        [
            ((width, keys), BF16),
            ((width, all_rows), BF16),
            ((keys, all_rows), BF16),
            ((keys, all_rows), BF16),
        ],
        flops=2 * keys * all_rows * (2 * width + lat),
    )
    parts, (gq_own, gq_core, gq_across) = list(outs[:lines]), outs[lines:]
    mine = climb(mine, hops[-1:], gq_own)
    kept = [parts[0]]
    for bit in range(line_bits):
        for m in reversed(range(1 << bit, lines, 2 << bit)):
            got_part = swap(parts[m], GROUP << bit)
            target = m ^ 1 << bit
            if target:
                parts[target] = (parts[target].astype(F32) + got_part.astype(F32)).astype(BF16)
            else:
                kept.append(got_part)
    gq_got = swap(gq_core, 1)
    gq_sum = (gq_across.astype(F32) + gq_got[heads:].astype(F32)).astype(BF16)
    gq_last = swap(gq_sum, 2)
    grad_lat = sum(p.astype(F32) for p in kept).astype(BF16)
    grad_q = sum(p.astype(F32) for p in (gq_own, gq_got[:heads], gq_last)).astype(BF16)
    pieces = [mine] + [swap(mine, k) for k in range(1, GROUP)]
    (grad_w,) = call(
        spread_kernel, "spread", [((heads, lat, HEAD_DIM), F32)], [idx] + pieces, smem=(0,)
    )
    return (jnp.transpose(grad_q, (2, 0, 1))[None], grad_lat.T[None], grad_w)


def solution(mesh):
    placed = (
        P("dp", "ctx"),
        P("dp", "ctx", None, None),
        P("dp", "ctx", None),
        P("dp", "ctx", None, None),
        P("dp", "ctx", None, None),
        P(),
    )
    return jax.shard_map(
        functools.partial(body, mesh.shape["ctx"], mesh.shape["dp"]),
        mesh=mesh,
        in_specs=placed,
        out_specs=(P("dp", "ctx", None, None), P("dp", "ctx", None), P()),
        check_vma=False,
    )
```

```python
import functools
import math

import jax
import jax.numpy as jnp
from jax import lax
from jax.experimental import pallas as pl
from jax.experimental.pallas import tpu as pltpu
from jax.sharding import PartitionSpec as P

ROPE = 64
HEAD_DIM = 128
GROUP = 4
EXTRA = 16
PACK_LIMIT = 63 << 20
F32 = jnp.float32
BF16 = jnp.bfloat16


def mm(a, b):
    return jnp.dot(a, b, preferred_element_type=F32)


def mm_t(a, b):
    return lax.dot_general(a, b, (((1,), (1,)), ((), ())), preferred_element_type=F32)


def size_of(shape, dtype):
    return math.prod(shape) * jnp.dtype(dtype).itemsize


def call(kernel, name, outs, args, scratch=(), flops=0, smem=(), hbm=(), copies=0, limit=None):
    def place(i):
        return pltpu.SMEM if i in smem else pltpu.HBM if i in hbm else pltpu.VMEM

    moved = sum(size_of(a.shape, a.dtype) for a in args) + sum(size_of(*o) for o in outs)
    held = moved + sum(size_of(*s) for s in scratch)
    semaphores = [pltpu.SemaphoreType.DMA((copies,))] if copies else []
    return pl.pallas_call(
        kernel,
        out_shape=[jax.ShapeDtypeStruct(s, d) for s, d in outs],
        in_specs=[pl.BlockSpec(memory_space=place(i)) for i in range(len(args))],
        out_specs=[pl.BlockSpec(memory_space=pltpu.VMEM) for _ in outs],
        scratch_shapes=[pltpu.VMEM(s, d) for s, d in scratch] + semaphores,
        compiler_params=pltpu.CompilerParams(vmem_limit_bytes=limit or int(1.2 * held) + (8 << 20)),
        cost_estimate=pl.CostEstimate(flops=flops, bytes_accessed=moved, transcendentals=0),
        name=name,
    )(*args)


def fetch(pairs, sems):
    copies = [pltpu.make_async_copy(src, dst, sems.at[i]) for i, (src, dst) in enumerate(pairs)]
    for copy in copies:
        copy.start()
    return copies


def pack_kernel(
    idx_ref, pos_hbm, q_hbm, og_hbm, lat_hbm, attn_hbm, wuv_hbm,
    lat_msg, q_msg, delta_ref, term_ref,
    pos_ref, og_ref, attn_ref, wuv_ref, term, sems,
):
    heads, width, tok = q_hbm.shape
    pairs = [(pos_hbm, pos_ref), (og_hbm, og_ref), (wuv_hbm, wuv_ref), (attn_hbm, attn_ref)]
    pairs += [(lat_hbm, lat_msg.at[pl.ds(0, width), :])]
    pairs += [(q_hbm.at[h], q_msg.at[pl.ds(h * width, width), :]) for h in range(heads)]
    copies = [pltpu.make_async_copy(src, dst, sems.at[i]) for i, (src, dst) in enumerate(pairs)]
    for copy in copies:
        copy.start()
    copies[0].wait()
    pos = jnp.broadcast_to(pos_ref[...], (EXTRA, tok))
    row = lax.broadcasted_iota(jnp.int32, (EXTRA, tok), 0)
    high = lax.shift_right_logical(pos, 6)
    both = jnp.where(row == 0, high, jnp.where(row == 1, pos - high * 64, 0))
    rows = both.astype(F32).astype(BF16)
    lat_msg[width:, :] = rows
    q_msg[heads * (width + HEAD_DIM) :, :] = rows
    delta_ref[...] = jnp.zeros_like(delta_ref)
    for copy in copies[1:4]:
        copy.wait()
    _, lat, _ = wuv_ref.shape
    for h in range(heads):
        og = og_ref[:, h, :].T
        at = heads * width + h * HEAD_DIM
        q_msg[at : at + HEAD_DIM, :] = og
        attn = attn_ref[:, h, :].T
        g = mm(wuv_ref[h], og).astype(BF16).astype(F32)
        delta_ref[h : h + 1, :] = jnp.sum(g * attn.astype(F32), axis=0, keepdims=True)
        term[h] = mm_t(attn, og)
    step = lat // GROUP
    me = lax.rem(idx_ref[0], GROUP)
    for k in range(GROUP):
        at = pl.multiple_of(jnp.bitwise_xor(me, k) * step, step)
        term_ref[k * heads : (k + 1) * heads] = term[:, pl.ds(at, step), :].astype(BF16)
    for copy in copies[4:]:
        copy.wait()


def score_kernel(factor, nkey, width, heads, *refs):
    lat_refs = refs[:nkey]
    q_refs = refs[nkey : nkey + GROUP]
    delta_ref, s_ref, k_ref, stat_ref, kt, qt = refs[nkey + GROUP :]
    wide = kt.shape[0]
    tok = lat_refs[0].shape[1]
    rows = heads * tok
    for a in range(nkey):
        kt[: width + EXTRA, a * tok : (a + 1) * tok] = lat_refs[a][...]
    kt[width + EXTRA :, :] = jnp.zeros((wide - width - EXTRA, nkey * tok), BF16)
    k_ref[...] = kt[...].T
    pos = k_ref[:, wide - 128 :].astype(F32)
    at = width - (wide - 128)
    key_pos = pos[:, at : at + 1] * 64.0 + pos[:, at + 1 : at + 2]
    qt[width:, :] = jnp.zeros((wide - width, rows), BF16)
    stat_ref[...] = jnp.zeros_like(stat_ref)
    stat_ref[GROUP * heads : GROUP * heads + heads, :] = delta_ref[:heads, :]
    for j in range(GROUP):
        q_ref = q_refs[j]
        for h in range(heads):
            qt[:width, h * tok : (h + 1) * tok] = q_ref[h * width : (h + 1) * width, :]
        base = q_ref.shape[0] - EXTRA
        qp = q_ref[base:, :].astype(F32)
        one = qp[0:1, :] * 64.0 + qp[1:2, :]
        row_pos = jnp.concatenate([one] * heads, axis=1)
        s = mm(k_ref[...], qt[...]) * factor
        s = jnp.where(key_pos <= row_pos, s, -1e30)
        s_ref[:, j * rows : (j + 1) * rows] = s
        top = jnp.max(s, axis=0, keepdims=True)
        lse = top + jnp.log(jnp.sum(jnp.exp(s - top), axis=0, keepdims=True))
        for h in range(heads):
            at = j * heads + h
            stat_ref[at : at + 1, :] = lse[:, h * tok : (h + 1) * tok]


def context_kernel(width, heads, *refs):
    q_refs = refs[:GROUP]
    wuv_ref, k_ref, g_ref, gp_ref = refs[GROUP:]
    lat, all_rows = g_ref.shape
    tok = q_refs[0].shape[1]
    rows = heads * tok
    for j in range(GROUP):
        for h in range(heads):
            at = heads * width + h * HEAD_DIM
            og = q_refs[j][at : at + HEAD_DIM, :]
            col = j * rows + h * tok
            g_ref[:, col : col + tok] = mm(wuv_ref[h], og).astype(BF16)
        cols = slice(j * rows, (j + 1) * rows)
        gp_ref[:, cols] = mm(k_ref[:, :lat], g_ref[:, cols])


def grad_kernel(factor, nkey, width, heads, *refs):
    lat_refs, refs = refs[:nkey], refs[nkey:]
    q_refs, refs = refs[:GROUP], refs[GROUP:]
    stats, refs = refs[:GROUP], refs[GROUP:]
    (s_ref, gp_ref, g_ref), refs = refs[:3], refs[3:]
    part_refs, refs = refs[:nkey], refs[nkey:]
    own_ref, core_ref, across_ref, kt, qt, gs_all, p_all = refs
    tok = q_refs[0].shape[1]
    rows = heads * tok
    lat = g_ref.shape[0]
    for a in range(nkey):
        kt[:, a * tok : (a + 1) * tok] = lat_refs[a][:width, :]
    for j in range(GROUP):
        cols = slice(j * rows, (j + 1) * rows)
        lse_parts = []
        for k in range(GROUP):
            at = (j ^ k) * heads
            lse_parts.append(
                jnp.concatenate([stats[k][at + h : at + h + 1, :] for h in range(heads)], axis=1)
            )
        top = functools.reduce(jnp.maximum, lse_parts)
        lse = top + jnp.log(sum(jnp.exp(part - top) for part in lse_parts))
        at = GROUP * heads
        delta = jnp.concatenate([stats[j][at + h : at + h + 1, :] for h in range(heads)], axis=1)
        p = jnp.exp(s_ref[:, cols] - lse)
        gs = (p * (gp_ref[:, cols] - delta)).astype(BF16)
        gs_all[:, cols] = gs
        p_all[:, cols] = p.astype(BF16)
        gq = (mm(kt[...], gs) * factor).astype(BF16)
        for h in range(heads):
            head_cols = slice(j * rows + h * tok, j * rows + (h + 1) * tok)
            qt[:, head_cols] = q_refs[j][h * width : (h + 1) * width, :]
            part = gq[:, h * tok : (h + 1) * tok]
            if j == 0:
                own_ref[h] = part
            elif j == 2:
                across_ref[h] = part
            else:
                core_ref[j // 2 * heads + h] = part
    for a in range(nkey):
        at = slice(a * tok, (a + 1) * tok)
        along = mm_t(qt[...], gs_all[at, :]) * factor
        value = mm_t(g_ref[...], p_all[at, :])
        part_refs[a][:lat, :] = (along[:lat] + value).astype(BF16)
        part_refs[a][lat:, :] = along[lat:].astype(BF16)


def spread_kernel(scale, idx_ref, *refs):
    chunks, out_ref = refs[:GROUP], refs[GROUP]
    step = chunks[0].shape[1]
    me = lax.rem(idx_ref[0], GROUP)
    for k in range(GROUP):
        at = pl.multiple_of(jnp.bitwise_xor(me, k) * step, step)
        out_ref[:, pl.ds(at, step), :] = chunks[k][...].astype(F32) * scale


def body(n_ctx, n_dp, positions, queries, latent, out_grad, attn_out, wuv):
    tok, heads, width = queries.shape[1:]
    lat = attn_out.shape[3]
    lines = n_ctx // GROUP
    line_bits = (lines - 1).bit_length()
    rows = heads * tok
    all_rows = GROUP * rows
    keys = lines * tok
    wide = -(-(width + EXTRA) // 128) * 128
    factor = (HEAD_DIM + ROPE) ** (-0.5)

    def swap(x, mask):
        return lax.ppermute(x, "ctx", [(i, i ^ mask) for i in range(n_ctx)])

    def after(x, *done):
        return lax.optimization_barrier((x, done))[0]

    idx = lax.axis_index("ctx").reshape(1)
    step = lat // GROUP
    lat_msg, q_msg, delta, term = call(
        pack_kernel,
        "pack",
        [
            ((width + EXTRA, tok), BF16),
            ((heads * (width + HEAD_DIM) + EXTRA, tok), BF16),
            ((8, tok), F32),
            ((GROUP * heads, step, HEAD_DIM), BF16),
        ],
        [
            idx,
            positions,
            jnp.transpose(queries[0], (1, 2, 0)),
            out_grad[0],
            latent[0].T,
            attn_out[0],
            wuv,
        ],
        [
            ((1, tok), jnp.int32),
            (out_grad.shape[1:], BF16),
            (attn_out.shape[1:], BF16),
            (wuv.shape, BF16),
            ((heads, lat, HEAD_DIM), F32),
        ],
        smem=(0,),
        hbm=(1, 2, 3, 4, 5, 6),
        copies=5 + heads,
        limit=PACK_LIMIT,
    )

    def hop(total, axis, size, mask, *done):
        other = lax.ppermute(total, axis, [(i, i ^ mask) for i in range(size)])
        return total, after(other, *done) if done else other

    def add(pair):
        return (pair[0].astype(F32) + pair[1].astype(F32)).astype(BF16)

    dp_hops = [("dp", n_dp, 1 << bit) for bit in range((n_dp - 1).bit_length())]
    line_hops = [("ctx", n_ctx, GROUP << bit) for bit in range(line_bits)]

    firsts = {1 << bit: swap(lat_msg, GROUP << bit) for bit in range(line_bits)}
    q_across = swap(q_msg, 2)
    q_core = swap(q_msg, 1)
    twins = hop(term, *dp_hops[0])
    firsts, q_across, q_core, twins = lax.optimization_barrier((firsts, q_across, q_core, twins))
    for step_hop in dp_hops[1:]:
        twins = hop(add(twins), *step_hop)
    total = add(twins)

    held = {0: lat_msg}
    for bit in reversed(range(line_bits)):
        held.update({m | 1 << bit: swap(x, GROUP << bit) for m, x in held.items() if m})
        held[1 << bit] = firsts[1 << bit]
    lats = [held[m] for m in range(lines)]
    q_far = swap(q_across, 1)
    half = 2 * heads
    got_half = swap(total[half:], 2)
    lats, q_far, got_half = lax.optimization_barrier((lats, q_far, got_half))
    qs = [q_msg, q_core, q_across, q_far]
    total = add((total[:half], got_half))
    got_own = swap(total[heads:], 1)

    s, k_nat, stat = call(
        functools.partial(score_kernel, factor, lines, width, heads),
        "scores",
        [((keys, all_rows), F32), ((keys, wide), BF16), ((EXTRA, tok), F32)],
        lats + qs + [delta],
        [((wide, keys), BF16), ((wide, rows), BF16)],
        flops=2 * keys * all_rows * wide,
    )
    stats = [stat] + [swap(stat, k) for k in range(1, GROUP)]
    mine = add((total[:heads], after(got_own, stat)))
    near = hop(mine, *line_hops[0])
    g, gp = call(
        functools.partial(context_kernel, width, heads),
        "context",
        [((lat, all_rows), BF16), ((keys, all_rows), F32)],
        qs + [wuv, k_nat],
        flops=2 * keys * all_rows * lat + 2 * all_rows * lat * HEAD_DIM,
    )
    mine = add((near[0], after(near[1], gp)))
    mine, stats = lax.optimization_barrier((mine, stats))
    outs = call(
        functools.partial(grad_kernel, factor, lines, width, heads),
        "gradients",
        [((width, tok), BF16)] * lines
        + [((heads, width, tok), BF16), ((2 * heads, width, tok), BF16), ((heads, width, tok), BF16)],
        lats + qs + stats + [s, gp, g],
        [
            ((width, keys), BF16),
            ((width, all_rows), BF16),
            ((keys, all_rows), BF16),
            ((keys, all_rows), BF16),
        ],
        flops=2 * keys * all_rows * (2 * width + lat),
    )
    parts, (gq_own, gq_core, gq_across) = list(outs[:lines]), outs[lines:]
    kept = [parts[0]]
    gq_got = swap(gq_core, 1)
    for step_hop in line_hops[1:]:
        mine = add(hop(after(mine, gq_own), *step_hop))
    for bit in range(line_bits):
        for m in [m for m in range(2 << bit, lines) if m >> bit & 1 and not m & (1 << bit) - 1]:
            parts[m ^ 1 << bit] = add((parts[m ^ 1 << bit], swap(parts[m], GROUP << bit)))
        if bit == 0:
            parts, gq_got, mine = lax.optimization_barrier((parts, gq_got, mine))
    kept += [swap(parts[1 << bit], GROUP << bit) for bit in reversed(range(line_bits))]
    gq_last = swap(add((gq_across, gq_got[heads:])), 2)
    mine_two = jnp.concatenate([mine, swap(mine, 2)], axis=0)
    kept, gq_last, mine_two = lax.optimization_barrier((kept, gq_last, mine_two))
    other_two = swap(mine_two, 1)
    grad_lat = sum(p.astype(F32) for p in kept).astype(BF16)
    grad_q = sum(p.astype(F32) for p in (gq_own, gq_got[:heads], gq_last)).astype(BF16)
    scale = 1.0 / math.sqrt(tok * n_ctx * n_dp)
    pieces = [mine_two[:heads], other_two[:heads], mine_two[heads:], other_two[heads:]]
    (grad_w,) = call(
        functools.partial(spread_kernel, scale), "spread", [((heads, lat, HEAD_DIM), F32)], [idx] + pieces, smem=(0,)
    )
    return (jnp.transpose(grad_q, (2, 0, 1))[None], grad_lat.T[None], grad_w)


def solution(mesh):
    placed = (
        P("dp", "ctx"),
        P("dp", "ctx", None, None),
        P("dp", "ctx", None),
        P("dp", "ctx", None, None),
        P("dp", "ctx", None, None),
        P(),
    )
    return jax.shard_map(
        functools.partial(body, mesh.shape["ctx"], mesh.shape["dp"]),
        mesh=mesh,
        in_specs=placed,
        out_specs=(P("dp", "ctx", None, None), P("dp", "ctx", None), P()),
        check_vma=False,
    )
```

```python
import functools
import math

import jax
import jax.numpy as jnp
from jax import lax
from jax.experimental import pallas as pl
from jax.experimental.pallas import tpu as pltpu
from jax.sharding import PartitionSpec as P

ROPE = 64
HEAD_DIM = 128
GROUP = 4
EXTRA = 16
PACK_LIMIT = 63 << 20
F32 = jnp.float32
BF16 = jnp.bfloat16


def mm(a, b):
    return jnp.dot(a, b, preferred_element_type=F32)


def mm_t(a, b):
    return lax.dot_general(a, b, (((1,), (1,)), ((), ())), preferred_element_type=F32)


def size_of(shape, dtype):
    return math.prod(shape) * jnp.dtype(dtype).itemsize


def call(kernel, name, outs, args, scratch=(), flops=0, smem=(), hbm=(), copies=0, limit=None):
    def place(i):
        return pltpu.SMEM if i in smem else pltpu.HBM if i in hbm else pltpu.VMEM

    moved = sum(size_of(a.shape, a.dtype) for a in args) + sum(size_of(*o) for o in outs)
    held = moved + sum(size_of(*s) for s in scratch)
    semaphores = [pltpu.SemaphoreType.DMA((copies,))] if copies else []
    return pl.pallas_call(
        kernel,
        out_shape=[jax.ShapeDtypeStruct(s, d) for s, d in outs],
        in_specs=[pl.BlockSpec(memory_space=place(i)) for i in range(len(args))],
        out_specs=[pl.BlockSpec(memory_space=pltpu.VMEM) for _ in outs],
        scratch_shapes=[pltpu.VMEM(s, d) for s, d in scratch] + semaphores,
        compiler_params=pltpu.CompilerParams(vmem_limit_bytes=limit or int(1.2 * held) + (8 << 20)),
        cost_estimate=pl.CostEstimate(flops=flops, bytes_accessed=moved, transcendentals=0),
        name=name,
    )(*args)


def fetch(pairs, sems):
    copies = [pltpu.make_async_copy(src, dst, sems.at[i]) for i, (src, dst) in enumerate(pairs)]
    for copy in copies:
        copy.start()
    return copies


def pack_kernel(
    idx_ref, pos_hbm, q_hbm, og_hbm, lat_hbm, attn_hbm, wuv_hbm,
    lat_msg, q_msg, delta_ref, term_ref,
    pos_ref, og_ref, attn_ref, wuv_ref, term, sems,
):
    heads, width, tok = q_hbm.shape
    pairs = [(pos_hbm, pos_ref), (og_hbm, og_ref), (wuv_hbm, wuv_ref), (attn_hbm, attn_ref)]
    pairs += [(lat_hbm, lat_msg.at[pl.ds(0, width), :])]
    pairs += [(q_hbm.at[h], q_msg.at[pl.ds(h * width, width), :]) for h in range(heads)]
    copies = [pltpu.make_async_copy(src, dst, sems.at[i]) for i, (src, dst) in enumerate(pairs)]
    for copy in copies:
        copy.start()
    copies[0].wait()
    pos = jnp.broadcast_to(pos_ref[...], (EXTRA, tok))
    row = lax.broadcasted_iota(jnp.int32, (EXTRA, tok), 0)
    high = lax.shift_right_logical(pos, 6)
    both = jnp.where(row == 0, high, jnp.where(row == 1, pos - high * 64, 0))
    rows = both.astype(F32).astype(BF16)
    lat_msg[width:, :] = rows
    q_msg[heads * (width + HEAD_DIM) :, :] = rows
    delta_ref[...] = jnp.zeros_like(delta_ref)
    for copy in copies[1:4]:
        copy.wait()
    _, lat, _ = wuv_ref.shape
    for h in range(heads):
        og = og_ref[:, h, :].T
        at = heads * width + h * HEAD_DIM
        q_msg[at : at + HEAD_DIM, :] = og
        attn = attn_ref[:, h, :].T
        g = mm(wuv_ref[h], og).astype(BF16).astype(F32)
        delta_ref[h : h + 1, :] = jnp.sum(g * attn.astype(F32), axis=0, keepdims=True)
        term[h] = mm_t(attn, og)
    step = lat // GROUP
    me = lax.rem(idx_ref[0], GROUP)
    for k in range(GROUP):
        at = pl.multiple_of(jnp.bitwise_xor(me, k) * step, step)
        term_ref[k * heads : (k + 1) * heads] = term[:, pl.ds(at, step), :].astype(BF16)
    for copy in copies[4:]:
        copy.wait()


def score_kernel(factor, nkey, width, heads, *refs):
    lat_ref = refs[0]
    q_refs = refs[1 : 1 + GROUP]
    delta_ref, s_ref, k_ref, stat_ref, kt, qt = refs[1 + GROUP :]
    wide = kt.shape[0]
    tok = lat_ref.shape[2]
    rows = heads * tok
    for a in range(nkey):
        kt[: width + EXTRA, a * tok : (a + 1) * tok] = lat_ref[a]
    kt[width + EXTRA :, :] = jnp.zeros((wide - width - EXTRA, nkey * tok), BF16)
    k_ref[...] = kt[...].T
    pos = k_ref[:, wide - 128 :].astype(F32)
    at = width - (wide - 128)
    key_pos = pos[:, at : at + 1] * 64.0 + pos[:, at + 1 : at + 2]
    qt[width:, :] = jnp.zeros((wide - width, rows), BF16)
    stat_ref[...] = jnp.zeros_like(stat_ref)
    stat_ref[GROUP * heads : GROUP * heads + heads, :] = delta_ref[:heads, :]
    for j in range(GROUP):
        q_ref = q_refs[j]
        for h in range(heads):
            qt[:width, h * tok : (h + 1) * tok] = q_ref[h * width : (h + 1) * width, :]
        base = q_ref.shape[0] - EXTRA
        qp = q_ref[base:, :].astype(F32)
        one = qp[0:1, :] * 64.0 + qp[1:2, :]
        row_pos = jnp.concatenate([one] * heads, axis=1)
        s = mm(k_ref[...], qt[...]) * factor
        s = jnp.where(key_pos <= row_pos, s, -1e30)
        s_ref[:, j * rows : (j + 1) * rows] = s
        top = jnp.max(s, axis=0, keepdims=True)
        lse = top + jnp.log(jnp.sum(jnp.exp(s - top), axis=0, keepdims=True))
        for h in range(heads):
            at = j * heads + h
            stat_ref[at : at + 1, :] = lse[:, h * tok : (h + 1) * tok]


def context_kernel(width, heads, *refs):
    q_refs = refs[:GROUP]
    wuv_ref, k_ref, g_ref, gp_ref = refs[GROUP:]
    lat, all_rows = g_ref.shape
    tok = q_refs[0].shape[1]
    rows = heads * tok
    for j in range(GROUP):
        for h in range(heads):
            at = heads * width + h * HEAD_DIM
            og = q_refs[j][at : at + HEAD_DIM, :]
            col = j * rows + h * tok
            g_ref[:, col : col + tok] = mm(wuv_ref[h], og).astype(BF16)
        cols = slice(j * rows, (j + 1) * rows)
        gp_ref[:, cols] = mm(k_ref[:, :lat], g_ref[:, cols])


def grad_kernel(factor, nkey, width, heads, *refs):
    lat_ref, refs = refs[0], refs[1:]
    q_refs, refs = refs[:GROUP], refs[GROUP:]
    stats, refs = refs[:GROUP], refs[GROUP:]
    (s_ref, gp_ref, g_ref), refs = refs[:3], refs[3:]
    part_ref, refs = refs[0], refs[1:]
    own_ref, core_ref, across_ref, kt, qt, gs_all, p_all = refs
    tok = q_refs[0].shape[1]
    rows = heads * tok
    lat = g_ref.shape[0]
    for a in range(nkey):
        kt[:, a * tok : (a + 1) * tok] = lat_ref[a, :width, :]
    for j in range(GROUP):
        cols = slice(j * rows, (j + 1) * rows)
        lse_parts = []
        for k in range(GROUP):
            at = (j ^ k) * heads
            lse_parts.append(
                jnp.concatenate([stats[k][at + h : at + h + 1, :] for h in range(heads)], axis=1)
            )
        top = functools.reduce(jnp.maximum, lse_parts)
        lse = top + jnp.log(sum(jnp.exp(part - top) for part in lse_parts))
        at = GROUP * heads
        delta = jnp.concatenate([stats[j][at + h : at + h + 1, :] for h in range(heads)], axis=1)
        p = jnp.exp(s_ref[:, cols] - lse)
        gs = (p * (gp_ref[:, cols] - delta)).astype(BF16)
        gs_all[:, cols] = gs
        p_all[:, cols] = p.astype(BF16)
        gq = (mm(kt[...], gs) * factor).astype(BF16)
        for h in range(heads):
            head_cols = slice(j * rows + h * tok, j * rows + (h + 1) * tok)
            qt[:, head_cols] = q_refs[j][h * width : (h + 1) * width, :]
            part = gq[:, h * tok : (h + 1) * tok]
            if j == 0:
                own_ref[h] = part
            elif j == 2:
                across_ref[h] = part
            else:
                core_ref[j // 2 * heads + h] = part
    for a in range(nkey):
        at = slice(a * tok, (a + 1) * tok)
        along = mm_t(qt[...], gs_all[at, :]) * factor
        value = mm_t(g_ref[...], p_all[at, :])
        part_ref[a, :lat, :] = (along[:lat] + value).astype(BF16)
        part_ref[a, lat:, :] = along[lat:].astype(BF16)


def spread_kernel(scale, idx_ref, *refs):
    chunks, out_ref = refs[:GROUP], refs[GROUP]
    step = chunks[0].shape[1]
    me = lax.rem(idx_ref[0], GROUP)
    for k in range(GROUP):
        at = pl.multiple_of(jnp.bitwise_xor(me, k) * step, step)
        out_ref[:, pl.ds(at, step), :] = chunks[k][...].astype(F32) * scale


def body(n_ctx, n_dp, positions, queries, latent, out_grad, attn_out, wuv):
    tok, heads, width = queries.shape[1:]
    lat = attn_out.shape[3]
    lines = n_ctx // GROUP
    rows = heads * tok
    all_rows = GROUP * rows
    keys = lines * tok
    wide = -(-(width + EXTRA) // 128) * 128
    factor = (HEAD_DIM + ROPE) ** (-0.5)

    def swap(x, mask):
        return lax.ppermute(x, "ctx", [(i, i ^ mask) for i in range(n_ctx)])

    def after(x, *done):
        return lax.optimization_barrier((x, done))[0]

    idx = lax.axis_index("ctx").reshape(1)
    step = lat // GROUP
    lat_msg, q_msg, delta, term = call(
        pack_kernel,
        "pack",
        [
            ((width + EXTRA, tok), BF16),
            ((heads * (width + HEAD_DIM) + EXTRA, tok), BF16),
            ((8, tok), F32),
            ((GROUP * heads, step, HEAD_DIM), BF16),
        ],
        [
            idx,
            positions,
            jnp.transpose(queries[0], (1, 2, 0)),
            out_grad[0],
            latent[0].T,
            attn_out[0],
            wuv,
        ],
        [
            ((1, tok), jnp.int32),
            (out_grad.shape[1:], BF16),
            (attn_out.shape[1:], BF16),
            (wuv.shape, BF16),
            ((heads, lat, HEAD_DIM), F32),
        ],
        smem=(0,),
        hbm=(1, 2, 3, 4, 5, 6),
        copies=5 + heads,
        limit=PACK_LIMIT,
    )

    def hop(total, axis, size, mask, *done):
        other = lax.ppermute(total, axis, [(i, i ^ mask) for i in range(size)])
        return total, after(other, *done) if done else other

    def add(pair):
        return (pair[0].astype(F32) + pair[1].astype(F32)).astype(BF16)

    dp_hops = [("dp", n_dp, 1 << bit) for bit in range((n_dp - 1).bit_length())]

    line_bits = (lines - 1).bit_length()
    line_hops = [("ctx", n_ctx, GROUP << bit) for bit in range(line_bits)]
    line_groups = [[r + GROUP * a for a in range(lines)] for r in range(GROUP)]
    lats = lax.all_gather(lat_msg, "ctx", axis_index_groups=line_groups)
    q_across = swap(q_msg, 2)
    q_core = swap(q_msg, 1)
    twins = hop(term, *dp_hops[0])
    q_across, q_core, twins = lax.optimization_barrier((q_across, q_core, twins))
    for step_hop in dp_hops[1:]:
        twins = hop(add(twins), *step_hop)
    total = add(twins)
    q_far = swap(q_across, 1)
    half = 2 * heads
    got_half = swap(total[half:], 2)
    q_far, got_half = lax.optimization_barrier((q_far, got_half))
    qs = [q_msg, q_core, q_across, q_far]
    total = add((total[:half], got_half))
    got_own = swap(total[heads:], 1)

    s, k_nat, stat = call(
        functools.partial(score_kernel, factor, lines, width, heads),
        "scores",
        [((keys, all_rows), F32), ((keys, wide), BF16), ((EXTRA, tok), F32)],
        [lats] + qs + [delta],
        [((wide, keys), BF16), ((wide, rows), BF16)],
        flops=2 * keys * all_rows * wide,
    )
    stats = [stat] + [swap(stat, k) for k in range(1, GROUP)]
    mine = add((total[:heads], after(got_own, stat)))
    near = hop(mine, *line_hops[0])
    g, gp = call(
        functools.partial(context_kernel, width, heads),
        "context",
        [((lat, all_rows), BF16), ((keys, all_rows), F32)],
        qs + [wuv, k_nat],
        flops=2 * keys * all_rows * lat + 2 * all_rows * lat * HEAD_DIM,
    )
    mine = add((near[0], after(near[1], gp)))
    mine, stats = lax.optimization_barrier((mine, stats))
    outs = call(
        functools.partial(grad_kernel, factor, lines, width, heads),
        "gradients",
        [((lines, width, tok), BF16)]
        + [((heads, width, tok), BF16), ((2 * heads, width, tok), BF16), ((heads, width, tok), BF16)],
        [lats] + qs + stats + [s, gp, g],
        [
            ((width, keys), BF16),
            ((width, all_rows), BF16),
            ((keys, all_rows), BF16),
            ((keys, all_rows), BF16),
        ],
        flops=2 * keys * all_rows * (2 * width + lat),
    )
    parts, gq_own, gq_core, gq_across = outs
    grad_lat = lax.psum_scatter(parts, "ctx", axis_index_groups=line_groups)
    gq_got = swap(gq_core, 1)
    for step_hop in line_hops[1:]:
        mine = add(hop(after(mine, gq_own), *step_hop))
    gq_got, mine = lax.optimization_barrier((gq_got, mine))
    gq_last = swap(add((gq_across, gq_got[heads:])), 2)
    mine_two = jnp.concatenate([mine, swap(mine, 2)], axis=0)
    other_two = swap(mine_two, 1)
    grad_q = sum(p.astype(F32) for p in (gq_own, gq_got[:heads], gq_last)).astype(BF16)
    scale = 1.0 / math.sqrt(tok * n_ctx * n_dp)
    pieces = [mine_two[:heads], other_two[:heads], mine_two[heads:], other_two[heads:]]
    (grad_w,) = call(
        functools.partial(spread_kernel, scale), "spread", [((heads, lat, HEAD_DIM), F32)], [idx] + pieces, smem=(0,)
    )
    return (jnp.transpose(grad_q, (2, 0, 1))[None], grad_lat.T[None], grad_w)


def solution(mesh):
    placed = (
        P("dp", "ctx"),
        P("dp", "ctx", None, None),
        P("dp", "ctx", None),
        P("dp", "ctx", None, None),
        P("dp", "ctx", None, None),
        P(),
    )
    return jax.shard_map(
        functools.partial(body, mesh.shape["ctx"], mesh.shape["dp"]),
        mesh=mesh,
        in_specs=placed,
        out_specs=(P("dp", "ctx", None, None), P("dp", "ctx", None), P()),
        check_vma=False,
    )
```

```python
import functools
import math

import jax
import jax.numpy as jnp
from jax import lax
from jax.experimental import pallas as pl
from jax.experimental.pallas import tpu as pltpu
from jax.sharding import PartitionSpec as P

ROPE = 64
HEAD_DIM = 128
GROUP = 4
EXTRA = 16
PACK_LIMIT = 63 << 20
F32 = jnp.float32
BF16 = jnp.bfloat16


def mm(a, b):
    return jnp.dot(a, b, preferred_element_type=F32)


def mm_t(a, b):
    return lax.dot_general(a, b, (((1,), (1,)), ((), ())), preferred_element_type=F32)


def size_of(shape, dtype):
    return math.prod(shape) * jnp.dtype(dtype).itemsize


def call(kernel, name, outs, args, scratch=(), flops=0, smem=(), hbm=(), copies=0, limit=None):
    def place(i):
        return pltpu.SMEM if i in smem else pltpu.HBM if i in hbm else pltpu.VMEM

    moved = sum(size_of(a.shape, a.dtype) for a in args) + sum(size_of(*o) for o in outs)
    held = moved + sum(size_of(*s) for s in scratch)
    semaphores = [pltpu.SemaphoreType.DMA((copies,))] if copies else []
    return pl.pallas_call(
        kernel,
        out_shape=[jax.ShapeDtypeStruct(s, d) for s, d in outs],
        in_specs=[pl.BlockSpec(memory_space=place(i)) for i in range(len(args))],
        out_specs=[pl.BlockSpec(memory_space=pltpu.VMEM) for _ in outs],
        scratch_shapes=[pltpu.VMEM(s, d) for s, d in scratch] + semaphores,
        compiler_params=pltpu.CompilerParams(vmem_limit_bytes=limit or int(1.2 * held) + (8 << 20)),
        cost_estimate=pl.CostEstimate(flops=flops, bytes_accessed=moved, transcendentals=0),
        name=name,
    )(*args)


def fetch(pairs, sems):
    copies = [pltpu.make_async_copy(src, dst, sems.at[i]) for i, (src, dst) in enumerate(pairs)]
    for copy in copies:
        copy.start()
    return copies


def pack_kernel(
    idx_ref, pos_hbm, q_hbm, og_hbm, lat_hbm, attn_hbm, wuv_hbm,
    lat_msg, q_msg, delta_ref, keep_ref, send_ref,
    pos_ref, og_ref, attn_ref, wuv_ref, term, sems,
):
    heads, width, tok = q_hbm.shape
    pairs = [(pos_hbm, pos_ref), (og_hbm, og_ref), (wuv_hbm, wuv_ref), (attn_hbm, attn_ref)]
    pairs += [(lat_hbm, lat_msg.at[pl.ds(0, width), :])]
    pairs += [(q_hbm.at[h], q_msg.at[pl.ds(h * width, width), :]) for h in range(heads)]
    copies = [pltpu.make_async_copy(src, dst, sems.at[i]) for i, (src, dst) in enumerate(pairs)]
    for copy in copies:
        copy.start()
    copies[0].wait()
    pos = jnp.broadcast_to(pos_ref[...], (EXTRA, tok))
    row = lax.broadcasted_iota(jnp.int32, (EXTRA, tok), 0)
    high = lax.shift_right_logical(pos, 6)
    both = jnp.where(row == 0, high, jnp.where(row == 1, pos - high * 64, 0))
    rows = both.astype(F32).astype(BF16)
    lat_msg[width:, :] = rows
    q_msg[heads * (width + HEAD_DIM) :, :] = rows
    delta_ref[...] = jnp.zeros_like(delta_ref)
    for copy in copies[1:4]:
        copy.wait()
    _, lat, _ = wuv_ref.shape
    for h in range(heads):
        og = og_ref[:, h, :].T
        at = heads * width + h * HEAD_DIM
        q_msg[at : at + HEAD_DIM, :] = og
        attn = attn_ref[:, h, :].T
        g = mm(wuv_ref[h], og).astype(BF16).astype(F32)
        delta_ref[h : h + 1, :] = jnp.sum(g * attn.astype(F32), axis=0, keepdims=True)
        term[h] = mm_t(attn, og)
    step = lat // GROUP
    me = lax.rem(idx_ref[0], GROUP)
    for k in range(GROUP):
        at = pl.multiple_of(jnp.bitwise_xor(me, k) * step, step)
        target = send_ref if k % 2 else keep_ref
        target[k // 2 * heads : (k // 2 + 1) * heads] = term[:, pl.ds(at, step), :].astype(BF16)
    for copy in copies[4:]:
        copy.wait()


def score_kernel(factor, nkey, width, heads, *refs):
    lat_refs = refs[:nkey]
    q_refs = refs[nkey : nkey + GROUP]
    delta_ref, s_ref, k_ref, stat_ref, kt, qt = refs[nkey + GROUP :]
    wide = kt.shape[0]
    tok = lat_refs[0].shape[1]
    rows = heads * tok
    for a in range(nkey):
        kt[: width + EXTRA, a * tok : (a + 1) * tok] = lat_refs[a][...]
    kt[width + EXTRA :, :] = jnp.zeros((wide - width - EXTRA, nkey * tok), BF16)
    k_ref[...] = kt[...].T
    pos = k_ref[:, wide - 128 :].astype(F32)
    at = width - (wide - 128)
    key_pos = pos[:, at : at + 1] * 64.0 + pos[:, at + 1 : at + 2]
    qt[width:, :] = jnp.zeros((wide - width, rows), BF16)
    stat_ref[...] = jnp.zeros_like(stat_ref)
    stat_ref[GROUP * heads : GROUP * heads + heads, :] = delta_ref[:heads, :]
    for j in range(GROUP):
        q_ref = q_refs[j]
        for h in range(heads):
            qt[:width, h * tok : (h + 1) * tok] = q_ref[h * width : (h + 1) * width, :]
        base = q_ref.shape[0] - EXTRA
        qp = q_ref[base:, :].astype(F32)
        one = qp[0:1, :] * 64.0 + qp[1:2, :]
        row_pos = jnp.concatenate([one] * heads, axis=1)
        s = mm(k_ref[...], qt[...]) * factor
        s = jnp.where(key_pos <= row_pos, s, -1e30)
        s_ref[:, j * rows : (j + 1) * rows] = s
        top = jnp.max(s, axis=0, keepdims=True)
        lse = top + jnp.log(jnp.sum(jnp.exp(s - top), axis=0, keepdims=True))
        for h in range(heads):
            at = j * heads + h
            stat_ref[at : at + 1, :] = lse[:, h * tok : (h + 1) * tok]


def context_kernel(width, heads, *refs):
    q_refs = refs[:GROUP]
    wuv_ref, k_ref, g_ref, gp_ref = refs[GROUP:]
    lat, all_rows = g_ref.shape
    tok = q_refs[0].shape[1]
    rows = heads * tok
    for j in range(GROUP):
        for h in range(heads):
            at = heads * width + h * HEAD_DIM
            og = q_refs[j][at : at + HEAD_DIM, :]
            col = j * rows + h * tok
            g_ref[:, col : col + tok] = mm(wuv_ref[h], og).astype(BF16)
        cols = slice(j * rows, (j + 1) * rows)
        gp_ref[:, cols] = mm(k_ref[:, :lat], g_ref[:, cols])


def grad_kernel(factor, nkey, width, heads, *refs):
    lat_refs, refs = refs[:nkey], refs[nkey:]
    q_refs, refs = refs[:GROUP], refs[GROUP:]
    stats, refs = refs[:GROUP], refs[GROUP:]
    (s_ref, gp_ref, g_ref), refs = refs[:3], refs[3:]
    part_refs, refs = refs[:nkey], refs[nkey:]
    own_ref, core_ref, across_ref, kt, qt, gs_all, p_all = refs
    tok = q_refs[0].shape[1]
    rows = heads * tok
    lat = g_ref.shape[0]
    for a in range(nkey):
        kt[:, a * tok : (a + 1) * tok] = lat_refs[a][:width, :]
    for j in range(GROUP):
        cols = slice(j * rows, (j + 1) * rows)
        lse_parts = []
        for k in range(GROUP):
            at = (j ^ k) * heads
            lse_parts.append(
                jnp.concatenate([stats[k][at + h : at + h + 1, :] for h in range(heads)], axis=1)
            )
        top = functools.reduce(jnp.maximum, lse_parts)
        lse = top + jnp.log(sum(jnp.exp(part - top) for part in lse_parts))
        at = GROUP * heads
        delta = jnp.concatenate([stats[j][at + h : at + h + 1, :] for h in range(heads)], axis=1)
        p = jnp.exp(s_ref[:, cols] - lse)
        gs = (p * (gp_ref[:, cols] - delta)).astype(BF16)
        gs_all[:, cols] = gs
        p_all[:, cols] = p.astype(BF16)
        gq = (mm(kt[...], gs) * factor).astype(BF16)
        for h in range(heads):
            head_cols = slice(j * rows + h * tok, j * rows + (h + 1) * tok)
            qt[:, head_cols] = q_refs[j][h * width : (h + 1) * width, :]
            part = gq[:, h * tok : (h + 1) * tok]
            if j == 0:
                own_ref[h] = part
            elif j == 2:
                across_ref[h] = part
            else:
                core_ref[j // 2 * heads + h] = part
    for a in range(nkey):
        at = slice(a * tok, (a + 1) * tok)
        along = mm_t(qt[...], gs_all[at, :]) * factor
        value = mm_t(g_ref[...], p_all[at, :])
        part_refs[a][:lat, :] = (along[:lat] + value).astype(BF16)
        part_refs[a][lat:, :] = along[lat:].astype(BF16)


def sum_kernel(gq_own_ref, gq_got_ref, gq_last_ref, *refs):
    parts, (lat_out_ref, q_out_ref) = refs[:-2], refs[-2:]
    lat_out_ref[...] = sum(part[...].astype(F32) for part in parts).astype(BF16)
    for h in range(q_out_ref.shape[0]):
        pieces = (gq_own_ref[h], gq_got_ref[h], gq_last_ref[h])
        q_out_ref[h] = sum(piece.astype(F32) for piece in pieces).astype(BF16)


def spread_kernel(scale, idx_ref, *refs):
    chunks, out_ref = refs[:GROUP], refs[GROUP]
    step = chunks[0].shape[1]
    me = lax.rem(idx_ref[0], GROUP)
    for k in range(GROUP):
        at = pl.multiple_of(jnp.bitwise_xor(me, k) * step, step)
        out_ref[:, pl.ds(at, step), :] = chunks[k][...].astype(F32) * scale


def body(n_ctx, n_dp, positions, queries, latent, out_grad, attn_out, wuv):
    tok, heads, width = queries.shape[1:]
    lat = attn_out.shape[3]
    lines = n_ctx // GROUP
    line_bits = (lines - 1).bit_length()
    rows = heads * tok
    all_rows = GROUP * rows
    keys = lines * tok
    wide = -(-(width + EXTRA) // 128) * 128
    factor = (HEAD_DIM + ROPE) ** (-0.5)

    def swap(x, mask, axis="ctx", size=n_ctx):
        return lax.ppermute(x, axis, [(i, i ^ mask) for i in range(size)])

    def after(x, *done):
        return lax.optimization_barrier((x, done))[0]

    idx = lax.axis_index("ctx").reshape(1)
    step = lat // GROUP
    lat_msg, q_msg, delta, keep, send = call(
        pack_kernel,
        "pack",
        [
            ((width + EXTRA, tok), BF16),
            ((heads * (width + HEAD_DIM) + EXTRA, tok), BF16),
            ((8, tok), F32),
            ((2 * heads, step, HEAD_DIM), BF16),
            ((2 * heads, step, HEAD_DIM), BF16),
        ],
        [
            idx,
            positions,
            jnp.transpose(queries[0], (1, 2, 0)),
            out_grad[0],
            latent[0].T,
            attn_out[0],
            wuv,
        ],
        [
            ((1, tok), jnp.int32),
            (out_grad.shape[1:], BF16),
            (attn_out.shape[1:], BF16),
            (wuv.shape, BF16),
            ((heads, lat, HEAD_DIM), F32),
        ],
        smem=(0,),
        hbm=(1, 2, 3, 4, 5, 6),
        copies=5 + heads,
        limit=PACK_LIMIT,
    )

    def add(a, b):
        return (a.astype(F32) + b.astype(F32)).astype(BF16)

    dp_hops = [(1 << bit, "dp", n_dp) for bit in range((n_dp - 1).bit_length())]
    line_hops = [(GROUP << bit,) for bit in range(line_bits)]

    firsts = [swap(lat_msg, GROUP << bit) for bit in range(line_bits)]
    q_across = swap(q_msg, 2)
    q_core = swap(q_msg, 1)
    got_pair = swap(send, 1)
    q_core, q_across, firsts, got_pair = lax.optimization_barrier(
        (q_core, q_across, firsts, got_pair)
    )
    pair = add(keep, got_pair)

    held = {0: lat_msg}
    for bit in reversed(range(line_bits)):
        held.update({m | 1 << bit: swap(x, GROUP << bit) for m, x in held.items() if m})
        held[1 << bit] = firsts[bit]
    lats = [held[m] for m in range(lines)]
    q_far = swap(q_across, 1)
    got_pair = swap(pair, *dp_hops[0])
    q_far, lats, got_pair = lax.optimization_barrier((q_far, lats, got_pair))
    pair = add(pair, got_pair)
    for step_hop in dp_hops[1:]:
        pair = add(pair, swap(pair, *step_hop))
    qs = [q_msg, q_core, q_across, q_far]
    got_own = swap(pair[heads:], 2)

    s, k_nat, stat = call(
        functools.partial(score_kernel, factor, lines, width, heads),
        "scores",
        [((keys, all_rows), F32), ((keys, wide), BF16), ((EXTRA, tok), F32)],
        lats + qs + [delta],
        [((wide, keys), BF16), ((wide, rows), BF16)],
        flops=2 * keys * all_rows * wide,
    )
    stats = [stat] + [swap(stat, k) for k in range(1, GROUP)]
    mine = add(pair[:heads], after(got_own, stat))
    near = swap(mine, *line_hops[0])
    g, gp = call(
        functools.partial(context_kernel, width, heads),
        "context",
        [((lat, all_rows), BF16), ((keys, all_rows), F32)],
        qs + [wuv, k_nat],
        flops=2 * keys * all_rows * lat + 2 * all_rows * lat * HEAD_DIM,
    )
    near, stats = lax.optimization_barrier((after(near, gp), stats))
    mine = add(mine, near)
    outs = call(
        functools.partial(grad_kernel, factor, lines, width, heads),
        "gradients",
        [((width, tok), BF16)] * lines
        + [((heads, width, tok), BF16), ((2 * heads, width, tok), BF16), ((heads, width, tok), BF16)],
        lats + qs + stats + [s, gp, g],
        [
            ((width, keys), BF16),
            ((width, all_rows), BF16),
            ((keys, all_rows), BF16),
            ((keys, all_rows), BF16),
        ],
        flops=2 * keys * all_rows * (2 * width + lat),
    )
    parts, (gq_own, gq_core, gq_across) = list(outs[:lines]), outs[lines:]
    gq_got = swap(gq_core, 1)
    for step_hop in line_hops[1:-1]:
        mine = add(mine, swap(mine, *step_hop))
    far = [m for m in range(3, lines, 2)]
    got_far = [swap(parts[m], GROUP) for m in far]
    got_mine = swap(mine, *line_hops[-1])
    gq_got, got_far, got_mine = lax.optimization_barrier((gq_got, got_far, got_mine))
    mine = add(mine, got_mine)
    for m, got in zip(far, got_far):
        parts[m ^ 1] = add(parts[m ^ 1], got)
    for bit in range(1, line_bits):
        for m in range(3 << bit, lines, 2 << bit):
            parts[m ^ 1 << bit] = add(parts[m ^ 1 << bit], swap(parts[m], GROUP << bit))
    gq_last = swap(add(gq_across, gq_got[heads:]), 2)
    kept = [swap(parts[1 << bit], GROUP << bit) for bit in reversed(range(line_bits))]
    across = swap(mine, 2)
    gq_last, kept, across = lax.optimization_barrier((gq_last, kept, across))
    mine_two = jnp.concatenate([mine, across], axis=0)
    other_two = swap(mine_two, 1)
    grad_lat, grad_q = call(
        sum_kernel,
        "last_sums",
        [((width, tok), BF16), ((heads, width, tok), BF16)],
        [gq_own, gq_got, gq_last, parts[0]] + kept,
    )
    scale = 1.0 / math.sqrt(tok * n_ctx * n_dp)
    pieces = [mine_two[:heads], other_two[:heads], mine_two[heads:], other_two[heads:]]
    (grad_w,) = call(
        functools.partial(spread_kernel, scale), "spread", [((heads, lat, HEAD_DIM), F32)], [idx] + pieces, smem=(0,)
    )
    return (jnp.transpose(grad_q, (2, 0, 1))[None], grad_lat.T[None], grad_w)


def solution(mesh):
    placed = (
        P("dp", "ctx"),
        P("dp", "ctx", None, None),
        P("dp", "ctx", None),
        P("dp", "ctx", None, None),
        P("dp", "ctx", None, None),
        P(),
    )
    return jax.shard_map(
        functools.partial(body, mesh.shape["ctx"], mesh.shape["dp"]),
        mesh=mesh,
        in_specs=placed,
        out_specs=(P("dp", "ctx", None, None), P("dp", "ctx", None), P()),
        check_vma=False,
    )
```

```python
import functools
import math

import jax
import jax.numpy as jnp
from jax import lax
from jax.experimental import pallas as pl
from jax.experimental.pallas import tpu as pltpu
from jax.sharding import PartitionSpec as P

ROPE = 64
HEAD_DIM = 128
GROUP = 4
EXTRA = 16
PACK_LIMIT = 63 << 20
F32 = jnp.float32
BF16 = jnp.bfloat16


def mm(a, b):
    return jnp.dot(a, b, preferred_element_type=F32)


def mm_t(a, b):
    return lax.dot_general(a, b, (((1,), (1,)), ((), ())), preferred_element_type=F32)


def size_of(shape, dtype):
    return math.prod(shape) * jnp.dtype(dtype).itemsize


def call(kernel, name, outs, args, scratch=(), flops=0, smem=(), hbm=(), copies=0, limit=None):
    def place(i):
        return pltpu.SMEM if i in smem else pltpu.HBM if i in hbm else pltpu.VMEM

    moved = sum(size_of(a.shape, a.dtype) for a in args) + sum(size_of(*o) for o in outs)
    held = moved + sum(size_of(*s) for s in scratch)
    semaphores = [pltpu.SemaphoreType.DMA((copies,))] if copies else []
    return pl.pallas_call(
        kernel,
        out_shape=[jax.ShapeDtypeStruct(s, d) for s, d in outs],
        in_specs=[pl.BlockSpec(memory_space=place(i)) for i in range(len(args))],
        out_specs=[pl.BlockSpec(memory_space=pltpu.VMEM) for _ in outs],
        scratch_shapes=[pltpu.VMEM(s, d) for s, d in scratch] + semaphores,
        compiler_params=pltpu.CompilerParams(vmem_limit_bytes=limit or int(1.2 * held) + (8 << 20)),
        cost_estimate=pl.CostEstimate(flops=flops, bytes_accessed=moved, transcendentals=0),
        name=name,
    )(*args)


def fetch(pairs, sems):
    copies = [pltpu.make_async_copy(src, dst, sems.at[i]) for i, (src, dst) in enumerate(pairs)]
    for copy in copies:
        copy.start()
    return copies


def pack_kernel(
    idx_ref, pos_hbm, q_hbm, og_hbm, lat_hbm, attn_hbm, wuv_hbm,
    lat_msg, q_msg, delta_ref, keep_ref, send_ref,
    pos_ref, og_ref, attn_ref, wuv_ref, term, sems,
):
    heads, width, tok = q_hbm.shape
    pairs = [(pos_hbm, pos_ref), (og_hbm, og_ref), (wuv_hbm, wuv_ref), (attn_hbm, attn_ref)]
    pairs += [(lat_hbm, lat_msg.at[pl.ds(0, width), :])]
    pairs += [(q_hbm.at[h], q_msg.at[pl.ds(h * width, width), :]) for h in range(heads)]
    copies = [pltpu.make_async_copy(src, dst, sems.at[i]) for i, (src, dst) in enumerate(pairs)]
    for copy in copies:
        copy.start()
    copies[0].wait()
    pos = jnp.broadcast_to(pos_ref[...], (EXTRA, tok))
    row = lax.broadcasted_iota(jnp.int32, (EXTRA, tok), 0)
    high = lax.shift_right_logical(pos, 6)
    both = jnp.where(row == 0, high, jnp.where(row == 1, pos - high * 64, 0))
    rows = both.astype(F32).astype(BF16)
    lat_msg[width:, :] = rows
    q_msg[heads * (width + HEAD_DIM) :, :] = rows
    delta_ref[...] = jnp.zeros_like(delta_ref)
    for copy in copies[1:4]:
        copy.wait()
    _, lat, _ = wuv_ref.shape
    for h in range(heads):
        og = og_ref[:, h, :].T
        at = heads * width + h * HEAD_DIM
        q_msg[at : at + HEAD_DIM, :] = og
        attn = attn_ref[:, h, :].T
        g = mm(wuv_ref[h], og).astype(BF16).astype(F32)
        delta_ref[h : h + 1, :] = jnp.sum(g * attn.astype(F32), axis=0, keepdims=True)
        term[h] = mm_t(attn, og)
    step = lat // GROUP
    me = lax.rem(idx_ref[0], GROUP)
    for k in range(GROUP):
        at = pl.multiple_of(jnp.bitwise_xor(me, k) * step, step)
        target = send_ref if k % 2 else keep_ref
        target[k // 2 * heads : (k // 2 + 1) * heads] = term[:, pl.ds(at, step), :].astype(BF16)
    for copy in copies[4:]:
        copy.wait()


def hold_kernel(*refs):
    half = len(refs) // 2
    for source, target in zip(refs[:half], refs[half:]):
        target[...] = source[...]


def score_kernel(factor, nkey, width, heads, *refs):
    lat_refs = refs[:nkey]
    q_refs = refs[nkey : nkey + GROUP]
    delta_ref, s_ref, k_ref, stat_ref, kt, qt = refs[nkey + GROUP :]
    wide = kt.shape[0]
    tok = lat_refs[0].shape[1]
    rows = heads * tok
    for a in range(nkey):
        kt[: width + EXTRA, a * tok : (a + 1) * tok] = lat_refs[a][...]
    kt[width + EXTRA :, :] = jnp.zeros((wide - width - EXTRA, nkey * tok), BF16)
    k_ref[...] = kt[...].T
    pos = k_ref[:, wide - 128 :].astype(F32)
    at = width - (wide - 128)
    key_pos = pos[:, at : at + 1] * 64.0 + pos[:, at + 1 : at + 2]
    qt[width:, :] = jnp.zeros((wide - width, rows), BF16)
    stat_ref[...] = jnp.zeros_like(stat_ref)
    stat_ref[GROUP * heads : GROUP * heads + heads, :] = delta_ref[:heads, :]
    for j in range(GROUP):
        q_ref = q_refs[j]
        for h in range(heads):
            qt[:width, h * tok : (h + 1) * tok] = q_ref[h * width : (h + 1) * width, :]
        base = q_ref.shape[0] - EXTRA
        qp = q_ref[base:, :].astype(F32)
        one = qp[0:1, :] * 64.0 + qp[1:2, :]
        row_pos = jnp.concatenate([one] * heads, axis=1)
        s = mm(k_ref[...], qt[...]) * factor
        s = jnp.where(key_pos <= row_pos, s, -1e30)
        s_ref[:, j * rows : (j + 1) * rows] = s
        top = jnp.max(s, axis=0, keepdims=True)
        lse = top + jnp.log(jnp.sum(jnp.exp(s - top), axis=0, keepdims=True))
        for h in range(heads):
            at = j * heads + h
            stat_ref[at : at + 1, :] = lse[:, h * tok : (h + 1) * tok]


def context_kernel(width, heads, *refs):
    q_refs = refs[:GROUP]
    wuv_ref, k_ref, g_ref, gp_ref = refs[GROUP:]
    lat, all_rows = g_ref.shape
    tok = q_refs[0].shape[1]
    rows = heads * tok
    for j in range(GROUP):
        for h in range(heads):
            at = heads * width + h * HEAD_DIM
            og = q_refs[j][at : at + HEAD_DIM, :]
            col = j * rows + h * tok
            g_ref[:, col : col + tok] = mm(wuv_ref[h], og).astype(BF16)
        cols = slice(j * rows, (j + 1) * rows)
        gp_ref[:, cols] = mm(k_ref[:, :lat], g_ref[:, cols])


def grad_kernel(factor, nkey, width, heads, *refs):
    lat_refs, refs = refs[:nkey], refs[nkey:]
    q_refs, refs = refs[:GROUP], refs[GROUP:]
    stats, refs = refs[:GROUP], refs[GROUP:]
    (s_ref, gp_ref, g_ref), refs = refs[:3], refs[3:]
    part_refs, refs = refs[:nkey], refs[nkey:]
    own_ref, core_ref, across_ref, kt, qt, gs_all, p_all = refs
    tok = q_refs[0].shape[1]
    rows = heads * tok
    lat = g_ref.shape[0]
    for a in range(nkey):
        kt[:, a * tok : (a + 1) * tok] = lat_refs[a][:width, :]
    for j in range(GROUP):
        cols = slice(j * rows, (j + 1) * rows)
        lse_parts = []
        for k in range(GROUP):
            at = (j ^ k) * heads
            lse_parts.append(
                jnp.concatenate([stats[k][at + h : at + h + 1, :] for h in range(heads)], axis=1)
            )
        top = functools.reduce(jnp.maximum, lse_parts)
        lse = top + jnp.log(sum(jnp.exp(part - top) for part in lse_parts))
        at = GROUP * heads
        delta = jnp.concatenate([stats[j][at + h : at + h + 1, :] for h in range(heads)], axis=1)
        p = jnp.exp(s_ref[:, cols] - lse)
        gs = (p * (gp_ref[:, cols] - delta)).astype(BF16)
        gs_all[:, cols] = gs
        p_all[:, cols] = p.astype(BF16)
        gq = (mm(kt[...], gs) * factor).astype(BF16)
        for h in range(heads):
            head_cols = slice(j * rows + h * tok, j * rows + (h + 1) * tok)
            qt[:, head_cols] = q_refs[j][h * width : (h + 1) * width, :]
            part = gq[:, h * tok : (h + 1) * tok]
            if j == 0:
                own_ref[h] = part
            elif j == 2:
                across_ref[h] = part
            else:
                core_ref[j // 2 * heads + h] = part
    for a in range(nkey):
        at = slice(a * tok, (a + 1) * tok)
        along = mm_t(qt[...], gs_all[at, :]) * factor
        value = mm_t(g_ref[...], p_all[at, :])
        part_refs[a][:lat, :] = (along[:lat] + value).astype(BF16)
        part_refs[a][lat:, :] = along[lat:].astype(BF16)


def sum_kernel(gq_own_ref, gq_got_ref, gq_last_ref, *refs):
    parts, (lat_out_ref, q_out_ref) = refs[:-2], refs[-2:]
    lat_out_ref[...] = sum(part[...].astype(F32) for part in parts).astype(BF16)
    for h in range(q_out_ref.shape[0]):
        pieces = (gq_own_ref[h], gq_got_ref[h], gq_last_ref[h])
        q_out_ref[h] = sum(piece.astype(F32) for piece in pieces).astype(BF16)


def spread_kernel(scale, idx_ref, *refs):
    chunks, out_ref = refs[:GROUP], refs[GROUP]
    step = chunks[0].shape[1]
    me = lax.rem(idx_ref[0], GROUP)
    for k in range(GROUP):
        at = pl.multiple_of(jnp.bitwise_xor(me, k) * step, step)
        out_ref[:, pl.ds(at, step), :] = chunks[k][...].astype(F32) * scale


def body(n_ctx, n_dp, positions, queries, latent, out_grad, attn_out, wuv):
    tok, heads, width = queries.shape[1:]
    lat = attn_out.shape[3]
    lines = n_ctx // GROUP
    line_bits = (lines - 1).bit_length()
    rows = heads * tok
    all_rows = GROUP * rows
    keys = lines * tok
    wide = -(-(width + EXTRA) // 128) * 128
    factor = (HEAD_DIM + ROPE) ** (-0.5)

    def swap(x, mask, axis="ctx", size=n_ctx):
        return lax.ppermute(x, axis, [(i, i ^ mask) for i in range(size)])

    def after(x, *done):
        return lax.optimization_barrier((x, done))[0]

    idx = lax.axis_index("ctx").reshape(1)
    step = lat // GROUP
    lat_msg, q_msg, delta, keep, send = call(
        pack_kernel,
        "pack",
        [
            ((width + EXTRA, tok), BF16),
            ((heads * (width + HEAD_DIM) + EXTRA, tok), BF16),
            ((8, tok), F32),
            ((2 * heads, step, HEAD_DIM), BF16),
            ((2 * heads, step, HEAD_DIM), BF16),
        ],
        [
            idx,
            positions,
            jnp.transpose(queries[0], (1, 2, 0)),
            out_grad[0],
            latent[0].T,
            attn_out[0],
            wuv,
        ],
        [
            ((1, tok), jnp.int32),
            (out_grad.shape[1:], BF16),
            (attn_out.shape[1:], BF16),
            (wuv.shape, BF16),
            ((heads, lat, HEAD_DIM), F32),
        ],
        smem=(0,),
        hbm=(1, 2, 3, 4, 5, 6),
        copies=5 + heads,
        limit=PACK_LIMIT,
    )

    def add(a, b):
        return (a.astype(F32) + b.astype(F32)).astype(BF16)

    dp_hops = [(1 << bit, "dp", n_dp) for bit in range((n_dp - 1).bit_length())]
    line_hops = [(GROUP << bit,) for bit in range(line_bits)]

    q_across = swap(q_msg, 2)
    q_core = swap(q_msg, 1)
    pair = add(keep, swap(send, 1))
    got_pair = swap(pair, *dp_hops[0])
    firsts = [swap(after(lat_msg, pair) if bit + 1 < line_bits else lat_msg, GROUP << bit) for bit in range(line_bits)]
    own = call(
        hold_kernel,
        "hold_own",
        [(lat_msg.shape, BF16), (q_msg.shape, BF16), (delta.shape, F32)],
        [lat_msg, q_msg, delta],
    )
    q_core, q_across, firsts, got_pair = lax.optimization_barrier((q_core, q_across, firsts, got_pair))
    held = {0: lat_msg}
    for bit in reversed(range(line_bits)):
        held.update({m | 1 << bit: swap(x, GROUP << bit) for m, x in held.items() if m})
        held[1 << bit] = firsts[bit]
    pair = add(pair, got_pair)
    for step_hop in dp_hops[1:]:
        pair = add(pair, swap(pair, *step_hop))
    lats = [held[m] for m in range(lines)]
    q_far = swap(q_across, 1)
    got_own = swap(pair[heads:], 2)
    q_far, lats, got_own, own = lax.optimization_barrier((q_far, lats, got_own, own))
    lat_own, q_own, delta = own
    lats[0] = lat_own
    qs = [q_own, q_core, q_across, q_far]
    mine = add(pair[:heads], got_own)
    near = swap(mine, *line_hops[0])

    s, k_nat, stat = call(
        functools.partial(score_kernel, factor, lines, width, heads),
        "scores",
        [((keys, all_rows), F32), ((keys, wide), BF16), ((EXTRA, tok), F32)],
        lats + qs + [delta],
        [((wide, keys), BF16), ((wide, rows), BF16)],
        flops=2 * keys * all_rows * wide,
    )
    stats = [stat] + [swap(stat, k) for k in range(1, GROUP)]
    mine = add(mine, after(near, stat))
    for step_hop in line_hops[1:-1]:
        mine = add(mine, swap(mine, *step_hop))
    near = swap(mine, *line_hops[-1])
    g, gp = call(
        functools.partial(context_kernel, width, heads),
        "context",
        [((lat, all_rows), BF16), ((keys, all_rows), F32)],
        qs + [wuv, k_nat],
        flops=2 * keys * all_rows * lat + 2 * all_rows * lat * HEAD_DIM,
    )
    near, stats = lax.optimization_barrier((after(near, gp), stats))
    mine = add(mine, near)
    outs = call(
        functools.partial(grad_kernel, factor, lines, width, heads),
        "gradients",
        [((width, tok), BF16)] * lines
        + [((heads, width, tok), BF16), ((2 * heads, width, tok), BF16), ((heads, width, tok), BF16)],
        lats + qs + stats + [s, gp, g],
        [
            ((width, keys), BF16),
            ((width, all_rows), BF16),
            ((keys, all_rows), BF16),
            ((keys, all_rows), BF16),
        ],
        flops=2 * keys * all_rows * (2 * width + lat),
    )
    parts, (gq_own, gq_core, gq_across) = list(outs[:lines]), outs[lines:]
    gq_got = swap(gq_core, 1)
    gq_sum = add(gq_across, gq_got[heads:])
    gq_last = swap(gq_sum, 2)
    across = swap(after(mine, gq_sum), 2)
    for bit in range(line_bits):
        for m in range(3 << bit, lines, 2 << bit):
            got = swap(parts[m], GROUP << bit)
            parts[m ^ 1 << bit] = add(parts[m ^ 1 << bit], after(got, gq_sum))
    parts[1] = after(parts[1], parts[lines // 2])
    kept = [swap(parts[1 << bit], GROUP << bit) for bit in reversed(range(line_bits))]
    mine_two = jnp.concatenate([mine, after(across, gq_sum)], axis=0)
    other_two = swap(mine_two, 1)
    scale = 1.0 / math.sqrt(tok * n_ctx * n_dp)
    pieces = [mine_two[:heads], other_two[:heads], mine_two[heads:], other_two[heads:]]
    (grad_w,) = call(
        functools.partial(spread_kernel, scale), "spread", [((heads, lat, HEAD_DIM), F32)], [idx] + pieces, smem=(0,)
    )
    grad_lat, grad_q = call(
        sum_kernel,
        "last_sums",
        [((width, tok), BF16), ((heads, width, tok), BF16)],
        [gq_own, gq_got, gq_last, after(parts[0], grad_w)] + kept,
    )
    return (jnp.transpose(grad_q, (2, 0, 1))[None], grad_lat.T[None], grad_w)


def solution(mesh):
    placed = (
        P("dp", "ctx"),
        P("dp", "ctx", None, None),
        P("dp", "ctx", None),
        P("dp", "ctx", None, None),
        P("dp", "ctx", None, None),
        P(),
    )
    return jax.shard_map(
        functools.partial(body, mesh.shape["ctx"], mesh.shape["dp"]),
        mesh=mesh,
        in_specs=placed,
        out_specs=(P("dp", "ctx", None, None), P("dp", "ctx", None), P()),
        check_vma=False,
    )
```

```python
import functools
import math

import jax
import jax.numpy as jnp
from jax import lax
from jax.experimental import pallas as pl
from jax.experimental.pallas import tpu as pltpu
from jax.sharding import PartitionSpec as P

ROPE = 64
HEAD_DIM = 128
GROUP = 4
EXTRA = 16
PACK_LIMIT = 63 << 20
F32 = jnp.float32
BF16 = jnp.bfloat16


def mm(a, b):
    return jnp.dot(a, b, preferred_element_type=F32)


def mm_t(a, b):
    return lax.dot_general(a, b, (((1,), (1,)), ((), ())), preferred_element_type=F32)


def size_of(shape, dtype):
    return math.prod(shape) * jnp.dtype(dtype).itemsize


def call(kernel, name, outs, args, scratch=(), flops=0, smem=(), hbm=(), copies=0, limit=None, share=1):
    def place(i):
        return pltpu.SMEM if i in smem else pltpu.HBM if i in hbm else pltpu.VMEM

    moved = sum(size_of(a.shape, a.dtype) for a in args) + sum(size_of(*o) for o in outs)
    held = moved + sum(size_of(*s) for s in scratch)
    semaphores = [pltpu.SemaphoreType.DMA((copies,))] if copies else []
    return pl.pallas_call(
        kernel,
        out_shape=[jax.ShapeDtypeStruct(s, d) for s, d in outs],
        in_specs=[pl.BlockSpec(memory_space=place(i)) for i in range(len(args))],
        out_specs=[pl.BlockSpec(memory_space=pltpu.VMEM) for _ in outs],
        scratch_shapes=[pltpu.VMEM(s, d) for s, d in scratch] + semaphores,
        compiler_params=pltpu.CompilerParams(vmem_limit_bytes=limit or int(1.2 * held) + (8 << 20)),
        cost_estimate=pl.CostEstimate(flops=flops * share, bytes_accessed=moved * share, transcendentals=0),
        name=name,
    )(*args)


def fetch(pairs, sems):
    copies = [pltpu.make_async_copy(src, dst, sems.at[i]) for i, (src, dst) in enumerate(pairs)]
    for copy in copies:
        copy.start()
    return copies


def pack_kernel(
    idx_ref, pos_hbm, q_hbm, og_hbm, lat_hbm, attn_hbm, wuv_hbm,
    lat_msg, q_msg, delta_ref, keep_ref, send_ref,
    pos_ref, og_ref, attn_ref, wuv_ref, term, sems,
):
    heads, width, tok = q_hbm.shape
    pairs = [(pos_hbm, pos_ref), (og_hbm, og_ref), (wuv_hbm, wuv_ref), (attn_hbm, attn_ref)]
    pairs += [(lat_hbm, lat_msg.at[pl.ds(0, width), :])]
    pairs += [(q_hbm.at[h], q_msg.at[pl.ds(h * width, width), :]) for h in range(heads)]
    copies = [pltpu.make_async_copy(src, dst, sems.at[i]) for i, (src, dst) in enumerate(pairs)]
    for copy in copies:
        copy.start()
    copies[0].wait()
    pos = jnp.broadcast_to(pos_ref[...], (EXTRA, tok))
    row = lax.broadcasted_iota(jnp.int32, (EXTRA, tok), 0)
    high = lax.shift_right_logical(pos, 6)
    both = jnp.where(row == 0, high, jnp.where(row == 1, pos - high * 64, 0))
    rows = both.astype(F32).astype(BF16)
    lat_msg[width:, :] = rows
    q_msg[heads * (width + HEAD_DIM) :, :] = rows
    delta_ref[...] = jnp.zeros_like(delta_ref)
    for copy in copies[1:4]:
        copy.wait()
    _, lat, _ = wuv_ref.shape
    for h in range(heads):
        og = og_ref[:, h, :].T
        at = heads * width + h * HEAD_DIM
        q_msg[at : at + HEAD_DIM, :] = og
        attn = attn_ref[:, h, :].T
        g = mm(wuv_ref[h], og).astype(BF16).astype(F32)
        delta_ref[h : h + 1, :] = jnp.sum(g * attn.astype(F32), axis=0, keepdims=True)
        term[h] = mm_t(attn, og)
    step = lat // GROUP
    me = lax.rem(idx_ref[0], GROUP)
    for k in range(GROUP):
        at = pl.multiple_of(jnp.bitwise_xor(me, k) * step, step)
        target = send_ref if k % 2 else keep_ref
        target[k // 2 * heads : (k // 2 + 1) * heads] = term[:, pl.ds(at, step), :].astype(BF16)
    for copy in copies[4:]:
        copy.wait()


def hold_kernel(*refs):
    half = len(refs) // 2
    for source, target in zip(refs[:half], refs[half:]):
        target[...] = source[...]


def score_kernel(factor, nkey, width, heads, last, *refs):
    lat_refs, refs = refs[:nkey], refs[nkey:]
    tok = lat_refs[0].shape[1]
    rows = heads * tok
    if last:
        q_all_ref, near_ref, delta_ref, s_ref, k_ref, stat_ref, kt = refs
    else:
        q_refs, refs = refs[:GROUP], refs[GROUP:]
        s_ref, k_ref, stat_ref, q_all_ref, kt = refs
        for j in range(GROUP):
            for h in range(heads):
                cols = slice(j * rows + h * tok, j * rows + (h + 1) * tok)
                q_all_ref[:width, cols] = q_refs[j][h * width : (h + 1) * width, :]
                q_all_ref[width : width + EXTRA, cols] = q_refs[j][q_refs[j].shape[0] - EXTRA :, :]
        spare = q_all_ref.shape[0] - width - EXTRA
        q_all_ref[width + EXTRA :, :] = jnp.zeros((spare, GROUP * rows), BF16)
    wide = kt.shape[0]
    for a in range(nkey):
        kt[: width + EXTRA, a * tok : (a + 1) * tok] = lat_refs[a][...]
    kt[width + EXTRA :, :] = jnp.zeros((wide - width - EXTRA, nkey * tok), BF16)
    keys = kt[...].T
    pos = keys[:, wide - 128 :].astype(F32)
    at = width - (wide - 128)
    key_pos = pos[:, at : at + 1] * 64.0 + pos[:, at + 1 : at + 2]
    lane = lax.broadcasted_iota(jnp.int32, keys.shape, 1)
    k_ref[...] = jnp.where(lane < width, keys, jnp.zeros_like(keys))
    stat_ref[...] = jnp.zeros_like(stat_ref)
    if last:
        stat_ref[GROUP * heads : GROUP * heads + heads, :] = delta_ref[:heads, :]
    for j in range(GROUP):
        cols = slice(j * rows, (j + 1) * rows)
        qp = q_all_ref[width : width + EXTRA, cols].astype(F32)
        row_pos = qp[0:1, :] * 64.0 + qp[1:2, :]
        s = mm(k_ref[...], q_all_ref[:, cols]) * factor
        s = jnp.where(key_pos <= row_pos, s, -1e30)
        s_ref[:, cols] = s
        top = jnp.max(s, axis=0, keepdims=True)
        lse = top + jnp.log(jnp.sum(jnp.exp(s - top), axis=0, keepdims=True))
        for h in range(heads):
            at = j * heads + h
            part = lse[:, h * tok : (h + 1) * tok]
            if last:
                near = near_ref[at : at + 1, :]
                most = jnp.maximum(part, near)
                part = most + jnp.log(jnp.exp(part - most) + jnp.exp(near - most))
            stat_ref[at : at + 1, :] = part


def context_kernel(width, heads, *refs):
    q_refs = refs[:GROUP]
    wuv_ref, near_k_ref, last_k_ref, g_ref, near_gp_ref, last_gp_ref = refs[GROUP:]
    lat, all_rows = g_ref.shape
    tok = q_refs[0].shape[1]
    rows = heads * tok
    for j in range(GROUP):
        for h in range(heads):
            at = heads * width + h * HEAD_DIM
            og = q_refs[j][at : at + HEAD_DIM, :]
            col = j * rows + h * tok
            g_ref[:, col : col + tok] = mm(wuv_ref[h], og).astype(BF16)
        cols = slice(j * rows, (j + 1) * rows)
        near_gp_ref[:, cols] = mm(near_k_ref[:, :lat], g_ref[:, cols])
        last_gp_ref[:, cols] = mm(last_k_ref[:, :lat], g_ref[:, cols])


def grad_kernel(factor, nkey, width, heads, last, *refs):
    stats, refs = refs[:GROUP], refs[GROUP:]
    (s_ref, gp_ref, g_ref, q_all_ref), refs = refs[:4], refs[4:]
    if last:
        part_refs, gs_all, p_all = refs[:nkey], refs[nkey], refs[nkey + 1]
    else:
        lat_refs, refs = refs[: nkey + 1], refs[nkey + 1 :]
        last_gs_ref, refs = refs[0], refs[1:]
        part_refs, refs = refs[:nkey], refs[nkey:]
        own_ref, core_ref, across_ref, kt, gs_all, p_all = refs
    lat, all_rows = g_ref.shape
    rows = all_rows // GROUP
    tok = rows // heads
    keys = nkey * tok
    if not last:
        for a in range(nkey + 1):
            kt[:, a * tok : (a + 1) * tok] = lat_refs[a][:width, :]
    for j in range(GROUP):
        cols = slice(j * rows, (j + 1) * rows)
        lse_parts = []
        for k in range(GROUP):
            at = (j ^ k) * heads
            lse_parts.append(
                jnp.concatenate([stats[k][at + h : at + h + 1, :] for h in range(heads)], axis=1)
            )
        top = functools.reduce(jnp.maximum, lse_parts)
        lse = top + jnp.log(sum(jnp.exp(part - top) for part in lse_parts))
        at = GROUP * heads
        delta = jnp.concatenate([stats[j][at + h : at + h + 1, :] for h in range(heads)], axis=1)
        p = jnp.exp(s_ref[:, cols] - lse)
        gs = (p * (gp_ref[:, cols] - delta)).astype(BF16)
        gs_all[:, cols] = gs
        p_all[:, cols] = p.astype(BF16)
        if last:
            continue
        gq = mm(kt[:, :keys], gs) + mm(kt[:, keys:], last_gs_ref[:, cols])
        gq = (gq * factor).astype(BF16)
        for h in range(heads):
            part = gq[:, h * tok : (h + 1) * tok]
            if j == 0:
                own_ref[h] = part
            elif j == 2:
                across_ref[h] = part
            else:
                core_ref[j // 2 * heads + h] = part
    for a in range(nkey):
        at = slice(a * tok, (a + 1) * tok)
        along = mm_t(q_all_ref[:width, :], gs_all[at, :]) * factor
        value = mm_t(g_ref[...], p_all[at, :])
        part_refs[a][:lat, :] = (along[:lat] + value).astype(BF16)
        part_refs[a][lat:, :] = along[lat:].astype(BF16)


def sum_kernel(*refs):
    refs[-1][...] = sum(ref[...].astype(F32) for ref in refs[:-1]).astype(BF16)


def spread_kernel(scale, idx_ref, *refs):
    chunks, out_ref = refs[:GROUP], refs[GROUP]
    step = chunks[0].shape[1]
    me = lax.rem(idx_ref[0], GROUP)
    for k in range(GROUP):
        at = pl.multiple_of(jnp.bitwise_xor(me, k) * step, step)
        out_ref[:, pl.ds(at, step), :] = chunks[k][...].astype(F32) * scale


def body(n_ctx, n_dp, positions, queries, latent, out_grad, attn_out, wuv):
    tok, heads, width = queries.shape[1:]
    lat = attn_out.shape[3]
    lines = n_ctx // GROUP
    line_bits = (lines - 1).bit_length()
    rows = heads * tok
    all_rows = GROUP * rows
    keys = lines * tok
    wide = -(-(width + EXTRA) // 128) * 128
    factor = (HEAD_DIM + ROPE) ** (-0.5)

    def swap(x, mask, axis="ctx", size=n_ctx):
        return lax.ppermute(x, axis, [(i, i ^ mask) for i in range(size)])

    def after(x, *done):
        return lax.optimization_barrier((x, done))[0]

    idx = lax.axis_index("ctx").reshape(1)
    step = lat // GROUP
    lat_msg, q_msg, delta, keep, send = call(
        pack_kernel,
        "pack",
        [
            ((width + EXTRA, tok), BF16),
            ((heads * (width + HEAD_DIM) + EXTRA, tok), BF16),
            ((8, tok), F32),
            ((2 * heads, step, HEAD_DIM), BF16),
            ((2 * heads, step, HEAD_DIM), BF16),
        ],
        [
            idx,
            positions,
            jnp.transpose(queries[0], (1, 2, 0)),
            out_grad[0],
            latent[0].T,
            attn_out[0],
            wuv,
        ],
        [
            ((1, tok), jnp.int32),
            (out_grad.shape[1:], BF16),
            (attn_out.shape[1:], BF16),
            (wuv.shape, BF16),
            ((heads, lat, HEAD_DIM), F32),
        ],
        smem=(0,),
        hbm=(1, 2, 3, 4, 5, 6),
        copies=5 + heads,
        limit=PACK_LIMIT,
    )

    def add(a, b):
        return (a.astype(F32) + b.astype(F32)).astype(BF16)

    dp_hops = [(1 << bit, "dp", n_dp) for bit in range((n_dp - 1).bit_length())]
    line_hops = [(GROUP << bit,) for bit in range(line_bits)]

    q_across = swap(q_msg, 2)
    q_core = swap(q_msg, 1)
    pair = add(keep, swap(send, 1))
    got_pair = swap(pair, *dp_hops[0])
    firsts = [swap(after(lat_msg, pair) if bit + 1 < line_bits else lat_msg, GROUP << bit) for bit in range(line_bits)]
    own = call(
        hold_kernel,
        "hold_own",
        [(lat_msg.shape, BF16), (q_msg.shape, BF16), (delta.shape, F32)],
        [lat_msg, q_msg, delta],
        share=0,
    )
    q_core, q_across, firsts, got_pair, own = lax.optimization_barrier(
        (q_core, q_across, firsts, got_pair, own)
    )
    held = {0: lat_msg}
    for bit in reversed(range(line_bits)):
        held.update({m | 1 << bit: swap(x, GROUP << bit) for m, x in held.items() if m})
        held[1 << bit] = firsts[bit]
    pair = add(pair, got_pair)
    for step_hop in dp_hops[1:]:
        pair = add(pair, swap(pair, *step_hop))
    lats = [held[m] for m in range(lines)]
    q_far = swap(q_across, 1)
    got_own = swap(pair[heads:], 2)
    lat_own, q_own, delta = own
    lats[0] = lat_own
    qs = [q_own, q_core, q_across, q_far]

    most = lines - 1
    keys = most * tok
    score_flops = 2 * tok * all_rows * wide
    near_s, near_k, near_stat, q_all = call(
        functools.partial(score_kernel, factor, most, width, heads, False),
        "near_scores",
        [((keys, all_rows), F32), ((keys, wide), BF16), ((EXTRA, tok), F32), ((wide, all_rows), BF16)],
        lats[:most] + qs,
        [((wide, keys), BF16)],
        flops=most * score_flops,
        share=0,
    )
    mine = add(pair[:heads], after(got_own, near_stat))
    near = swap(mine, *line_hops[0])
    last_s, last_k, stat = call(
        functools.partial(score_kernel, factor, 1, width, heads, True),
        "last_scores",
        [((tok, all_rows), F32), ((tok, wide), BF16), ((EXTRA, tok), F32)],
        [lats[most], q_all, near_stat, delta],
        [((wide, tok), BF16)],
        flops=score_flops,
    )
    stats = [stat] + [swap(stat, k) for k in range(1, GROUP)]
    g, near_gp, last_gp = call(
        functools.partial(context_kernel, width, heads),
        "context",
        [((lat, all_rows), BF16), ((keys, all_rows), F32), ((tok, all_rows), F32)],
        qs + [wuv, near_k, last_k],
        flops=2 * lines * tok * all_rows * lat + 2 * all_rows * lat * HEAD_DIM,
    )
    near, stats = lax.optimization_barrier((after(near, last_gp), stats))
    mine = add(mine, near)
    for step_hop in line_hops[1:-1]:
        mine = add(mine, swap(mine, *step_hop))
    near = swap(mine, *line_hops[-1])
    last_part, last_gs = call(
        functools.partial(grad_kernel, factor, 1, width, heads, True),
        "last_gradients",
        [((width, tok), BF16), ((tok, all_rows), BF16)],
        stats + [last_s, last_gp, g, q_all],
        [((tok, all_rows), BF16)],
        flops=2 * tok * all_rows * (width + lat),
    )
    last_got = swap(last_part, GROUP)
    outs = call(
        functools.partial(grad_kernel, factor, most, width, heads, False),
        "near_gradients",
        [((width, tok), BF16)] * most
        + [((heads, width, tok), BF16), ((2 * heads, width, tok), BF16), ((heads, width, tok), BF16)],
        stats + [near_s, near_gp, g, q_all] + lats + [last_gs],
        [((width, lines * tok), BF16), ((keys, all_rows), BF16), ((keys, all_rows), BF16)],
        flops=2 * keys * all_rows * (width + lat) + 2 * lines * tok * all_rows * width,
    )
    parts, (gq_own, gq_core, gq_across) = list(outs[:most]) + [last_part], outs[most:]
    mine = add(mine, near)
    kept = [parts[0]]
    gq_got = swap(after(gq_core, last_got, near), 1)
    gq_sum = add(gq_across, gq_got[heads:])
    gq_last = swap(gq_sum, 2)
    for bit in range(line_bits):
        for m in range(3 << bit, lines, 2 << bit):
            got = last_got if m == most and bit == 0 else swap(parts[m], GROUP << bit)
            parts[m ^ 1 << bit] = add(parts[m ^ 1 << bit], got)
    pieces = [mine] + [swap(mine, k) for k in range(1, GROUP)]
    parts[1] = after(parts[1], gq_sum)
    kept += [swap(parts[1 << bit], GROUP << bit) for bit in reversed(range(line_bits))]
    scale = 1.0 / math.sqrt(tok * n_ctx * n_dp)
    (grad_w,) = call(
        functools.partial(spread_kernel, scale), "spread", [((heads, lat, HEAD_DIM), F32)], [idx] + pieces, smem=(0,)
    )
    (grad_lat,) = call(sum_kernel, "latent_sum", [((width, tok), BF16)], kept)
    gq_pieces = [gq_own, gq_got[:heads], after(gq_last, grad_lat)]
    (grad_q,) = call(sum_kernel, "query_sum", [((heads, width, tok), BF16)], gq_pieces)
    return (jnp.transpose(grad_q, (2, 0, 1))[None], grad_lat.T[None], grad_w)


def solution(mesh):
    placed = (
        P("dp", "ctx"),
        P("dp", "ctx", None, None),
        P("dp", "ctx", None),
        P("dp", "ctx", None, None),
        P("dp", "ctx", None, None),
        P(),
    )
    return jax.shard_map(
        functools.partial(body, mesh.shape["ctx"], mesh.shape["dp"]),
        mesh=mesh,
        in_specs=placed,
        out_specs=(P("dp", "ctx", None, None), P("dp", "ctx", None), P()),
        check_vma=False,
    )
```

```python
import functools
import math

import jax
import jax.numpy as jnp
from jax import lax
from jax.experimental import pallas as pl
from jax.experimental.pallas import tpu as pltpu
from jax.sharding import PartitionSpec as P

ROPE = 64
HEAD_DIM = 128
GROUP = 4
EXTRA = 16
PACK_LIMIT = 63 << 20
F32 = jnp.float32
BF16 = jnp.bfloat16


def mm(a, b):
    return jnp.dot(a, b, preferred_element_type=F32)


def mm_t(a, b):
    return lax.dot_general(a, b, (((1,), (1,)), ((), ())), preferred_element_type=F32)


def size_of(shape, dtype):
    return math.prod(shape) * jnp.dtype(dtype).itemsize


def call(kernel, name, outs, args, scratch=(), flops=0, smem=(), hbm=(), copies=0, limit=None, share=1, out=pltpu.VMEM):
    def place(i):
        return pltpu.SMEM if i in smem else pltpu.HBM if i in hbm else pltpu.VMEM

    moved = sum(size_of(a.shape, a.dtype) for a in args) + sum(size_of(*o) for o in outs)
    held = moved + sum(size_of(*s) for s in scratch)
    semaphores = [pltpu.SemaphoreType.DMA((copies,))] if copies else []
    return pl.pallas_call(
        kernel,
        out_shape=[jax.ShapeDtypeStruct(s, d) for s, d in outs],
        in_specs=[pl.BlockSpec(memory_space=place(i)) for i in range(len(args))],
        out_specs=[pl.BlockSpec(memory_space=out) for _ in outs],
        scratch_shapes=[pltpu.VMEM(s, d) for s, d in scratch] + semaphores,
        compiler_params=pltpu.CompilerParams(vmem_limit_bytes=limit or int(1.2 * held) + (8 << 20)),
        cost_estimate=pl.CostEstimate(flops=flops * share, bytes_accessed=moved * share, transcendentals=0),
        name=name,
    )(*args)


def fetch(pairs, sems):
    copies = [pltpu.make_async_copy(src, dst, sems.at[i]) for i, (src, dst) in enumerate(pairs)]
    for copy in copies:
        copy.start()
    return copies


def pack_kernel(
    idx_ref, pos_hbm, q_hbm, og_hbm, lat_hbm, attn_hbm, wuv_hbm,
    lat_msg, q_msg, delta_hbm, keep_hbm, send_hbm,
    pos_ref, og_ref, attn_ref, wuv_ref, term, rows_ref, og_t_ref, delta_ref, keep_ref, send_ref, sems,
):
    heads, width, tok = q_hbm.shape
    _, lat, _ = wuv_ref.shape
    started = []

    def send_off(src, dst):
        copy = pltpu.make_async_copy(src, dst, sems.at[len(started)])
        copy.start()
        started.append(copy)

    send_off(og_hbm, og_ref)
    send_off(pos_hbm, pos_ref)
    send_off(attn_hbm, attn_ref)
    send_off(wuv_hbm, wuv_ref)
    send_off(lat_hbm, lat_msg.at[pl.ds(0, width), :])
    for h in range(heads):
        send_off(q_hbm.at[h], q_msg.at[pl.ds(h * width, width), :])
    started[0].wait()
    for h in range(heads):
        og_t_ref[h] = og_ref[:, h, :].T
        send_off(og_t_ref.at[h], q_msg.at[pl.ds(heads * width + h * HEAD_DIM, HEAD_DIM), :])
    started[1].wait()
    pos = jnp.broadcast_to(pos_ref[...], (EXTRA, tok))
    row = lax.broadcasted_iota(jnp.int32, (EXTRA, tok), 0)
    high = lax.shift_right_logical(pos, 6)
    both = jnp.where(row == 0, high, jnp.where(row == 1, pos - high * 64, 0))
    rows_ref[...] = both.astype(F32).astype(BF16)
    send_off(rows_ref, lat_msg.at[pl.ds(width, EXTRA), :])
    send_off(rows_ref, q_msg.at[pl.ds(heads * (width + HEAD_DIM), EXTRA), :])
    delta_ref[...] = jnp.zeros_like(delta_ref)
    started[2].wait()
    attn = [attn_ref[:, h, :].T for h in range(heads)]
    for h in range(heads):
        term[h] = mm_t(attn[h], og_t_ref[h])
    step = lat // GROUP
    me = lax.rem(idx_ref[0], GROUP)
    for k in range(GROUP):
        at = pl.multiple_of(jnp.bitwise_xor(me, k) * step, step)
        target = send_ref if k % 2 else keep_ref
        target[k // 2 * heads : (k // 2 + 1) * heads] = term[:, pl.ds(at, step), :].astype(BF16)
    send_off(send_ref, send_hbm)
    send_off(keep_ref, keep_hbm)
    started[3].wait()
    for h in range(heads):
        g = mm(wuv_ref[h], og_t_ref[h]).astype(BF16).astype(F32)
        delta_ref[h : h + 1, :] = jnp.sum(g * attn[h].astype(F32), axis=0, keepdims=True)
    send_off(delta_ref, delta_hbm)
    for copy in started[4:]:
        copy.wait()


def hold_kernel(*refs):
    half = len(refs) // 2
    for source, target in zip(refs[:half], refs[half:]):
        target[...] = source[...]


def score_kernel(factor, nkey, width, heads, last, *refs):
    lat_refs, refs = refs[:nkey], refs[nkey:]
    tok = lat_refs[0].shape[1]
    rows = heads * tok
    if last:
        q_all_ref, near_ref, delta_ref, s_ref, k_ref, stat_ref, kt = refs
    else:
        q_refs, refs = refs[:GROUP], refs[GROUP:]
        s_ref, k_ref, stat_ref, q_all_ref, kt = refs
        for j in range(GROUP):
            for h in range(heads):
                cols = slice(j * rows + h * tok, j * rows + (h + 1) * tok)
                q_all_ref[:width, cols] = q_refs[j][h * width : (h + 1) * width, :]
                q_all_ref[width : width + EXTRA, cols] = q_refs[j][q_refs[j].shape[0] - EXTRA :, :]
        spare = q_all_ref.shape[0] - width - EXTRA
        q_all_ref[width + EXTRA :, :] = jnp.zeros((spare, GROUP * rows), BF16)
    wide = kt.shape[0]
    for a in range(nkey):
        kt[: width + EXTRA, a * tok : (a + 1) * tok] = lat_refs[a][...]
    kt[width + EXTRA :, :] = jnp.zeros((wide - width - EXTRA, nkey * tok), BF16)
    keys = kt[...].T
    pos = keys[:, wide - 128 :].astype(F32)
    at = width - (wide - 128)
    key_pos = pos[:, at : at + 1] * 64.0 + pos[:, at + 1 : at + 2]
    lane = lax.broadcasted_iota(jnp.int32, keys.shape, 1)
    k_ref[...] = jnp.where(lane < width, keys, jnp.zeros_like(keys))
    stat_ref[...] = jnp.zeros_like(stat_ref)
    if last:
        stat_ref[GROUP * heads : GROUP * heads + heads, :] = delta_ref[:heads, :]
    for j in range(GROUP):
        cols = slice(j * rows, (j + 1) * rows)
        qp = q_all_ref[width : width + EXTRA, cols].astype(F32)
        row_pos = qp[0:1, :] * 64.0 + qp[1:2, :]
        s = mm(k_ref[...], q_all_ref[:, cols]) * factor
        s = jnp.where(key_pos <= row_pos, s, -1e30)
        s_ref[:, cols] = s
        top = jnp.max(s, axis=0, keepdims=True)
        lse = top + jnp.log(jnp.sum(jnp.exp(s - top), axis=0, keepdims=True))
        for h in range(heads):
            at = j * heads + h
            part = lse[:, h * tok : (h + 1) * tok]
            if last:
                near = near_ref[at : at + 1, :]
                most = jnp.maximum(part, near)
                part = most + jnp.log(jnp.exp(part - most) + jnp.exp(near - most))
            stat_ref[at : at + 1, :] = part


def context_kernel(width, heads, *refs):
    q_refs = refs[:GROUP]
    wuv_ref, near_k_ref, last_k_ref, g_ref, near_gp_ref, last_gp_ref = refs[GROUP:]
    lat, all_rows = g_ref.shape
    tok = q_refs[0].shape[1]
    rows = heads * tok
    for j in range(GROUP):
        for h in range(heads):
            at = heads * width + h * HEAD_DIM
            og = q_refs[j][at : at + HEAD_DIM, :]
            col = j * rows + h * tok
            g_ref[:, col : col + tok] = mm(wuv_ref[h], og).astype(BF16)
        cols = slice(j * rows, (j + 1) * rows)
        near_gp_ref[:, cols] = mm(near_k_ref[:, :lat], g_ref[:, cols])
        last_gp_ref[:, cols] = mm(last_k_ref[:, :lat], g_ref[:, cols])


def grad_kernel(factor, nkey, width, heads, last, *refs):
    stats, refs = refs[:GROUP], refs[GROUP:]
    (s_ref, gp_ref, g_ref, q_all_ref), refs = refs[:4], refs[4:]
    if last:
        part_refs, gs_all, p_all = refs[:nkey], refs[nkey], refs[nkey + 1]
    else:
        lat_refs, refs = refs[: nkey + 1], refs[nkey + 1 :]
        last_gs_ref, refs = refs[0], refs[1:]
        part_refs, refs = refs[:nkey], refs[nkey:]
        own_ref, core_ref, across_ref, kt, gs_all, p_all = refs
    lat, all_rows = g_ref.shape
    rows = all_rows // GROUP
    tok = rows // heads
    keys = nkey * tok
    if not last:
        for a in range(nkey + 1):
            kt[:, a * tok : (a + 1) * tok] = lat_refs[a][:width, :]
    for j in range(GROUP):
        cols = slice(j * rows, (j + 1) * rows)
        lse_parts = []
        for k in range(GROUP):
            at = (j ^ k) * heads
            lse_parts.append(
                jnp.concatenate([stats[k][at + h : at + h + 1, :] for h in range(heads)], axis=1)
            )
        top = functools.reduce(jnp.maximum, lse_parts)
        lse = top + jnp.log(sum(jnp.exp(part - top) for part in lse_parts))
        at = GROUP * heads
        delta = jnp.concatenate([stats[j][at + h : at + h + 1, :] for h in range(heads)], axis=1)
        p = jnp.exp(s_ref[:, cols] - lse)
        gs = (p * (gp_ref[:, cols] - delta)).astype(BF16)
        gs_all[:, cols] = gs
        p_all[:, cols] = p.astype(BF16)
        if last:
            continue
        gq = mm(kt[:, :keys], gs) + mm(kt[:, keys:], last_gs_ref[:, cols])
        gq = (gq * factor).astype(BF16)
        for h in range(heads):
            part = gq[:, h * tok : (h + 1) * tok]
            if j == 0:
                own_ref[h] = part
            elif j == 2:
                across_ref[h] = part
            else:
                core_ref[j // 2 * heads + h] = part
    for a in range(nkey):
        at = slice(a * tok, (a + 1) * tok)
        along = mm_t(q_all_ref[:width, :], gs_all[at, :]) * factor
        value = mm_t(g_ref[...], p_all[at, :])
        part_refs[a][:lat, :] = (along[:lat] + value).astype(BF16)
        part_refs[a][lat:, :] = along[lat:].astype(BF16)


def sum_kernel(*refs):
    refs[-1][...] = sum(ref[...].astype(F32) for ref in refs[:-1]).astype(BF16)


def spread_kernel(scale, idx_ref, *refs):
    chunks, out_ref = refs[:GROUP], refs[GROUP]
    step = chunks[0].shape[1]
    me = lax.rem(idx_ref[0], GROUP)
    for k in range(GROUP):
        at = pl.multiple_of(jnp.bitwise_xor(me, k) * step, step)
        out_ref[:, pl.ds(at, step), :] = chunks[k][...].astype(F32) * scale


def body(n_ctx, n_dp, positions, queries, latent, out_grad, attn_out, wuv):
    tok, heads, width = queries.shape[1:]
    lat = attn_out.shape[3]
    lines = n_ctx // GROUP
    line_bits = (lines - 1).bit_length()
    rows = heads * tok
    all_rows = GROUP * rows
    keys = lines * tok
    wide = -(-(width + EXTRA) // 128) * 128
    factor = (HEAD_DIM + ROPE) ** (-0.5)

    def swap(x, mask, axis="ctx", size=n_ctx):
        return lax.ppermute(x, axis, [(i, i ^ mask) for i in range(size)])

    def after(x, *done):
        return lax.optimization_barrier((x, done))[0]

    idx = lax.axis_index("ctx").reshape(1)
    step = lat // GROUP
    lat_msg, q_msg, delta, keep, send = call(
        pack_kernel,
        "pack",
        [
            ((width + EXTRA, tok), BF16),
            ((heads * (width + HEAD_DIM) + EXTRA, tok), BF16),
            ((8, tok), F32),
            ((2 * heads, step, HEAD_DIM), BF16),
            ((2 * heads, step, HEAD_DIM), BF16),
        ],
        [
            idx,
            positions,
            jnp.transpose(queries[0], (1, 2, 0)),
            out_grad[0],
            latent[0].T,
            attn_out[0],
            wuv,
        ],
        [
            ((1, tok), jnp.int32),
            (out_grad.shape[1:], BF16),
            (attn_out.shape[1:], BF16),
            (wuv.shape, BF16),
            ((heads, lat, HEAD_DIM), F32),
            ((EXTRA, tok), BF16),
            ((heads, HEAD_DIM, tok), BF16),
            ((8, tok), F32),
            ((2 * heads, step, HEAD_DIM), BF16),
            ((2 * heads, step, HEAD_DIM), BF16),
        ],
        smem=(0,),
        hbm=(1, 2, 3, 4, 5, 6),
        copies=10 + 2 * heads,
        out=pltpu.HBM,
        limit=PACK_LIMIT,
    )

    def add(a, b):
        return (a.astype(F32) + b.astype(F32)).astype(BF16)

    dp_hops = [(1 << bit, "dp", n_dp) for bit in range((n_dp - 1).bit_length())]
    line_hops = [(GROUP << bit,) for bit in range(line_bits)]

    q_across = swap(q_msg, 2)
    q_core = swap(q_msg, 1)
    pair = add(keep, swap(send, 1))
    got_pair = swap(pair, *dp_hops[0])
    firsts = [swap(after(lat_msg, q_core) if bit + 1 < line_bits else lat_msg, GROUP << bit) for bit in range(line_bits)]
    own = call(
        hold_kernel,
        "hold_own",
        [(lat_msg.shape, BF16), (q_msg.shape, BF16), (delta.shape, F32)],
        [lat_msg, q_msg, delta],
        share=0,
    )
    q_core, q_across, firsts, got_pair, own = lax.optimization_barrier(
        (q_core, q_across, firsts, got_pair, own)
    )
    held = {0: lat_msg}
    for bit in reversed(range(line_bits)):
        held.update({m | 1 << bit: swap(x, GROUP << bit) for m, x in held.items() if m})
        held[1 << bit] = firsts[bit]
    pair = add(pair, got_pair)
    for step_hop in dp_hops[1:]:
        pair = add(pair, swap(pair, *step_hop))
    lats = [held[m] for m in range(lines)]
    q_far = swap(q_across, 1)
    got_own = swap(pair[heads:], 2)
    lat_own, q_own, delta = own
    lats[0] = lat_own
    qs = [q_own, q_core, q_across, q_far]

    most = lines - 1
    keys = most * tok
    score_flops = 2 * tok * all_rows * wide
    near_s, near_k, near_stat, q_all = call(
        functools.partial(score_kernel, factor, most, width, heads, False),
        "near_scores",
        [((keys, all_rows), F32), ((keys, wide), BF16), ((EXTRA, tok), F32), ((wide, all_rows), BF16)],
        lats[:most] + qs,
        [((wide, keys), BF16)],
        flops=most * score_flops,
        share=0,
    )
    mine = add(pair[:heads], after(got_own, near_stat))
    near = swap(mine, *line_hops[0])
    last_s, last_k, stat = call(
        functools.partial(score_kernel, factor, 1, width, heads, True),
        "last_scores",
        [((tok, all_rows), F32), ((tok, wide), BF16), ((EXTRA, tok), F32)],
        [lats[most], q_all, near_stat, delta],
        [((wide, tok), BF16)],
        flops=score_flops,
    )
    stats = [stat] + [swap(stat, k) for k in range(1, GROUP)]
    g, near_gp, last_gp = call(
        functools.partial(context_kernel, width, heads),
        "context",
        [((lat, all_rows), BF16), ((keys, all_rows), F32), ((tok, all_rows), F32)],
        qs + [wuv, near_k, last_k],
        flops=2 * lines * tok * all_rows * lat + 2 * all_rows * lat * HEAD_DIM,
    )
    near, stats = lax.optimization_barrier((after(near, last_gp), stats))
    mine = add(mine, near)
    for step_hop in line_hops[1:-1]:
        mine = add(mine, swap(mine, *step_hop))
    near = swap(mine, *line_hops[-1])
    last_part, last_gs = call(
        functools.partial(grad_kernel, factor, 1, width, heads, True),
        "last_gradients",
        [((width, tok), BF16), ((tok, all_rows), BF16)],
        stats + [last_s, last_gp, g, q_all],
        [((tok, all_rows), BF16)],
        flops=2 * tok * all_rows * (width + lat),
    )
    last_got = swap(last_part, GROUP)
    mine = add(mine, near)
    outs = call(
        functools.partial(grad_kernel, factor, most, width, heads, False),
        "near_gradients",
        [((width, tok), BF16)] * most
        + [((heads, width, tok), BF16), ((2 * heads, width, tok), BF16), ((heads, width, tok), BF16)],
        stats + [near_s, near_gp, g, q_all] + lats + [after(last_gs, mine)],
        [((width, lines * tok), BF16), ((keys, all_rows), BF16), ((keys, all_rows), BF16)],
        flops=2 * keys * all_rows * (width + lat) + 2 * lines * tok * all_rows * width,
    )
    parts, (gq_own, gq_core, gq_across) = list(outs[:most]) + [last_part], outs[most:]
    across = swap(mine, 2)
    kept = [parts[0]]
    gq_got = swap(after(gq_core, last_got, across), 1)
    gq_sum = add(gq_across, gq_got[heads:])
    gq_last = swap(gq_sum, 2)
    for bit in range(line_bits):
        for m in range(3 << bit, lines, 2 << bit):
            got = last_got if m == most and bit == 0 else swap(parts[m], GROUP << bit)
            parts[m ^ 1 << bit] = add(parts[m ^ 1 << bit], got)
    mine_two = jnp.concatenate([mine, across], axis=0)
    other_two = swap(mine_two, 1)
    pieces = [mine_two[:heads], other_two[:heads], mine_two[heads:], other_two[heads:]]
    parts[1] = after(parts[1], gq_sum)
    kept += [swap(parts[1 << bit], GROUP << bit) for bit in reversed(range(line_bits))]
    scale = 1.0 / math.sqrt(tok * n_ctx * n_dp)
    (grad_w,) = call(
        functools.partial(spread_kernel, scale), "spread", [((heads, lat, HEAD_DIM), F32)], [idx] + pieces, smem=(0,)
    )
    (grad_lat,) = call(sum_kernel, "latent_sum", [((width, tok), BF16)], kept, flops=3*10**9)
    gq_pieces = [gq_own, gq_got[:heads], after(gq_last, grad_lat)]
    (grad_q,) = call(sum_kernel, "query_sum", [((heads, width, tok), BF16)], gq_pieces)
    return (jnp.transpose(grad_q, (2, 0, 1))[None], grad_lat.T[None], grad_w)


def solution(mesh):
    placed = (
        P("dp", "ctx"),
        P("dp", "ctx", None, None),
        P("dp", "ctx", None),
        P("dp", "ctx", None, None),
        P("dp", "ctx", None, None),
        P(),
    )
    return jax.shard_map(
        functools.partial(body, mesh.shape["ctx"], mesh.shape["dp"]),
        mesh=mesh,
        in_specs=placed,
        out_specs=(P("dp", "ctx", None, None), P("dp", "ctx", None), P()),
        check_vma=False,
    )
```

```python
import functools
import math

import jax
import jax.numpy as jnp
from jax import lax
from jax.experimental import pallas as pl
from jax.experimental.pallas import tpu as pltpu
from jax.sharding import PartitionSpec as P

ROPE = 64
HEAD_DIM = 128
GROUP = 4
EXTRA = 16
PACK_LIMIT = 63 << 20
F32 = jnp.float32
BF16 = jnp.bfloat16


def mm(a, b):
    return jnp.dot(a, b, preferred_element_type=F32)


def mm_t(a, b):
    return lax.dot_general(a, b, (((1,), (1,)), ((), ())), preferred_element_type=F32)


def size_of(shape, dtype):
    return math.prod(shape) * jnp.dtype(dtype).itemsize


def call(kernel, name, outs, args, scratch=(), flops=0, smem=(), hbm=(), copies=0, limit=None, share=1, out=pltpu.VMEM):
    def place(i):
        return pltpu.SMEM if i in smem else pltpu.HBM if i in hbm else pltpu.VMEM

    moved = sum(size_of(a.shape, a.dtype) for a in args) + sum(size_of(*o) for o in outs)
    held = moved + sum(size_of(*s) for s in scratch)
    semaphores = [pltpu.SemaphoreType.DMA((copies,))] if copies else []
    return pl.pallas_call(
        kernel,
        out_shape=[jax.ShapeDtypeStruct(s, d) for s, d in outs],
        in_specs=[pl.BlockSpec(memory_space=place(i)) for i in range(len(args))],
        out_specs=[pl.BlockSpec(memory_space=out) for _ in outs],
        scratch_shapes=[pltpu.VMEM(s, d) for s, d in scratch] + semaphores,
        compiler_params=pltpu.CompilerParams(vmem_limit_bytes=limit or int(1.2 * held) + (8 << 20)),
        cost_estimate=pl.CostEstimate(flops=flops * share, bytes_accessed=moved * share, transcendentals=0),
        name=name,
    )(*args)


def fetch(pairs, sems):
    copies = [pltpu.make_async_copy(src, dst, sems.at[i]) for i, (src, dst) in enumerate(pairs)]
    for copy in copies:
        copy.start()
    return copies


def pack_kernel(
    idx_ref, pos_hbm, q_hbm, og_hbm, lat_hbm, attn_hbm, wuv_hbm,
    lat_msg, q_msg, delta_hbm, keep_hbm, send_hbm,
    pos_ref, og_ref, attn_ref, wuv_ref, term, rows_ref, og_t_ref, delta_ref, keep_ref, send_ref,
    lat_ref, q_ref, sems,
):
    heads, width, tok = q_hbm.shape
    _, lat, _ = wuv_ref.shape
    started = []

    def send_off(src, dst):
        copy = pltpu.make_async_copy(src, dst, sems.at[len(started)])
        copy.start()
        started.append(copy)

    send_off(og_hbm, og_ref)
    send_off(pos_hbm, pos_ref)
    send_off(attn_hbm, attn_ref)
    send_off(wuv_hbm, wuv_ref)
    send_off(lat_hbm, lat_ref)
    for h in range(heads):
        send_off(q_hbm.at[h], q_ref.at[h])
    started[0].wait()
    for h in range(heads):
        og_t_ref[h] = og_ref[:, h, :].T
        send_off(og_t_ref.at[h], q_msg.at[pl.ds(heads * width + h * HEAD_DIM, HEAD_DIM), :])
    started[1].wait()
    pos = jnp.broadcast_to(pos_ref[...], (EXTRA, tok))
    row = lax.broadcasted_iota(jnp.int32, (EXTRA, tok), 0)
    high = lax.shift_right_logical(pos, 6)
    both = jnp.where(row == 0, high, jnp.where(row == 1, pos - high * 64, 0))
    rows_ref[...] = both.astype(F32).astype(BF16)
    send_off(rows_ref, lat_msg.at[pl.ds(width, EXTRA), :])
    send_off(rows_ref, q_msg.at[pl.ds(heads * (width + HEAD_DIM), EXTRA), :])
    started[4].wait()
    send_off(lat_ref, lat_msg.at[pl.ds(0, width), :])
    for h in range(heads):
        started[5 + h].wait()
        send_off(q_ref.at[h], q_msg.at[pl.ds(h * width, width), :])
    delta_ref[...] = jnp.zeros_like(delta_ref)
    started[2].wait()
    attn = [attn_ref[:, h, :].T for h in range(heads)]
    for h in range(heads):
        term[h] = mm_t(attn[h], og_t_ref[h])
    step = lat // GROUP
    me = lax.rem(idx_ref[0], GROUP)
    for k in range(GROUP):
        at = pl.multiple_of(jnp.bitwise_xor(me, k) * step, step)
        target = send_ref if k % 2 else keep_ref
        target[k // 2 * heads : (k // 2 + 1) * heads] = term[:, pl.ds(at, step), :].astype(BF16)
    send_off(send_ref, send_hbm)
    send_off(keep_ref, keep_hbm)
    started[3].wait()
    for h in range(heads):
        g = mm(wuv_ref[h], og_t_ref[h]).astype(BF16).astype(F32)
        delta_ref[h : h + 1, :] = jnp.sum(g * attn[h].astype(F32), axis=0, keepdims=True)
    send_off(delta_ref, delta_hbm)
    for copy in started[5 + heads :]:
        copy.wait()


def hold_kernel(*refs):
    half = len(refs) // 2
    for source, target in zip(refs[:half], refs[half:]):
        target[...] = source[...]


def score_kernel(factor, nkey, width, heads, last, *refs):
    lat_refs, refs = refs[:nkey], refs[nkey:]
    tok = lat_refs[0].shape[1]
    rows = heads * tok
    if last:
        q_all_ref, near_ref, delta_ref, s_ref, k_ref, stat_ref, kt = refs
    else:
        q_refs, refs = refs[:GROUP], refs[GROUP:]
        s_ref, k_ref, stat_ref, q_all_ref, kt = refs
        for j in range(GROUP):
            for h in range(heads):
                cols = slice(j * rows + h * tok, j * rows + (h + 1) * tok)
                q_all_ref[:width, cols] = q_refs[j][h * width : (h + 1) * width, :]
                q_all_ref[width : width + EXTRA, cols] = q_refs[j][q_refs[j].shape[0] - EXTRA :, :]
        spare = q_all_ref.shape[0] - width - EXTRA
        q_all_ref[width + EXTRA :, :] = jnp.zeros((spare, GROUP * rows), BF16)
    wide = kt.shape[0]
    for a in range(nkey):
        kt[: width + EXTRA, a * tok : (a + 1) * tok] = lat_refs[a][...]
    kt[width + EXTRA :, :] = jnp.zeros((wide - width - EXTRA, nkey * tok), BF16)
    keys = kt[...].T
    pos = keys[:, wide - 128 :].astype(F32)
    at = width - (wide - 128)
    key_pos = pos[:, at : at + 1] * 64.0 + pos[:, at + 1 : at + 2]
    lane = lax.broadcasted_iota(jnp.int32, keys.shape, 1)
    k_ref[...] = jnp.where(lane < width, keys, jnp.zeros_like(keys))
    stat_ref[...] = jnp.zeros_like(stat_ref)
    if last:
        stat_ref[GROUP * heads : GROUP * heads + heads, :] = delta_ref[:heads, :]
    for j in range(GROUP):
        cols = slice(j * rows, (j + 1) * rows)
        qp = q_all_ref[width : width + EXTRA, cols].astype(F32)
        row_pos = qp[0:1, :] * 64.0 + qp[1:2, :]
        s = mm(k_ref[...], q_all_ref[:, cols]) * factor
        s = jnp.where(key_pos <= row_pos, s, -1e30)
        s_ref[:, cols] = s
        top = jnp.max(s, axis=0, keepdims=True)
        lse = top + jnp.log(jnp.sum(jnp.exp(s - top), axis=0, keepdims=True))
        for h in range(heads):
            at = j * heads + h
            part = lse[:, h * tok : (h + 1) * tok]
            if last:
                near = near_ref[at : at + 1, :]
                most = jnp.maximum(part, near)
                part = most + jnp.log(jnp.exp(part - most) + jnp.exp(near - most))
            stat_ref[at : at + 1, :] = part


def context_kernel(width, heads, *refs):
    q_refs = refs[:GROUP]
    wuv_ref, near_k_ref, last_k_ref, g_ref, near_gp_ref, last_gp_ref = refs[GROUP:]
    lat, all_rows = g_ref.shape
    tok = q_refs[0].shape[1]
    rows = heads * tok
    for j in range(GROUP):
        for h in range(heads):
            at = heads * width + h * HEAD_DIM
            og = q_refs[j][at : at + HEAD_DIM, :]
            col = j * rows + h * tok
            g_ref[:, col : col + tok] = mm(wuv_ref[h], og).astype(BF16)
        cols = slice(j * rows, (j + 1) * rows)
        near_gp_ref[:, cols] = mm(near_k_ref[:, :lat], g_ref[:, cols])
        last_gp_ref[:, cols] = mm(last_k_ref[:, :lat], g_ref[:, cols])


def grad_kernel(factor, nkey, width, heads, last, *refs):
    stats, refs = refs[:GROUP], refs[GROUP:]
    (s_ref, gp_ref, g_ref, q_all_ref), refs = refs[:4], refs[4:]
    if last:
        part_refs, gs_all, p_all = refs[:nkey], refs[nkey], refs[nkey + 1]
    else:
        lat_refs, refs = refs[: nkey + 1], refs[nkey + 1 :]
        last_gs_ref, refs = refs[0], refs[1:]
        part_refs, refs = refs[:nkey], refs[nkey:]
        own_ref, core_ref, across_ref, kt, gs_all, p_all = refs
    lat, all_rows = g_ref.shape
    rows = all_rows // GROUP
    tok = rows // heads
    keys = nkey * tok
    if not last:
        for a in range(nkey + 1):
            kt[:, a * tok : (a + 1) * tok] = lat_refs[a][:width, :]
    for j in range(GROUP):
        cols = slice(j * rows, (j + 1) * rows)
        lse_parts = []
        for k in range(GROUP):
            at = (j ^ k) * heads
            lse_parts.append(
                jnp.concatenate([stats[k][at + h : at + h + 1, :] for h in range(heads)], axis=1)
            )
        top = functools.reduce(jnp.maximum, lse_parts)
        lse = top + jnp.log(sum(jnp.exp(part - top) for part in lse_parts))
        at = GROUP * heads
        delta = jnp.concatenate([stats[j][at + h : at + h + 1, :] for h in range(heads)], axis=1)
        p = jnp.exp(s_ref[:, cols] - lse)
        gs = (p * (gp_ref[:, cols] - delta)).astype(BF16)
        gs_all[:, cols] = gs
        p_all[:, cols] = p.astype(BF16)
        if last:
            continue
        gq = mm(kt[:, :keys], gs) + mm(kt[:, keys:], last_gs_ref[:, cols])
        gq = (gq * factor).astype(BF16)
        for h in range(heads):
            part = gq[:, h * tok : (h + 1) * tok]
            if j == 0:
                own_ref[h] = part
            elif j == 2:
                across_ref[h] = part
            else:
                core_ref[j // 2 * heads + h] = part
    for a in range(nkey):
        at = slice(a * tok, (a + 1) * tok)
        along = mm_t(q_all_ref[:width, :], gs_all[at, :]) * factor
        value = mm_t(g_ref[...], p_all[at, :])
        part_refs[a][:lat, :] = (along[:lat] + value).astype(BF16)
        part_refs[a][lat:, :] = along[lat:].astype(BF16)


def sum_kernel(*refs):
    refs[-1][...] = sum(ref[...].astype(F32) for ref in refs[:-1]).astype(BF16)


def spread_kernel(scale, idx_ref, *refs):
    chunks, out_ref = refs[:GROUP], refs[GROUP]
    step = chunks[0].shape[1]
    me = lax.rem(idx_ref[0], GROUP)
    for k in range(GROUP):
        at = pl.multiple_of(jnp.bitwise_xor(me, k) * step, step)
        out_ref[:, pl.ds(at, step), :] = chunks[k][...].astype(F32) * scale


def body(n_ctx, n_dp, positions, queries, latent, out_grad, attn_out, wuv):
    tok, heads, width = queries.shape[1:]
    lat = attn_out.shape[3]
    lines = n_ctx // GROUP
    line_bits = (lines - 1).bit_length()
    rows = heads * tok
    all_rows = GROUP * rows
    keys = lines * tok
    wide = -(-(width + EXTRA) // 128) * 128
    factor = (HEAD_DIM + ROPE) ** (-0.5)

    def swap(x, mask, axis="ctx", size=n_ctx):
        return lax.ppermute(x, axis, [(i, i ^ mask) for i in range(size)])

    def after(x, *done):
        return lax.optimization_barrier((x, done))[0]

    idx = lax.axis_index("ctx").reshape(1)
    step = lat // GROUP
    lat_msg, q_msg, delta, keep, send = call(
        pack_kernel,
        "pack",
        [
            ((width + EXTRA, tok), BF16),
            ((heads * (width + HEAD_DIM) + EXTRA, tok), BF16),
            ((8, tok), F32),
            ((2 * heads, step, HEAD_DIM), BF16),
            ((2 * heads, step, HEAD_DIM), BF16),
        ],
        [
            idx,
            positions,
            jnp.transpose(queries[0], (1, 2, 0)),
            out_grad[0],
            latent[0].T,
            attn_out[0],
            wuv,
        ],
        [
            ((1, tok), jnp.int32),
            (out_grad.shape[1:], BF16),
            (attn_out.shape[1:], BF16),
            (wuv.shape, BF16),
            ((heads, lat, HEAD_DIM), F32),
            ((EXTRA, tok), BF16),
            ((heads, HEAD_DIM, tok), BF16),
            ((8, tok), F32),
            ((2 * heads, step, HEAD_DIM), BF16),
            ((2 * heads, step, HEAD_DIM), BF16),
            ((width, tok), BF16),
            ((heads, width, tok), BF16),
        ],
        smem=(0,),
        hbm=(1, 2, 3, 4, 5, 6),
        copies=11 + 3 * heads,
        out=pltpu.HBM,
        limit=PACK_LIMIT,
    )

    def add(a, b):
        return (a.astype(F32) + b.astype(F32)).astype(BF16)

    dp_hops = [(1 << bit, "dp", n_dp) for bit in range((n_dp - 1).bit_length())]
    line_hops = [(GROUP << bit,) for bit in range(line_bits)]

    q_across = swap(q_msg, 2)
    q_core = swap(q_msg, 1)
    pair = add(keep, swap(send, 1))
    got_pair = swap(pair, *dp_hops[0])
    firsts = [swap(after(lat_msg, q_core) if bit + 1 < line_bits else lat_msg, GROUP << bit) for bit in range(line_bits)]
    own = call(
        hold_kernel,
        "hold_own",
        [(lat_msg.shape, BF16), (q_msg.shape, BF16), (delta.shape, F32)],
        [lat_msg, q_msg, delta],
        share=0,
    )
    q_core, q_across, firsts, got_pair, own = lax.optimization_barrier(
        (q_core, q_across, firsts, got_pair, own)
    )
    held = {0: lat_msg}
    for bit in reversed(range(line_bits)):
        held.update({m | 1 << bit: swap(x, GROUP << bit) for m, x in held.items() if m})
        held[1 << bit] = firsts[bit]
    pair = add(pair, got_pair)
    for step_hop in dp_hops[1:]:
        pair = add(pair, swap(pair, *step_hop))
    lats = [held[m] for m in range(lines)]
    q_far = swap(q_across, 1)
    got_own = swap(pair[heads:], 2)
    lat_own, q_own, delta = own
    lats[0] = lat_own
    qs = [q_own, q_core, q_across, q_far]

    most = lines - 1
    keys = most * tok
    score_flops = 2 * tok * all_rows * wide
    near_s, near_k, near_stat, q_all = call(
        functools.partial(score_kernel, factor, most, width, heads, False),
        "near_scores",
        [((keys, all_rows), F32), ((keys, wide), BF16), ((EXTRA, tok), F32), ((wide, all_rows), BF16)],
        lats[:most] + qs,
        [((wide, keys), BF16)],
        flops=most * score_flops,
        share=0,
    )
    mine = add(pair[:heads], after(got_own, near_stat))
    near = swap(mine, *line_hops[0])
    last_s, last_k, stat = call(
        functools.partial(score_kernel, factor, 1, width, heads, True),
        "last_scores",
        [((tok, all_rows), F32), ((tok, wide), BF16), ((EXTRA, tok), F32)],
        [lats[most], q_all, near_stat, delta],
        [((wide, tok), BF16)],
        flops=score_flops,
    )
    stats = [stat] + [swap(stat, k) for k in range(1, GROUP)]
    g, near_gp, last_gp = call(
        functools.partial(context_kernel, width, heads),
        "context",
        [((lat, all_rows), BF16), ((keys, all_rows), F32), ((tok, all_rows), F32)],
        qs + [wuv, near_k, last_k],
        flops=2 * lines * tok * all_rows * lat + 2 * all_rows * lat * HEAD_DIM,
    )
    mine = add(mine, after(near, stat))
    for step_hop in line_hops[1:-1]:
        mine = add(mine, swap(mine, *step_hop))
    near = swap(mine, *line_hops[-1])
    last_part, last_gs = call(
        functools.partial(grad_kernel, factor, 1, width, heads, True),
        "last_gradients",
        [((width, tok), BF16), ((tok, all_rows), BF16)],
        stats + [last_s, last_gp, g, q_all],
        [((tok, all_rows), BF16)],
        flops=2 * tok * all_rows * (width + lat),
    )
    last_got = swap(last_part, GROUP)
    mine = add(mine, near)
    outs = call(
        functools.partial(grad_kernel, factor, most, width, heads, False),
        "near_gradients",
        [((width, tok), BF16)] * most
        + [((heads, width, tok), BF16), ((2 * heads, width, tok), BF16), ((heads, width, tok), BF16)],
        stats + [near_s, near_gp, g, q_all] + lats + [after(last_gs, mine)],
        [((width, lines * tok), BF16), ((keys, all_rows), BF16), ((keys, all_rows), BF16)],
        flops=2 * keys * all_rows * (width + lat) + 2 * lines * tok * all_rows * width,
    )
    parts, (gq_own, gq_core, gq_across) = list(outs[:most]) + [last_part], outs[most:]
    across = swap(mine, 2)
    kept = [parts[0]]
    gq_got = swap(after(gq_core, last_got, across), 1)
    gq_sum = add(gq_across, gq_got[heads:])
    gq_last = swap(gq_sum, 2)
    for bit in range(line_bits):
        for m in range(3 << bit, lines, 2 << bit):
            got = last_got if m == most and bit == 0 else swap(parts[m], GROUP << bit)
            parts[m ^ 1 << bit] = add(parts[m ^ 1 << bit], got)
    mine_two = jnp.concatenate([mine, across], axis=0)
    other_two = swap(mine_two, 1)
    pieces = [mine_two[:heads], other_two[:heads], mine_two[heads:], other_two[heads:]]
    parts[1] = after(parts[1], gq_sum)
    kept += [swap(parts[1 << bit], GROUP << bit) for bit in reversed(range(line_bits))]
    scale = 1.0 / math.sqrt(tok * n_ctx * n_dp)
    (grad_w,) = call(
        functools.partial(spread_kernel, scale), "spread", [((heads, lat, HEAD_DIM), F32)], [idx] + pieces, smem=(0,)
    )
    (grad_lat,) = call(sum_kernel, "latent_sum", [((width, tok), BF16)], kept, flops=3*10**9)
    gq_pieces = [gq_own, gq_got[:heads], after(gq_last, grad_lat)]
    (grad_q,) = call(sum_kernel, "query_sum", [((heads, width, tok), BF16)], gq_pieces)
    return (jnp.transpose(grad_q, (2, 0, 1))[None], grad_lat.T[None], grad_w)


def solution(mesh):
    placed = (
        P("dp", "ctx"),
        P("dp", "ctx", None, None),
        P("dp", "ctx", None),
        P("dp", "ctx", None, None),
        P("dp", "ctx", None, None),
        P(),
    )
    return jax.shard_map(
        functools.partial(body, mesh.shape["ctx"], mesh.shape["dp"]),
        mesh=mesh,
        in_specs=placed,
        out_specs=(P("dp", "ctx", None, None), P("dp", "ctx", None), P()),
        check_vma=False,
    )
```

```python
import functools
import math

import jax
import jax.numpy as jnp
from jax import lax
from jax.experimental import pallas as pl
from jax.experimental.pallas import tpu as pltpu
from jax.sharding import PartitionSpec as P

ROPE = 64
HEAD_DIM = 128
GROUP = 4
EXTRA = 16
CUTS = 2
PACK_LIMIT = 63 << 20
F32 = jnp.float32
BF16 = jnp.bfloat16


def mm(a, b):
    return jnp.dot(a, b, preferred_element_type=F32)


def mm_t(a, b):
    return lax.dot_general(a, b, (((1,), (1,)), ((), ())), preferred_element_type=F32)


def size_of(shape, dtype):
    return math.prod(shape) * jnp.dtype(dtype).itemsize


def call(kernel, name, outs, args, scratch=(), flops=0, smem=(), hbm=(), copies=0, limit=None, share=1, out=pltpu.VMEM):
    def place(i):
        return pltpu.SMEM if i in smem else pltpu.HBM if i in hbm else pltpu.VMEM

    moved = sum(size_of(a.shape, a.dtype) for a in args) + sum(size_of(*o) for o in outs)
    held = moved + sum(size_of(*s) for s in scratch)
    semaphores = [pltpu.SemaphoreType.DMA((copies,))] if copies else []
    return pl.pallas_call(
        kernel,
        out_shape=[jax.ShapeDtypeStruct(s, d) for s, d in outs],
        in_specs=[pl.BlockSpec(memory_space=place(i)) for i in range(len(args))],
        out_specs=[pl.BlockSpec(memory_space=out) for _ in outs],
        scratch_shapes=[pltpu.VMEM(s, d) for s, d in scratch] + semaphores,
        compiler_params=pltpu.CompilerParams(vmem_limit_bytes=limit or int(1.2 * held) + (8 << 20)),
        cost_estimate=pl.CostEstimate(flops=flops * share, bytes_accessed=moved * share, transcendentals=0),
        name=name,
    )(*args)


def fetch(pairs, sems):
    copies = [pltpu.make_async_copy(src, dst, sems.at[i]) for i, (src, dst) in enumerate(pairs)]
    for copy in copies:
        copy.start()
    return copies


def pack_kernel(
    idx_ref, pos_hbm, q_hbm, og_hbm, lat_hbm, attn_hbm, wuv_hbm,
    lat_msg, q_msg, delta_hbm, keep_hbm, send_hbm,
    pos_ref, og_ref, attn_ref, wuv_ref, term, rows_ref, og_t_ref, delta_ref, keep_ref, send_ref,
    lat_ref, q_ref, sems,
):
    heads, width, tok = q_hbm.shape
    _, lat, _ = wuv_ref.shape
    started = []

    def send_off(src, dst):
        copy = pltpu.make_async_copy(src, dst, sems.at[len(started)])
        copy.start()
        started.append(copy)

    send_off(og_hbm, og_ref)
    send_off(pos_hbm, pos_ref)
    send_off(attn_hbm, attn_ref)
    send_off(wuv_hbm, wuv_ref)
    send_off(lat_hbm, lat_ref)
    for h in range(heads):
        send_off(q_hbm.at[h], q_ref.at[h])
    started[0].wait()
    for h in range(heads):
        og_t_ref[h] = og_ref[:, h, :].T
        send_off(og_t_ref.at[h], q_msg.at[pl.ds(heads * width + h * HEAD_DIM, HEAD_DIM), :])
    started[1].wait()
    pos = jnp.broadcast_to(pos_ref[...], (EXTRA, tok))
    row = lax.broadcasted_iota(jnp.int32, (EXTRA, tok), 0)
    high = lax.shift_right_logical(pos, 6)
    both = jnp.where(row == 0, high, jnp.where(row == 1, pos - high * 64, 0))
    rows_ref[...] = both.astype(F32).astype(BF16)
    send_off(rows_ref, lat_msg.at[pl.ds(width, EXTRA), :])
    send_off(rows_ref, q_msg.at[pl.ds(heads * (width + HEAD_DIM), EXTRA), :])
    started[4].wait()
    send_off(lat_ref, lat_msg.at[pl.ds(0, width), :])
    for h in range(heads):
        started[5 + h].wait()
        send_off(q_ref.at[h], q_msg.at[pl.ds(h * width, width), :])
    delta_ref[...] = jnp.zeros_like(delta_ref)
    started[2].wait()
    attn = [attn_ref[:, h, :].T for h in range(heads)]
    for h in range(heads):
        term[h] = mm_t(attn[h], og_t_ref[h])
    step = lat // GROUP
    side = lax.rem(idx_ref[0], 2)
    for i in range(GROUP // 2):
        rows = slice(i * heads, (i + 1) * heads)
        at = pl.multiple_of((2 * i + side) * step, step)
        keep_ref[rows] = term[:, pl.ds(at, step), :].astype(BF16)
        at = pl.multiple_of((2 * i + 1 - side) * step, step)
        send_ref[rows] = term[:, pl.ds(at, step), :].astype(BF16)
    send_off(send_ref, send_hbm)
    send_off(keep_ref, keep_hbm)
    started[3].wait()
    for h in range(heads):
        g = mm(wuv_ref[h], og_t_ref[h]).astype(BF16).astype(F32)
        delta_ref[h : h + 1, :] = jnp.sum(g * attn[h].astype(F32), axis=0, keepdims=True)
    send_off(delta_ref, delta_hbm)
    for copy in started[5 + heads :]:
        copy.wait()


def hold_kernel(*refs):
    half = len(refs) // 2
    for source, target in zip(refs[:half], refs[half:]):
        target[...] = source[...]


def score_kernel(factor, nkey, width, heads, last, *refs):
    lat_refs, refs = refs[:nkey], refs[nkey:]
    tok = lat_refs[0].shape[1]
    rows = heads * tok
    if last:
        q_all_ref, near_ref, delta_ref, s_ref, k_ref, stat_ref, kt = refs
    else:
        q_refs, refs = refs[:GROUP], refs[GROUP:]
        s_ref, k_ref, stat_ref, q_all_ref, kt = refs
        for j in range(GROUP):
            for h in range(heads):
                cols = slice(j * rows + h * tok, j * rows + (h + 1) * tok)
                q_all_ref[:width, cols] = q_refs[j][h * width : (h + 1) * width, :]
                q_all_ref[width : width + EXTRA, cols] = q_refs[j][q_refs[j].shape[0] - EXTRA :, :]
        spare = q_all_ref.shape[0] - width - EXTRA
        q_all_ref[width + EXTRA :, :] = jnp.zeros((spare, GROUP * rows), BF16)
    wide = kt.shape[0]
    for a in range(nkey):
        kt[: width + EXTRA, a * tok : (a + 1) * tok] = lat_refs[a][...]
    kt[width + EXTRA :, :] = jnp.zeros((wide - width - EXTRA, nkey * tok), BF16)
    keys = kt[...].T
    pos = keys[:, wide - 128 :].astype(F32)
    at = width - (wide - 128)
    key_pos = pos[:, at : at + 1] * 64.0 + pos[:, at + 1 : at + 2]
    lane = lax.broadcasted_iota(jnp.int32, keys.shape, 1)
    k_ref[...] = jnp.where(lane < width, keys, jnp.zeros_like(keys))
    stat_ref[...] = jnp.zeros_like(stat_ref)
    if last:
        stat_ref[GROUP * heads : GROUP * heads + heads, :] = delta_ref[:heads, :]
    for j in range(GROUP):
        cols = slice(j * rows, (j + 1) * rows)
        qp = q_all_ref[width : width + EXTRA, cols].astype(F32)
        row_pos = qp[0:1, :] * 64.0 + qp[1:2, :]
        s = mm(k_ref[...], q_all_ref[:, cols]) * factor
        s = jnp.where(key_pos <= row_pos, s, -1e30)
        s_ref[:, cols] = s
        top = jnp.max(s, axis=0, keepdims=True)
        lse = top + jnp.log(jnp.sum(jnp.exp(s - top), axis=0, keepdims=True))
        for h in range(heads):
            at = j * heads + h
            part = lse[:, h * tok : (h + 1) * tok]
            if last:
                near = near_ref[at : at + 1, :]
                most = jnp.maximum(part, near)
                part = most + jnp.log(jnp.exp(part - most) + jnp.exp(near - most))
            stat_ref[at : at + 1, :] = part


def context_kernel(width, heads, *refs):
    q_refs = refs[:GROUP]
    wuv_ref, near_k_ref, last_k_ref, g_ref, near_gp_ref, last_gp_ref = refs[GROUP:]
    lat, all_rows = g_ref.shape
    tok = q_refs[0].shape[1]
    rows = heads * tok
    for j in range(GROUP):
        for h in range(heads):
            at = heads * width + h * HEAD_DIM
            og = q_refs[j][at : at + HEAD_DIM, :]
            col = j * rows + h * tok
            g_ref[:, col : col + tok] = mm(wuv_ref[h], og).astype(BF16)
        cols = slice(j * rows, (j + 1) * rows)
        near_gp_ref[:, cols] = mm(near_k_ref[:, :lat], g_ref[:, cols])
        last_gp_ref[:, cols] = mm(last_k_ref[:, :lat], g_ref[:, cols])


def pair_kernel(heads, *refs):
    stats, (s_ref, gp_ref, gs_ref, p_ref) = refs[:GROUP], refs[GROUP : GROUP + 4]
    all_rows = s_ref.shape[1]
    rows = all_rows // GROUP
    for j in range(GROUP):
        cols = slice(j * rows, (j + 1) * rows)
        lse_parts = []
        for k in range(GROUP):
            at = (j ^ k) * heads
            lse_parts.append(
                jnp.concatenate([stats[k][at + h : at + h + 1, :] for h in range(heads)], axis=1)
            )
        top = functools.reduce(jnp.maximum, lse_parts)
        lse = top + jnp.log(sum(jnp.exp(part - top) for part in lse_parts))
        at = GROUP * heads
        delta = jnp.concatenate([stats[j][at + h : at + h + 1, :] for h in range(heads)], axis=1)
        p = jnp.exp(s_ref[:, cols] - lse)
        gs_ref[:, cols] = (p * (gp_ref[:, cols] - delta)).astype(BF16)
        p_ref[:, cols] = p.astype(BF16)


def partial_kernel(factor, nkey, width, g_ref, q_all_ref, gs_ref, p_ref, *part_refs):
    lat = g_ref.shape[0]
    tok = part_refs[0].shape[1]
    for a in range(nkey):
        at = slice(a * tok, (a + 1) * tok)
        along = mm_t(q_all_ref[:width, :], gs_ref[at, :]) * factor
        value = mm_t(g_ref[...], p_ref[at, :])
        part_refs[a][:lat, :] = (along[:lat] + value).astype(BF16)
        part_refs[a][lat:, :] = along[lat:].astype(BF16)


def last_kernel(factor, width, heads, *refs):
    stats, refs = refs[:GROUP], refs[GROUP:]
    s_ref, gp_ref, g_ref, q_all_ref, part_ref, gs_ref, p_ref = refs
    pair_kernel(heads, *stats, s_ref, gp_ref, gs_ref, p_ref)
    partial_kernel(factor, 1, width, g_ref, q_all_ref, gs_ref, p_ref, part_ref)


def query_kernel(factor, nkey, width, heads, *refs):
    stats, refs = refs[:GROUP], refs[GROUP:]
    (s_ref, gp_ref, last_gs_ref), refs = refs[:3], refs[3:]
    lat_refs, refs = refs[:nkey], refs[nkey:]
    gq_refs, far_refs, (gs_ref, p_ref, kt) = refs[: GROUP - 1], refs[GROUP - 1 : -3], refs[-3:]
    cut = far_refs[0].shape[0]
    cuts = width // cut
    tok = lat_refs[0].shape[1]
    keys = s_ref.shape[0]
    rows = heads * tok
    for a in range(nkey):
        kt[:, a * tok : (a + 1) * tok] = lat_refs[a][:width, :]
    pair_kernel(heads, *stats, s_ref, gp_ref, gs_ref, p_ref)
    for j in range(GROUP):
        cols = slice(j * rows, (j + 1) * rows)
        gq = mm(kt[:, :keys], gs_ref[:, cols]) + mm(kt[:, keys:], last_gs_ref[:, cols])
        gq = (gq * factor).astype(BF16)
        for h in range(heads):
            part = gq[:, h * tok : (h + 1) * tok]
            if j < GROUP - 1:
                gq_refs[j][h] = part
            else:
                for c in range(cuts):
                    far_refs[h * cuts + c][...] = part[c * cut : (c + 1) * cut]


def join_kernel(whole_ref, *refs):
    pieces, out_ref = refs[:-1], refs[-1]
    cut = pieces[0].shape[0]
    cuts = whole_ref.shape[1] // cut
    for i, piece in enumerate(pieces):
        at = (i // cuts, slice(i % cuts * cut, (i % cuts + 1) * cut))
        out_ref[at] = (whole_ref[at].astype(F32) + piece[...].astype(F32)).astype(BF16)


def sum_kernel(*refs):
    refs[-1][...] = sum(ref[...].astype(F32) for ref in refs[:-1]).astype(BF16)


def spread_kernel(scale, idx_ref, mine_ref, other_ref, out_ref):
    heads, lat, _ = out_ref.shape
    step = lat // GROUP
    side = lax.rem(idx_ref[0], 2)
    for i in range(GROUP // 2):
        rows = slice(i * heads, (i + 1) * heads)
        at = pl.multiple_of((2 * i + side) * step, step)
        out_ref[:, pl.ds(at, step), :] = mine_ref[rows].astype(F32) * scale
        at = pl.multiple_of((2 * i + 1 - side) * step, step)
        out_ref[:, pl.ds(at, step), :] = other_ref[rows].astype(F32) * scale


def body(n_ctx, n_dp, positions, queries, latent, out_grad, attn_out, wuv):
    tok, heads, width = queries.shape[1:]
    lat = attn_out.shape[3]
    lines = n_ctx // GROUP
    line_bits = (lines - 1).bit_length()
    rows = heads * tok
    all_rows = GROUP * rows
    keys = lines * tok
    wide = -(-(width + EXTRA) // 128) * 128
    factor = (HEAD_DIM + ROPE) ** (-0.5)

    def swap(x, mask, axis="ctx", size=n_ctx):
        return lax.ppermute(x, axis, [(i, i ^ mask) for i in range(size)])

    def after(x, *done):
        return lax.optimization_barrier((x, done))[0]

    idx = lax.axis_index("ctx").reshape(1)
    step = lat // GROUP
    lat_msg, q_msg, delta, keep, send = call(
        pack_kernel,
        "pack",
        [
            ((width + EXTRA, tok), BF16),
            ((heads * (width + HEAD_DIM) + EXTRA, tok), BF16),
            ((8, tok), F32),
            ((2 * heads, step, HEAD_DIM), BF16),
            ((2 * heads, step, HEAD_DIM), BF16),
        ],
        [
            idx,
            positions,
            jnp.transpose(queries[0], (1, 2, 0)),
            out_grad[0],
            latent[0].T,
            attn_out[0],
            wuv,
        ],
        [
            ((1, tok), jnp.int32),
            (out_grad.shape[1:], BF16),
            (attn_out.shape[1:], BF16),
            (wuv.shape, BF16),
            ((heads, lat, HEAD_DIM), F32),
            ((EXTRA, tok), BF16),
            ((heads, HEAD_DIM, tok), BF16),
            ((8, tok), F32),
            ((2 * heads, step, HEAD_DIM), BF16),
            ((2 * heads, step, HEAD_DIM), BF16),
            ((width, tok), BF16),
            ((heads, width, tok), BF16),
        ],
        smem=(0,),
        hbm=(1, 2, 3, 4, 5, 6),
        copies=11 + 3 * heads,
        out=pltpu.HBM,
        limit=PACK_LIMIT,
    )

    def add(a, b):
        return (a.astype(F32) + b.astype(F32)).astype(BF16)

    dp_hops = [(1 << bit, "dp", n_dp) for bit in range((n_dp - 1).bit_length())]
    line_hops = [(GROUP << bit,) for bit in range(line_bits)]

    q_across = swap(q_msg, 2)
    q_core = swap(q_msg, 1)
    pair = add(keep, swap(send, 1))
    got_pair = swap(pair, *dp_hops[0])
    firsts = [swap(after(lat_msg, q_core) if bit + 1 < line_bits else lat_msg, GROUP << bit) for bit in range(line_bits)]
    own = call(
        hold_kernel,
        "hold_own",
        [(lat_msg.shape, BF16), (q_msg.shape, BF16), (delta.shape, F32)],
        [lat_msg, q_msg, delta],
        share=0,
    )
    q_core, q_across, firsts, got_pair, own = lax.optimization_barrier(
        (q_core, q_across, firsts, got_pair, own)
    )
    held = {0: lat_msg}
    for bit in reversed(range(line_bits)):
        held.update({m | 1 << bit: swap(x, GROUP << bit) for m, x in held.items() if m})
        held[1 << bit] = firsts[bit]
    pair = add(pair, got_pair)
    for step_hop in dp_hops[1:]:
        pair = add(pair, swap(pair, *step_hop))
    lats = [held[m] for m in range(lines)]
    q_far = swap(q_across, 1)
    got_across = swap(pair, 2)
    lat_own, q_own, delta = own
    lats[0] = lat_own
    qs = [q_own, q_core, q_across, q_far]

    most = lines - 1
    keys = most * tok
    score_flops = 2 * tok * all_rows * wide
    near_s, near_k, near_stat, q_all = call(
        functools.partial(score_kernel, factor, most, width, heads, False),
        "near_scores",
        [((keys, all_rows), F32), ((keys, wide), BF16), ((EXTRA, tok), F32), ((wide, all_rows), BF16)],
        lats[:most] + qs,
        [((wide, keys), BF16)],
        flops=most * score_flops,
        share=0,
    )
    mine = add(pair, after(got_across, near_stat))
    near = swap(mine, *line_hops[0])
    last_s, last_k, stat = call(
        functools.partial(score_kernel, factor, 1, width, heads, True),
        "last_scores",
        [((tok, all_rows), F32), ((tok, wide), BF16), ((EXTRA, tok), F32)],
        [lats[most], q_all, near_stat, delta],
        [((wide, tok), BF16)],
        flops=score_flops,
    )
    stats = [stat] + [swap(stat, k) for k in range(1, GROUP)]
    g, near_gp, last_gp = call(
        functools.partial(context_kernel, width, heads),
        "context",
        [((lat, all_rows), BF16), ((keys, all_rows), F32), ((tok, all_rows), F32)],
        qs + [wuv, near_k, last_k],
        flops=2 * lines * tok * all_rows * lat + 2 * all_rows * lat * HEAD_DIM,
        share=3,
    )
    mine = add(mine, after(near, stat))
    for step_hop in line_hops[1:-1]:
        mine = add(mine, swap(mine, *step_hop))
    near = swap(mine, *line_hops[-1])
    last_part, last_gs = call(
        functools.partial(last_kernel, factor, width, heads),
        "last_gradients",
        [((width, tok), BF16), ((tok, all_rows), BF16)],
        stats + [last_s, last_gp, g, q_all],
        [((tok, all_rows), BF16)],
        flops=2 * tok * all_rows * (width + lat),
    )
    last_got = swap(last_part, GROUP)
    mine = add(mine, near)
    gq_shape, cut_shape = (heads, width, tok), (width // CUTS, tok)
    gq_own, gq_core, gq_across, *far_cuts, near_gs, near_p = call(
        functools.partial(query_kernel, factor, lines, width, heads),
        "query_gradients",
        [(gq_shape, BF16)] * 3 + [(cut_shape, BF16)] * (CUTS * heads) + [((keys, all_rows), BF16)] * 2,
        stats + [near_s, near_gp, after(last_gs, mine)] + lats,
        [((width, lines * tok), BF16)],
        flops=2 * lines * tok * all_rows * width,
        share=0,
    )
    far_cuts = [swap(cut, 1) for cut in far_cuts]
    (gq_sum,) = call(join_kernel, "join", [(gq_shape, BF16)], [gq_across] + far_cuts)
    gq_core = swap(gq_core, 1)
    gq_last = swap(gq_sum, 2)
    near_parts = call(
        functools.partial(partial_kernel, factor, most, width),
        "near_gradients",
        [((width, tok), BF16)] * most,
        [g, q_all, near_gs, near_p],
        flops=2 * keys * all_rows * (width + lat),
        share=0,
    )
    parts = list(near_parts) + [last_part]
    kept = [parts[0]]
    for bit in range(line_bits):
        for m in range(3 << bit, lines, 2 << bit):
            got = last_got if m == most and bit == 0 else swap(parts[m], GROUP << bit)
            parts[m ^ 1 << bit] = add(parts[m ^ 1 << bit], got)
    other = swap(mine, 1)
    parts[1] = after(parts[1], gq_sum)
    kept += [swap(parts[1 << bit], GROUP << bit) for bit in reversed(range(line_bits))]
    scale = 1.0 / math.sqrt(tok * n_ctx * n_dp)
    (grad_w,) = call(
        functools.partial(spread_kernel, scale),
        "spread",
        [((heads, lat, HEAD_DIM), F32)],
        [idx, mine, other],
        smem=(0,),
    )
    gq_pieces = [gq_own, gq_core, gq_last]
    (grad_q,) = call(sum_kernel, "query_sum", [((heads, width, tok), BF16)], gq_pieces)
    kept[0] = after(kept[0], grad_q)
    (grad_lat,) = call(sum_kernel, "latent_sum", [((width, tok), BF16)], kept)
    return (jnp.transpose(grad_q, (2, 0, 1))[None], grad_lat.T[None], grad_w)


def solution(mesh):
    placed = (
        P("dp", "ctx"),
        P("dp", "ctx", None, None),
        P("dp", "ctx", None),
        P("dp", "ctx", None, None),
        P("dp", "ctx", None, None),
        P(),
    )
    return jax.shard_map(
        functools.partial(body, mesh.shape["ctx"], mesh.shape["dp"]),
        mesh=mesh,
        in_specs=placed,
        out_specs=(P("dp", "ctx", None, None), P("dp", "ctx", None), P()),
        check_vma=False,
    )
```

```python
import functools
import math

import jax
import jax.numpy as jnp
from jax import lax
from jax.experimental import pallas as pl
from jax.experimental.pallas import tpu as pltpu
from jax.sharding import PartitionSpec as P

ROPE = 64
HEAD_DIM = 128
GROUP = 4
EXTRA = 16
CUTS = 2
PACK_LIMIT = 63 << 20
F32 = jnp.float32
BF16 = jnp.bfloat16


def mm(a, b):
    return jnp.dot(a, b, preferred_element_type=F32)


def mm_t(a, b):
    return lax.dot_general(a, b, (((1,), (1,)), ((), ())), preferred_element_type=F32)


def size_of(shape, dtype):
    return math.prod(shape) * jnp.dtype(dtype).itemsize


def call(kernel, name, outs, args, scratch=(), flops=0, smem=(), hbm=(), copies=0, limit=None, share=1, out=pltpu.VMEM):
    def place(i):
        return pltpu.SMEM if i in smem else pltpu.HBM if i in hbm else pltpu.VMEM

    moved = sum(size_of(a.shape, a.dtype) for a in args) + sum(size_of(*o) for o in outs)
    held = moved + sum(size_of(*s) for s in scratch)
    semaphores = [pltpu.SemaphoreType.DMA((copies,))] if copies else []
    return pl.pallas_call(
        kernel,
        out_shape=[jax.ShapeDtypeStruct(s, d) for s, d in outs],
        in_specs=[pl.BlockSpec(memory_space=place(i)) for i in range(len(args))],
        out_specs=[pl.BlockSpec(memory_space=out) for _ in outs],
        scratch_shapes=[pltpu.VMEM(s, d) for s, d in scratch] + semaphores,
        compiler_params=pltpu.CompilerParams(vmem_limit_bytes=limit or int(1.2 * held) + (8 << 20)),
        cost_estimate=pl.CostEstimate(flops=flops * share, bytes_accessed=moved * share, transcendentals=0),
        name=name,
    )(*args)


def fetch(pairs, sems):
    copies = [pltpu.make_async_copy(src, dst, sems.at[i]) for i, (src, dst) in enumerate(pairs)]
    for copy in copies:
        copy.start()
    return copies


def pack_kernel(
    idx_ref, pos_hbm, q_hbm, og_hbm, lat_hbm, attn_hbm, wuv_hbm,
    lat_msg, q_msg, delta_hbm, keep_hbm, send_hbm,
    pos_ref, og_ref, attn_ref, wuv_ref, term, rows_ref, og_t_ref, delta_ref, keep_ref, send_ref,
    lat_ref, q_ref, sems,
):
    heads, width, tok = q_hbm.shape
    _, lat, _ = wuv_ref.shape
    started = []

    def send_off(src, dst):
        copy = pltpu.make_async_copy(src, dst, sems.at[len(started)])
        copy.start()
        started.append(copy)

    send_off(og_hbm, og_ref)
    send_off(pos_hbm, pos_ref)
    send_off(attn_hbm, attn_ref)
    send_off(wuv_hbm, wuv_ref)
    send_off(lat_hbm, lat_ref)
    for h in range(heads):
        send_off(q_hbm.at[h], q_ref.at[h])
    started[0].wait()
    for h in range(heads):
        og_t_ref[h] = og_ref[:, h, :].T
        send_off(og_t_ref.at[h], q_msg.at[pl.ds(heads * width + h * HEAD_DIM, HEAD_DIM), :])
    started[1].wait()
    pos = jnp.broadcast_to(pos_ref[...], (EXTRA, tok))
    row = lax.broadcasted_iota(jnp.int32, (EXTRA, tok), 0)
    high = lax.shift_right_logical(pos, 6)
    both = jnp.where(row == 0, high, jnp.where(row == 1, pos - high * 64, 0))
    rows_ref[...] = both.astype(F32).astype(BF16)
    send_off(rows_ref, lat_msg.at[pl.ds(width, EXTRA), :])
    send_off(rows_ref, q_msg.at[pl.ds(heads * (width + HEAD_DIM), EXTRA), :])
    started[4].wait()
    send_off(lat_ref, lat_msg.at[pl.ds(0, width), :])
    for h in range(heads):
        started[5 + h].wait()
        send_off(q_ref.at[h], q_msg.at[pl.ds(h * width, width), :])
    delta_ref[...] = jnp.zeros_like(delta_ref)
    started[2].wait()
    attn = [attn_ref[:, h, :].T for h in range(heads)]
    for h in range(heads):
        term[h] = mm_t(attn[h], og_t_ref[h])
    step = lat // GROUP
    side = lax.rem(idx_ref[0], 2)
    for i in range(GROUP // 2):
        rows = slice(i * heads, (i + 1) * heads)
        at = pl.multiple_of((2 * i + side) * step, step)
        keep_ref[rows] = term[:, pl.ds(at, step), :].astype(BF16)
        at = pl.multiple_of((2 * i + 1 - side) * step, step)
        send_ref[rows] = term[:, pl.ds(at, step), :].astype(BF16)
    send_off(send_ref, send_hbm)
    send_off(keep_ref, keep_hbm)
    started[3].wait()
    for h in range(heads):
        g = mm(wuv_ref[h], og_t_ref[h]).astype(BF16).astype(F32)
        delta_ref[h : h + 1, :] = jnp.sum(g * attn[h].astype(F32), axis=0, keepdims=True)
    send_off(delta_ref, delta_hbm)
    for copy in started[5 + heads :]:
        copy.wait()


def hold_kernel(*refs):
    half = len(refs) // 2
    for source, target in zip(refs[:half], refs[half:]):
        target[...] = source[...]


def score_kernel(factor, nkey, width, heads, last, *refs):
    lat_refs, refs = refs[:nkey], refs[nkey:]
    tok = lat_refs[0].shape[1]
    rows = heads * tok
    if last:
        q_all_ref, near_ref, delta_ref, s_ref, k_ref, stat_ref, kt = refs
    else:
        q_refs, refs = refs[:GROUP], refs[GROUP:]
        s_ref, k_ref, stat_ref, q_all_ref, kt = refs
        for j in range(GROUP):
            for h in range(heads):
                cols = slice(j * rows + h * tok, j * rows + (h + 1) * tok)
                q_all_ref[:width, cols] = q_refs[j][h * width : (h + 1) * width, :]
                q_all_ref[width : width + EXTRA, cols] = q_refs[j][q_refs[j].shape[0] - EXTRA :, :]
        spare = q_all_ref.shape[0] - width - EXTRA
        q_all_ref[width + EXTRA :, :] = jnp.zeros((spare, GROUP * rows), BF16)
    wide = kt.shape[0]
    for a in range(nkey):
        kt[: width + EXTRA, a * tok : (a + 1) * tok] = lat_refs[a][...]
    kt[width + EXTRA :, :] = jnp.zeros((wide - width - EXTRA, nkey * tok), BF16)
    keys = kt[...].T
    pos = keys[:, wide - 128 :].astype(F32)
    at = width - (wide - 128)
    key_pos = pos[:, at : at + 1] * 64.0 + pos[:, at + 1 : at + 2]
    lane = lax.broadcasted_iota(jnp.int32, keys.shape, 1)
    k_ref[...] = jnp.where(lane < width, keys, jnp.zeros_like(keys))
    stat_ref[...] = jnp.zeros_like(stat_ref)
    if last:
        stat_ref[GROUP * heads : GROUP * heads + heads, :] = delta_ref[:heads, :]
    for j in range(GROUP):
        cols = slice(j * rows, (j + 1) * rows)
        qp = q_all_ref[width : width + EXTRA, cols].astype(F32)
        row_pos = qp[0:1, :] * 64.0 + qp[1:2, :]
        s = mm(k_ref[...], q_all_ref[:, cols]) * factor
        s = jnp.where(key_pos <= row_pos, s, -1e30)
        s_ref[:, cols] = s
        top = jnp.max(s, axis=0, keepdims=True)
        lse = top + jnp.log(jnp.sum(jnp.exp(s - top), axis=0, keepdims=True))
        for h in range(heads):
            at = j * heads + h
            part = lse[:, h * tok : (h + 1) * tok]
            if last:
                near = near_ref[at : at + 1, :]
                most = jnp.maximum(part, near)
                part = most + jnp.log(jnp.exp(part - most) + jnp.exp(near - most))
            stat_ref[at : at + 1, :] = part


def context_kernel(width, heads, *refs):
    q_refs = refs[:GROUP]
    wuv_ref, near_k_ref, last_k_ref, g_ref, near_gp_ref, last_gp_ref = refs[GROUP:]
    lat, all_rows = g_ref.shape
    tok = q_refs[0].shape[1]
    rows = heads * tok
    for j in range(GROUP):
        for h in range(heads):
            at = heads * width + h * HEAD_DIM
            og = q_refs[j][at : at + HEAD_DIM, :]
            col = j * rows + h * tok
            g_ref[:, col : col + tok] = mm(wuv_ref[h], og).astype(BF16)
        cols = slice(j * rows, (j + 1) * rows)
        near_gp_ref[:, cols] = mm(near_k_ref[:, :lat], g_ref[:, cols])
        last_gp_ref[:, cols] = mm(last_k_ref[:, :lat], g_ref[:, cols])


def pair_kernel(heads, *refs):
    stats, (s_ref, gp_ref, gs_ref, p_ref) = refs[:GROUP], refs[GROUP : GROUP + 4]
    all_rows = s_ref.shape[1]
    rows = all_rows // GROUP
    for j in range(GROUP):
        cols = slice(j * rows, (j + 1) * rows)
        lse_parts = []
        for k in range(GROUP):
            at = (j ^ k) * heads
            lse_parts.append(
                jnp.concatenate([stats[k][at + h : at + h + 1, :] for h in range(heads)], axis=1)
            )
        top = functools.reduce(jnp.maximum, lse_parts)
        lse = top + jnp.log(sum(jnp.exp(part - top) for part in lse_parts))
        at = GROUP * heads
        delta = jnp.concatenate([stats[j][at + h : at + h + 1, :] for h in range(heads)], axis=1)
        p = jnp.exp(s_ref[:, cols] - lse)
        gs_ref[:, cols] = (p * (gp_ref[:, cols] - delta)).astype(BF16)
        p_ref[:, cols] = p.astype(BF16)


def partial_kernel(factor, places, width, g_ref, q_all_ref, gs_ref, p_ref, *part_refs):
    lat = g_ref.shape[0]
    for a, at in enumerate(places):
        along = mm_t(q_all_ref[:width, :], gs_ref[at, :]) * factor
        value = mm_t(g_ref[...], p_ref[at, :])
        part_refs[a][:lat, :] = (along[:lat] + value).astype(BF16)
        part_refs[a][lat:, :] = along[lat:].astype(BF16)


def last_kernel(factor, width, heads, *refs):
    stats, refs = refs[:GROUP], refs[GROUP:]
    s_ref, gp_ref, g_ref, q_all_ref, part_ref, gs_ref, p_ref = refs
    pair_kernel(heads, *stats, s_ref, gp_ref, gs_ref, p_ref)
    partial_kernel(factor, [slice(None)], width, g_ref, q_all_ref, gs_ref, p_ref, part_ref)


def query_kernel(factor, nkey, width, heads, *refs):
    stats, refs = refs[:GROUP], refs[GROUP:]
    (s_ref, gp_ref, last_gs_ref), refs = refs[:3], refs[3:]
    lat_refs, refs = refs[:nkey], refs[nkey:]
    gq_refs, far_refs, (gs_ref, p_ref, kt) = refs[: GROUP - 1], refs[GROUP - 1 : -3], refs[-3:]
    cut = far_refs[0].shape[0]
    cuts = width // cut
    tok = lat_refs[0].shape[1]
    keys = s_ref.shape[0]
    rows = heads * tok
    for a in range(nkey):
        kt[:, a * tok : (a + 1) * tok] = lat_refs[a][:width, :]
    pair_kernel(heads, *stats, s_ref, gp_ref, gs_ref, p_ref)
    for j in range(GROUP):
        cols = slice(j * rows, (j + 1) * rows)
        gq = mm(kt[:, :keys], gs_ref[:, cols]) + mm(kt[:, keys:], last_gs_ref[:, cols])
        gq = (gq * factor).astype(BF16)
        for h in range(heads):
            part = gq[:, h * tok : (h + 1) * tok]
            if j < GROUP - 1:
                gq_refs[j][h] = part
            else:
                for c in range(cuts):
                    far_refs[h * cuts + c][...] = part[c * cut : (c + 1) * cut]


def join_kernel(whole_ref, *refs):
    pieces, out_ref = refs[:-1], refs[-1]
    cut = pieces[0].shape[0]
    cuts = whole_ref.shape[1] // cut
    for i, piece in enumerate(pieces):
        at = (i // cuts, slice(i % cuts * cut, (i % cuts + 1) * cut))
        out_ref[at] = (whole_ref[at].astype(F32) + piece[...].astype(F32)).astype(BF16)


def sum_kernel(*refs):
    refs[-1][...] = sum(ref[...].astype(F32) for ref in refs[:-1]).astype(BF16)


def spread_kernel(scale, idx_ref, mine_ref, other_ref, out_ref):
    heads, lat, _ = out_ref.shape
    step = lat // GROUP
    side = lax.rem(idx_ref[0], 2)
    for i in range(GROUP // 2):
        rows = slice(i * heads, (i + 1) * heads)
        at = pl.multiple_of((2 * i + side) * step, step)
        out_ref[:, pl.ds(at, step), :] = mine_ref[rows].astype(F32) * scale
        at = pl.multiple_of((2 * i + 1 - side) * step, step)
        out_ref[:, pl.ds(at, step), :] = other_ref[rows].astype(F32) * scale


def body(n_ctx, n_dp, positions, queries, latent, out_grad, attn_out, wuv):
    tok, heads, width = queries.shape[1:]
    lat = attn_out.shape[3]
    lines = n_ctx // GROUP
    line_bits = (lines - 1).bit_length()
    rows = heads * tok
    all_rows = GROUP * rows
    keys = lines * tok
    wide = -(-(width + EXTRA) // 128) * 128
    factor = (HEAD_DIM + ROPE) ** (-0.5)

    def swap(x, mask, axis="ctx", size=n_ctx):
        return lax.ppermute(x, axis, [(i, i ^ mask) for i in range(size)])

    def after(x, *done):
        return lax.optimization_barrier((x, done))[0]

    idx = lax.axis_index("ctx").reshape(1)
    step = lat // GROUP
    lat_msg, q_msg, delta, keep, send = call(
        pack_kernel,
        "pack",
        [
            ((width + EXTRA, tok), BF16),
            ((heads * (width + HEAD_DIM) + EXTRA, tok), BF16),
            ((8, tok), F32),
            ((2 * heads, step, HEAD_DIM), BF16),
            ((2 * heads, step, HEAD_DIM), BF16),
        ],
        [
            idx,
            positions,
            jnp.transpose(queries[0], (1, 2, 0)),
            out_grad[0],
            latent[0].T,
            attn_out[0],
            wuv,
        ],
        [
            ((1, tok), jnp.int32),
            (out_grad.shape[1:], BF16),
            (attn_out.shape[1:], BF16),
            (wuv.shape, BF16),
            ((heads, lat, HEAD_DIM), F32),
            ((EXTRA, tok), BF16),
            ((heads, HEAD_DIM, tok), BF16),
            ((8, tok), F32),
            ((2 * heads, step, HEAD_DIM), BF16),
            ((2 * heads, step, HEAD_DIM), BF16),
            ((width, tok), BF16),
            ((heads, width, tok), BF16),
        ],
        smem=(0,),
        hbm=(1, 2, 3, 4, 5, 6),
        copies=11 + 3 * heads,
        out=pltpu.HBM,
        limit=PACK_LIMIT,
    )

    def add(a, b):
        return (a.astype(F32) + b.astype(F32)).astype(BF16)

    dp_hops = [(1 << bit, "dp", n_dp) for bit in range((n_dp - 1).bit_length())]
    line_hops = [(GROUP << bit,) for bit in range(line_bits)]

    q_across = swap(q_msg, 2)
    q_core = swap(q_msg, 1)
    pair = add(keep, swap(send, 1))
    got_pair = swap(pair, *dp_hops[0])
    firsts = [swap(after(lat_msg, q_core) if bit + 1 < line_bits else lat_msg, GROUP << bit) for bit in range(line_bits)]
    own = call(
        hold_kernel,
        "hold_own",
        [(lat_msg.shape, BF16), (q_msg.shape, BF16), (delta.shape, F32)],
        [lat_msg, q_msg, delta],
        share=0,
    )
    q_core, q_across, firsts, got_pair, own = lax.optimization_barrier(
        (q_core, q_across, firsts, got_pair, own)
    )
    held = {0: lat_msg}
    for bit in reversed(range(line_bits)):
        held.update({m | 1 << bit: swap(x, GROUP << bit) for m, x in held.items() if m})
        held[1 << bit] = firsts[bit]
    pair = add(pair, got_pair)
    for step_hop in dp_hops[1:]:
        pair = add(pair, swap(pair, *step_hop))
    lats = [held[m] for m in range(lines)]
    q_far = swap(q_across, 1)
    got_across = swap(pair, 2)
    lat_own, q_own, delta = own
    lats[0] = lat_own
    qs = [q_own, q_core, q_across, q_far]

    most = lines - 1
    keys = most * tok
    score_flops = 2 * tok * all_rows * wide
    near_s, near_k, near_stat, q_all = call(
        functools.partial(score_kernel, factor, most, width, heads, False),
        "near_scores",
        [((keys, all_rows), F32), ((keys, wide), BF16), ((EXTRA, tok), F32), ((wide, all_rows), BF16)],
        lats[:most] + qs,
        [((wide, keys), BF16)],
        flops=most * score_flops,
        share=0,
    )
    mine = add(pair, after(got_across, near_stat))
    near = swap(mine, *line_hops[0])
    last_s, last_k, stat = call(
        functools.partial(score_kernel, factor, 1, width, heads, True),
        "last_scores",
        [((tok, all_rows), F32), ((tok, wide), BF16), ((EXTRA, tok), F32)],
        [lats[most], q_all, near_stat, delta],
        [((wide, tok), BF16)],
        flops=score_flops,
    )
    stats = [stat] + [swap(stat, k) for k in range(1, GROUP)]
    g, near_gp, last_gp = call(
        functools.partial(context_kernel, width, heads),
        "context",
        [((lat, all_rows), BF16), ((keys, all_rows), F32), ((tok, all_rows), F32)],
        qs + [wuv, near_k, last_k],
        flops=2 * lines * tok * all_rows * lat + 2 * all_rows * lat * HEAD_DIM,
        share=3,
    )
    mine = add(mine, after(near, stat))
    for step_hop in line_hops[1:-1]:
        mine = add(mine, swap(mine, *step_hop))
    near = swap(mine, *line_hops[-1])
    last_part, last_gs = call(
        functools.partial(last_kernel, factor, width, heads),
        "last_gradients",
        [((width, tok), BF16), ((tok, all_rows), BF16)],
        stats + [last_s, last_gp, g, q_all],
        [((tok, all_rows), BF16)],
        flops=2 * tok * all_rows * (width + lat),
    )
    last_got = swap(last_part, GROUP)
    mine = add(mine, near)
    gq_shape, cut_shape = (heads, width, tok), (width // CUTS, tok)
    gq_own, gq_core, gq_across, *far_cuts, near_gs, near_p = call(
        functools.partial(query_kernel, factor, lines, width, heads),
        "query_gradients",
        [(gq_shape, BF16)] * 3 + [(cut_shape, BF16)] * (CUTS * heads) + [((keys, all_rows), BF16)] * 2,
        stats + [near_s, near_gp, after(last_gs, mine)] + lats,
        [((width, lines * tok), BF16)],
        flops=2 * lines * tok * all_rows * width,
        share=0,
    )
    far_cuts = [swap(cut, 1) for cut in far_cuts]
    (gq_sum,) = call(join_kernel, "join", [(gq_shape, BF16)], [gq_across] + far_cuts)
    gq_core = swap(gq_core, 1)
    gq_last = swap(gq_sum, 2)
    def partials(name, blocks, gs, p):
        rows = [slice(m * tok, (m + 1) * tok) for m in blocks]
        made = call(
            functools.partial(partial_kernel, factor, rows, width),
            name,
            [((width, tok), BF16)] * len(blocks),
            [g, q_all, gs, p],
            flops=2 * len(blocks) * tok * all_rows * (width + lat),
        )
        return dict(zip(blocks, made))

    middle = lines // 2
    made = partials("middle_gradients", [middle], near_gs, near_p)
    made.update(partials("near_gradients", [m for m in range(most) if m != middle], near_gs, near_p))
    near_parts = [made[m] for m in range(most)]
    parts = list(near_parts) + [last_part]
    kept = [parts[0]]
    for bit in range(line_bits):
        for m in range(3 << bit, lines, 2 << bit):
            got = last_got if m == most and bit == 0 else swap(parts[m], GROUP << bit)
            parts[m ^ 1 << bit] = add(parts[m ^ 1 << bit], got)
    other = swap(mine, 1)
    parts[1] = after(parts[1], gq_sum)
    kept += [swap(parts[1 << bit], GROUP << bit) for bit in reversed(range(line_bits))]
    scale = 1.0 / math.sqrt(tok * n_ctx * n_dp)
    (grad_w,) = call(
        functools.partial(spread_kernel, scale),
        "spread",
        [((heads, lat, HEAD_DIM), F32)],
        [idx, mine, other],
        smem=(0,),
    )
    gq_pieces = [gq_own, gq_core, gq_last]
    (grad_q,) = call(sum_kernel, "query_sum", [((heads, width, tok), BF16)], gq_pieces)
    kept[0] = after(kept[0], grad_q)
    (grad_lat,) = call(sum_kernel, "latent_sum", [((width, tok), BF16)], kept)
    return (jnp.transpose(grad_q, (2, 0, 1))[None], grad_lat.T[None], grad_w)


def solution(mesh):
    placed = (
        P("dp", "ctx"),
        P("dp", "ctx", None, None),
        P("dp", "ctx", None),
        P("dp", "ctx", None, None),
        P("dp", "ctx", None, None),
        P(),
    )
    return jax.shard_map(
        functools.partial(body, mesh.shape["ctx"], mesh.shape["dp"]),
        mesh=mesh,
        in_specs=placed,
        out_specs=(P("dp", "ctx", None, None), P("dp", "ctx", None), P()),
        check_vma=False,
    )
```

```python
import functools
import math

import jax
import jax.numpy as jnp
from jax import lax
from jax.experimental import pallas as pl
from jax.experimental.pallas import tpu as pltpu
from jax.sharding import PartitionSpec as P

ROPE = 64
HEAD_DIM = 128
GROUP = 4
EXTRA = 16
CUTS = 2
PACK_LIMIT = 63 << 20
F32 = jnp.float32
BF16 = jnp.bfloat16


def mm(a, b):
    return jnp.dot(a, b, preferred_element_type=F32)


def mm_t(a, b):
    return lax.dot_general(a, b, (((1,), (1,)), ((), ())), preferred_element_type=F32)


def size_of(shape, dtype):
    return math.prod(shape) * jnp.dtype(dtype).itemsize


def call(kernel, name, outs, args, scratch=(), flops=0, smem=(), hbm=(), copies=0, limit=None, share=1, out=pltpu.VMEM):
    def place(i):
        return pltpu.SMEM if i in smem else pltpu.HBM if i in hbm else pltpu.VMEM

    moved = sum(size_of(a.shape, a.dtype) for a in args) + sum(size_of(*o) for o in outs)
    held = moved + sum(size_of(*s) for s in scratch)
    semaphores = [pltpu.SemaphoreType.DMA((copies,))] if copies else []
    return pl.pallas_call(
        kernel,
        out_shape=[jax.ShapeDtypeStruct(s, d) for s, d in outs],
        in_specs=[pl.BlockSpec(memory_space=place(i)) for i in range(len(args))],
        out_specs=[pl.BlockSpec(memory_space=out) for _ in outs],
        scratch_shapes=[pltpu.VMEM(s, d) for s, d in scratch] + semaphores,
        compiler_params=pltpu.CompilerParams(vmem_limit_bytes=limit or int(1.2 * held) + (8 << 20)),
        cost_estimate=pl.CostEstimate(flops=flops * share, bytes_accessed=moved * share, transcendentals=0),
        name=name,
    )(*args)


def fetch(pairs, sems):
    copies = [pltpu.make_async_copy(src, dst, sems.at[i]) for i, (src, dst) in enumerate(pairs)]
    for copy in copies:
        copy.start()
    return copies


def pack_kernel(
    idx_ref, pos_hbm, q_hbm, og_hbm, lat_hbm, attn_hbm, wuv_hbm,
    lat_msg, q_msg, delta_hbm, keep_hbm, send_hbm,
    pos_ref, og_ref, attn_ref, wuv_ref, term, rows_ref, og_t_ref, delta_ref, keep_ref, send_ref,
    lat_ref, q_ref, sems,
):
    heads, width, tok = q_hbm.shape
    _, lat, _ = wuv_ref.shape
    started = []

    def send_off(src, dst):
        copy = pltpu.make_async_copy(src, dst, sems.at[len(started)])
        copy.start()
        started.append(copy)

    send_off(og_hbm, og_ref)
    send_off(pos_hbm, pos_ref)
    send_off(attn_hbm, attn_ref)
    send_off(wuv_hbm, wuv_ref)
    send_off(lat_hbm, lat_ref)
    for h in range(heads):
        send_off(q_hbm.at[h], q_ref.at[h])
    started[0].wait()
    for h in range(heads):
        og_t_ref[h] = og_ref[:, h, :].T
        send_off(og_t_ref.at[h], q_msg.at[pl.ds(heads * width + h * HEAD_DIM, HEAD_DIM), :])
    started[1].wait()
    pos = jnp.broadcast_to(pos_ref[...], (EXTRA, tok))
    row = lax.broadcasted_iota(jnp.int32, (EXTRA, tok), 0)
    high = lax.shift_right_logical(pos, 6)
    both = jnp.where(row == 0, high, jnp.where(row == 1, pos - high * 64, 0))
    rows_ref[...] = both.astype(F32).astype(BF16)
    send_off(rows_ref, lat_msg.at[pl.ds(width, EXTRA), :])
    send_off(rows_ref, q_msg.at[pl.ds(heads * (width + HEAD_DIM), EXTRA), :])
    started[4].wait()
    send_off(lat_ref, lat_msg.at[pl.ds(0, width), :])
    for h in range(heads):
        started[5 + h].wait()
        send_off(q_ref.at[h], q_msg.at[pl.ds(h * width, width), :])
    delta_ref[...] = jnp.zeros_like(delta_ref)
    started[2].wait()
    attn = [attn_ref[:, h, :].T for h in range(heads)]
    for h in range(heads):
        term[h] = mm_t(attn[h], og_t_ref[h])
    step = lat // GROUP
    me = lax.rem(idx_ref[0], GROUP)
    for k in range(GROUP):
        at = pl.multiple_of(jnp.bitwise_xor(me, k) * step, step)
        target = send_ref if k % 2 else keep_ref
        target[k // 2 * heads : (k // 2 + 1) * heads] = term[:, pl.ds(at, step), :].astype(BF16)
    send_off(send_ref, send_hbm)
    send_off(keep_ref, keep_hbm)
    started[3].wait()
    for h in range(heads):
        g = mm(wuv_ref[h], og_t_ref[h]).astype(BF16).astype(F32)
        delta_ref[h : h + 1, :] = jnp.sum(g * attn[h].astype(F32), axis=0, keepdims=True)
    send_off(delta_ref, delta_hbm)
    for copy in started[5 + heads :]:
        copy.wait()


def hold_kernel(*refs):
    half = len(refs) // 2
    for source, target in zip(refs[:half], refs[half:]):
        target[...] = source[...]


def score_kernel(factor, nkey, width, heads, last, *refs):
    lat_refs, refs = refs[:nkey], refs[nkey:]
    tok = lat_refs[0].shape[1]
    rows = heads * tok
    if last:
        q_all_ref, near_ref, delta_ref, s_ref, k_ref, stat_ref, kt = refs
    else:
        q_refs, refs = refs[:GROUP], refs[GROUP:]
        s_ref, k_ref, stat_ref, q_all_ref, kt = refs
        for j in range(GROUP):
            for h in range(heads):
                cols = slice(j * rows + h * tok, j * rows + (h + 1) * tok)
                q_all_ref[:width, cols] = q_refs[j][h * width : (h + 1) * width, :]
                q_all_ref[width : width + EXTRA, cols] = q_refs[j][q_refs[j].shape[0] - EXTRA :, :]
        spare = q_all_ref.shape[0] - width - EXTRA
        q_all_ref[width + EXTRA :, :] = jnp.zeros((spare, GROUP * rows), BF16)
    wide = kt.shape[0]
    for a in range(nkey):
        kt[: width + EXTRA, a * tok : (a + 1) * tok] = lat_refs[a][...]
    kt[width + EXTRA :, :] = jnp.zeros((wide - width - EXTRA, nkey * tok), BF16)
    keys = kt[...].T
    pos = keys[:, wide - 128 :].astype(F32)
    at = width - (wide - 128)
    key_pos = pos[:, at : at + 1] * 64.0 + pos[:, at + 1 : at + 2]
    lane = lax.broadcasted_iota(jnp.int32, keys.shape, 1)
    k_ref[...] = jnp.where(lane < width, keys, jnp.zeros_like(keys))
    stat_ref[...] = jnp.zeros_like(stat_ref)
    if last:
        stat_ref[GROUP * heads : GROUP * heads + heads, :] = delta_ref[:heads, :]
    for j in range(GROUP):
        cols = slice(j * rows, (j + 1) * rows)
        qp = q_all_ref[width : width + EXTRA, cols].astype(F32)
        row_pos = qp[0:1, :] * 64.0 + qp[1:2, :]
        s = mm(k_ref[...], q_all_ref[:, cols]) * factor
        s = jnp.where(key_pos <= row_pos, s, -1e30)
        s_ref[:, cols] = s
        top = jnp.max(s, axis=0, keepdims=True)
        lse = top + jnp.log(jnp.sum(jnp.exp(s - top), axis=0, keepdims=True))
        for h in range(heads):
            at = j * heads + h
            part = lse[:, h * tok : (h + 1) * tok]
            if last:
                near = near_ref[at : at + 1, :]
                most = jnp.maximum(part, near)
                part = most + jnp.log(jnp.exp(part - most) + jnp.exp(near - most))
            stat_ref[at : at + 1, :] = part


def context_kernel(width, heads, *refs):
    q_refs = refs[:GROUP]
    wuv_ref, near_k_ref, last_k_ref, g_ref, near_gp_ref, last_gp_ref = refs[GROUP:]
    lat, all_rows = g_ref.shape
    tok = q_refs[0].shape[1]
    rows = heads * tok
    for j in range(GROUP):
        for h in range(heads):
            at = heads * width + h * HEAD_DIM
            og = q_refs[j][at : at + HEAD_DIM, :]
            col = j * rows + h * tok
            g_ref[:, col : col + tok] = mm(wuv_ref[h], og).astype(BF16)
        cols = slice(j * rows, (j + 1) * rows)
        near_gp_ref[:, cols] = mm(near_k_ref[:, :lat], g_ref[:, cols])
        last_gp_ref[:, cols] = mm(last_k_ref[:, :lat], g_ref[:, cols])


def pair_kernel(heads, *refs):
    stats, (s_ref, gp_ref, gs_ref, p_ref) = refs[:GROUP], refs[GROUP : GROUP + 4]
    all_rows = s_ref.shape[1]
    rows = all_rows // GROUP
    for j in range(GROUP):
        cols = slice(j * rows, (j + 1) * rows)
        lse_parts = []
        for k in range(GROUP):
            at = (j ^ k) * heads
            lse_parts.append(
                jnp.concatenate([stats[k][at + h : at + h + 1, :] for h in range(heads)], axis=1)
            )
        top = functools.reduce(jnp.maximum, lse_parts)
        lse = top + jnp.log(sum(jnp.exp(part - top) for part in lse_parts))
        at = GROUP * heads
        delta = jnp.concatenate([stats[j][at + h : at + h + 1, :] for h in range(heads)], axis=1)
        p = jnp.exp(s_ref[:, cols] - lse)
        gs_ref[:, cols] = (p * (gp_ref[:, cols] - delta)).astype(BF16)
        p_ref[:, cols] = p.astype(BF16)


def partial_kernel(factor, places, width, g_ref, q_all_ref, gs_ref, p_ref, *part_refs):
    lat = g_ref.shape[0]
    for a, at in enumerate(places):
        along = mm_t(q_all_ref[:width, :], gs_ref[at, :]) * factor
        value = mm_t(g_ref[...], p_ref[at, :])
        part_refs[a][:lat, :] = (along[:lat] + value).astype(BF16)
        part_refs[a][lat:, :] = along[lat:].astype(BF16)


def last_kernel(factor, width, heads, *refs):
    stats, refs = refs[:GROUP], refs[GROUP:]
    s_ref, gp_ref, g_ref, q_all_ref, part_ref, gs_ref, p_ref = refs
    pair_kernel(heads, *stats, s_ref, gp_ref, gs_ref, p_ref)
    partial_kernel(factor, [slice(None)], width, g_ref, q_all_ref, gs_ref, p_ref, part_ref)


def query_kernel(factor, nkey, width, heads, *refs):
    stats, refs = refs[:GROUP], refs[GROUP:]
    (s_ref, gp_ref, last_gs_ref), refs = refs[:3], refs[3:]
    lat_refs, refs = refs[:nkey], refs[nkey:]
    gq_refs, far_refs, (gs_ref, p_ref, kt) = refs[: GROUP - 1], refs[GROUP - 1 : -3], refs[-3:]
    cut = far_refs[0].shape[0]
    cuts = width // cut
    tok = lat_refs[0].shape[1]
    keys = s_ref.shape[0]
    rows = heads * tok
    for a in range(nkey):
        kt[:, a * tok : (a + 1) * tok] = lat_refs[a][:width, :]
    pair_kernel(heads, *stats, s_ref, gp_ref, gs_ref, p_ref)
    for j in range(GROUP):
        cols = slice(j * rows, (j + 1) * rows)
        gq = mm(kt[:, :keys], gs_ref[:, cols]) + mm(kt[:, keys:], last_gs_ref[:, cols])
        gq = (gq * factor).astype(BF16)
        for h in range(heads):
            part = gq[:, h * tok : (h + 1) * tok]
            if j < GROUP - 1:
                gq_refs[j][h] = part
            else:
                for c in range(cuts):
                    far_refs[h * cuts + c][...] = part[c * cut : (c + 1) * cut]


def join_kernel(whole_ref, *refs):
    pieces, out_ref = refs[:-1], refs[-1]
    cut = pieces[0].shape[0]
    cuts = whole_ref.shape[1] // cut
    for i, piece in enumerate(pieces):
        at = (i // cuts, slice(i % cuts * cut, (i % cuts + 1) * cut))
        out_ref[at] = (whole_ref[at].astype(F32) + piece[...].astype(F32)).astype(BF16)


def sum_kernel(*refs):
    refs[-1][...] = sum(ref[...].astype(F32) for ref in refs[:-1]).astype(BF16)


def spread_kernel(scale, idx_ref, *refs):
    chunks, out_ref = refs[:GROUP], refs[GROUP]
    step = chunks[0].shape[1]
    me = lax.rem(idx_ref[0], GROUP)
    for k in range(GROUP):
        at = pl.multiple_of(jnp.bitwise_xor(me, k) * step, step)
        out_ref[:, pl.ds(at, step), :] = chunks[k][...].astype(F32) * scale


def body(n_ctx, n_dp, positions, queries, latent, out_grad, attn_out, wuv):
    tok, heads, width = queries.shape[1:]
    lat = attn_out.shape[3]
    lines = n_ctx // GROUP
    line_bits = (lines - 1).bit_length()
    rows = heads * tok
    all_rows = GROUP * rows
    keys = lines * tok
    wide = -(-(width + EXTRA) // 128) * 128
    factor = (HEAD_DIM + ROPE) ** (-0.5)

    def swap(x, mask, axis="ctx", size=n_ctx):
        return lax.ppermute(x, axis, [(i, i ^ mask) for i in range(size)])

    def after(x, *done):
        return lax.optimization_barrier((x, done))[0]

    idx = lax.axis_index("ctx").reshape(1)
    step = lat // GROUP
    lat_msg, q_msg, delta, keep, send = call(
        pack_kernel,
        "pack",
        [
            ((width + EXTRA, tok), BF16),
            ((heads * (width + HEAD_DIM) + EXTRA, tok), BF16),
            ((8, tok), F32),
            ((2 * heads, step, HEAD_DIM), BF16),
            ((2 * heads, step, HEAD_DIM), BF16),
        ],
        [
            idx,
            positions,
            jnp.transpose(queries[0], (1, 2, 0)),
            out_grad[0],
            latent[0].T,
            attn_out[0],
            wuv,
        ],
        [
            ((1, tok), jnp.int32),
            (out_grad.shape[1:], BF16),
            (attn_out.shape[1:], BF16),
            (wuv.shape, BF16),
            ((heads, lat, HEAD_DIM), F32),
            ((EXTRA, tok), BF16),
            ((heads, HEAD_DIM, tok), BF16),
            ((8, tok), F32),
            ((2 * heads, step, HEAD_DIM), BF16),
            ((2 * heads, step, HEAD_DIM), BF16),
            ((width, tok), BF16),
            ((heads, width, tok), BF16),
        ],
        smem=(0,),
        hbm=(1, 2, 3, 4, 5, 6),
        copies=11 + 3 * heads,
        out=pltpu.HBM,
        limit=PACK_LIMIT,
    )

    def add(a, b):
        return (a.astype(F32) + b.astype(F32)).astype(BF16)

    dp_hops = [(1 << bit, "dp", n_dp) for bit in range((n_dp - 1).bit_length())]
    line_hops = [(GROUP << bit,) for bit in range(line_bits)]

    q_across = swap(q_msg, 2)
    q_core = swap(q_msg, 1)
    pair = add(keep, swap(send, 1))
    got_pair = swap(pair, *dp_hops[0])
    firsts = [swap(after(lat_msg, q_core) if bit + 1 < line_bits else lat_msg, GROUP << bit) for bit in range(line_bits)]
    own = call(
        hold_kernel,
        "hold_own",
        [(lat_msg.shape, BF16), (q_msg.shape, BF16), (delta.shape, F32)],
        [lat_msg, q_msg, delta],
        share=0,
    )
    q_core, q_across, firsts, got_pair, own = lax.optimization_barrier(
        (q_core, q_across, firsts, got_pair, own)
    )
    held = {0: lat_msg}
    for bit in reversed(range(line_bits)):
        held.update({m | 1 << bit: swap(x, GROUP << bit) for m, x in held.items() if m})
        held[1 << bit] = firsts[bit]
    pair = add(pair, got_pair)
    for step_hop in dp_hops[1:]:
        pair = add(pair, swap(pair, *step_hop))
    lats = [held[m] for m in range(lines)]
    q_far = swap(q_across, 1)
    got_own = swap(pair[heads:], 2)
    lat_own, q_own, delta = own
    lats[0] = lat_own
    qs = [q_own, q_core, q_across, q_far]

    most = lines - 1
    keys = most * tok
    score_flops = 2 * tok * all_rows * wide
    near_s, near_k, near_stat, q_all = call(
        functools.partial(score_kernel, factor, most, width, heads, False),
        "near_scores",
        [((keys, all_rows), F32), ((keys, wide), BF16), ((EXTRA, tok), F32), ((wide, all_rows), BF16)],
        lats[:most] + qs,
        [((wide, keys), BF16)],
        flops=most * score_flops,
        share=0,
    )
    mine = add(pair[:heads], after(got_own, near_stat))
    near = swap(mine, *line_hops[0])
    last_s, last_k, stat = call(
        functools.partial(score_kernel, factor, 1, width, heads, True),
        "last_scores",
        [((tok, all_rows), F32), ((tok, wide), BF16), ((EXTRA, tok), F32)],
        [lats[most], q_all, near_stat, delta],
        [((wide, tok), BF16)],
        flops=score_flops,
    )
    stats = [stat] + [swap(stat, k) for k in range(1, GROUP)]
    g, near_gp, last_gp = call(
        functools.partial(context_kernel, width, heads),
        "context",
        [((lat, all_rows), BF16), ((keys, all_rows), F32), ((tok, all_rows), F32)],
        qs + [wuv, near_k, last_k],
        flops=2 * lines * tok * all_rows * lat + 2 * all_rows * lat * HEAD_DIM,
        share=3,
    )
    mine = add(mine, after(near, stat))
    for step_hop in line_hops[1:-1]:
        mine = add(mine, swap(mine, *step_hop))
    near = swap(mine, *line_hops[-1])
    last_part, last_gs = call(
        functools.partial(last_kernel, factor, width, heads),
        "last_gradients",
        [((width, tok), BF16), ((tok, all_rows), BF16)],
        stats + [last_s, last_gp, g, q_all],
        [((tok, all_rows), BF16)],
        flops=2 * tok * all_rows * (width + lat),
    )
    last_got = swap(last_part, GROUP)
    mine = add(mine, near)
    gq_shape, cut_shape = (heads, width, tok), (width // CUTS, tok)
    gq_own, gq_core, gq_across, *far_cuts, near_gs, near_p = call(
        functools.partial(query_kernel, factor, lines, width, heads),
        "query_gradients",
        [(gq_shape, BF16)] * 3 + [(cut_shape, BF16)] * (CUTS * heads) + [((keys, all_rows), BF16)] * 2,
        stats + [near_s, near_gp, after(last_gs, mine)] + lats,
        [((width, lines * tok), BF16)],
        flops=2 * lines * tok * all_rows * width,
        share=0,
    )
    across = swap(mine, 2)
    far_cuts = [swap(cut, 1) for cut in far_cuts]
    (gq_sum,) = call(join_kernel, "join", [(gq_shape, BF16)], [after(gq_across, across)] + far_cuts)
    gq_core = swap(gq_core, 1)
    gq_last = swap(gq_sum, 2)
    def partials(name, blocks, gs, p):
        rows = [slice(m * tok, (m + 1) * tok) for m in blocks]
        made = call(
            functools.partial(partial_kernel, factor, rows, width),
            name,
            [((width, tok), BF16)] * len(blocks),
            [g, q_all, gs, p],
            flops=2 * len(blocks) * tok * all_rows * (width + lat),
        )
        return dict(zip(blocks, made))

    middle = lines // 2
    made = partials("middle_gradients", [middle], near_gs, near_p)
    made.update(partials("near_gradients", [m for m in range(most) if m != middle], near_gs, after(near_p, made[middle])))
    near_parts = [made[m] for m in range(most)]
    parts = list(near_parts) + [last_part]
    kept = [parts[0]]
    for bit in range(line_bits):
        for m in range(3 << bit, lines, 2 << bit):
            got = last_got if m == most and bit == 0 else swap(parts[m], GROUP << bit)
            parts[m ^ 1 << bit] = add(parts[m ^ 1 << bit], got)
    mine_two = jnp.concatenate([mine, across], axis=0)
    other_two = swap(mine_two, 1)
    pieces = [mine_two[:heads], other_two[:heads], mine_two[heads:], other_two[heads:]]
    parts[1] = after(parts[1], gq_sum)
    kept += [swap(parts[1 << bit], GROUP << bit) for bit in reversed(range(line_bits))]
    scale = 1.0 / math.sqrt(tok * n_ctx * n_dp)
    (grad_w,) = call(
        functools.partial(spread_kernel, scale),
        "spread",
        [((heads, lat, HEAD_DIM), F32)],
        [idx] + pieces,
        smem=(0,),
    )
    gq_pieces = [gq_own, gq_core, gq_last]
    (grad_q,) = call(sum_kernel, "query_sum", [((heads, width, tok), BF16)], gq_pieces)
    kept[0] = after(kept[0], grad_q)
    (grad_lat,) = call(sum_kernel, "latent_sum", [((width, tok), BF16)], kept)
    return (jnp.transpose(grad_q, (2, 0, 1))[None], grad_lat.T[None], grad_w)


def solution(mesh):
    placed = (
        P("dp", "ctx"),
        P("dp", "ctx", None, None),
        P("dp", "ctx", None),
        P("dp", "ctx", None, None),
        P("dp", "ctx", None, None),
        P(),
    )
    return jax.shard_map(
        functools.partial(body, mesh.shape["ctx"], mesh.shape["dp"]),
        mesh=mesh,
        in_specs=placed,
        out_specs=(P("dp", "ctx", None, None), P("dp", "ctx", None), P()),
        check_vma=False,
    )
```

```python
import functools
import math

import jax
import jax.numpy as jnp
from jax import lax
from jax.experimental import pallas as pl
from jax.experimental.pallas import tpu as pltpu
from jax.sharding import PartitionSpec as P

ROPE = 64
HEAD_DIM = 128
GROUP = 4
EXTRA = 16
CUTS = 3
PACK_LIMIT = 63 << 20
F32 = jnp.float32
BF16 = jnp.bfloat16


def mm(a, b):
    return jnp.dot(a, b, preferred_element_type=F32)


def mm_t(a, b):
    return lax.dot_general(a, b, (((1,), (1,)), ((), ())), preferred_element_type=F32)


def size_of(shape, dtype):
    return math.prod(shape) * jnp.dtype(dtype).itemsize


def call(kernel, name, outs, args, scratch=(), flops=0, smem=(), hbm=(), copies=0, limit=None, share=1, out=pltpu.VMEM):
    def place(i):
        return pltpu.SMEM if i in smem else pltpu.HBM if i in hbm else pltpu.VMEM

    moved = sum(size_of(a.shape, a.dtype) for a in args) + sum(size_of(*o) for o in outs)
    held = moved + sum(size_of(*s) for s in scratch)
    semaphores = [pltpu.SemaphoreType.DMA((copies,))] if copies else []
    return pl.pallas_call(
        kernel,
        out_shape=[jax.ShapeDtypeStruct(s, d) for s, d in outs],
        in_specs=[pl.BlockSpec(memory_space=place(i)) for i in range(len(args))],
        out_specs=[pl.BlockSpec(memory_space=out) for _ in outs],
        scratch_shapes=[pltpu.VMEM(s, d) for s, d in scratch] + semaphores,
        compiler_params=pltpu.CompilerParams(vmem_limit_bytes=limit or int(1.2 * held) + (8 << 20)),
        cost_estimate=pl.CostEstimate(flops=flops * share, bytes_accessed=moved * share, transcendentals=0),
        name=name,
    )(*args)


def fetch(pairs, sems):
    copies = [pltpu.make_async_copy(src, dst, sems.at[i]) for i, (src, dst) in enumerate(pairs)]
    for copy in copies:
        copy.start()
    return copies


def pack_kernel(
    idx_ref, pos_hbm, q_hbm, og_hbm, lat_hbm, attn_hbm, wuv_hbm,
    lat_msg, q_msg, delta_hbm, keep_hbm, send_hbm,
    pos_ref, og_ref, attn_ref, wuv_ref, term, rows_ref, og_t_ref, delta_ref, keep_ref, send_ref,
    lat_ref, q_ref, sems,
):
    heads, width, tok = q_hbm.shape
    _, lat, _ = wuv_ref.shape
    started = []

    def send_off(src, dst):
        copy = pltpu.make_async_copy(src, dst, sems.at[len(started)])
        copy.start()
        started.append(copy)

    send_off(og_hbm, og_ref)
    send_off(pos_hbm, pos_ref)
    send_off(attn_hbm, attn_ref)
    send_off(wuv_hbm, wuv_ref)
    send_off(lat_hbm, lat_ref)
    for h in range(heads):
        send_off(q_hbm.at[h], q_ref.at[h])
    started[0].wait()
    for h in range(heads):
        og_t_ref[h] = og_ref[:, h, :].T
        send_off(og_t_ref.at[h], q_msg.at[pl.ds(heads * width + h * HEAD_DIM, HEAD_DIM), :])
    started[1].wait()
    pos = jnp.broadcast_to(pos_ref[...], (EXTRA, tok))
    row = lax.broadcasted_iota(jnp.int32, (EXTRA, tok), 0)
    high = lax.shift_right_logical(pos, 6)
    both = jnp.where(row == 0, high, jnp.where(row == 1, pos - high * 64, 0))
    rows_ref[...] = both.astype(F32).astype(BF16)
    send_off(rows_ref, lat_msg.at[pl.ds(width, EXTRA), :])
    send_off(rows_ref, q_msg.at[pl.ds(heads * (width + HEAD_DIM), EXTRA), :])
    started[4].wait()
    send_off(lat_ref, lat_msg.at[pl.ds(0, width), :])
    for h in range(heads):
        started[5 + h].wait()
        send_off(q_ref.at[h], q_msg.at[pl.ds(h * width, width), :])
    delta_ref[...] = jnp.zeros_like(delta_ref)
    started[2].wait()
    attn = [attn_ref[:, h, :].T for h in range(heads)]
    for h in range(heads):
        term[h] = mm_t(attn[h], og_t_ref[h])
    step = lat // GROUP
    me = lax.rem(idx_ref[0], GROUP)
    for k in range(GROUP):
        at = pl.multiple_of(jnp.bitwise_xor(me, k) * step, step)
        target = send_ref if k % 2 else keep_ref
        target[k // 2 * heads : (k // 2 + 1) * heads] = term[:, pl.ds(at, step), :].astype(BF16)
    send_off(send_ref, send_hbm)
    send_off(keep_ref, keep_hbm)
    started[3].wait()
    for h in range(heads):
        g = mm(wuv_ref[h], og_t_ref[h]).astype(BF16).astype(F32)
        delta_ref[h : h + 1, :] = jnp.sum(g * attn[h].astype(F32), axis=0, keepdims=True)
    send_off(delta_ref, delta_hbm)
    for copy in started[5 + heads :]:
        copy.wait()


def hold_kernel(*refs):
    half = len(refs) // 2
    for source, target in zip(refs[:half], refs[half:]):
        target[...] = source[...]


def score_kernel(factor, nkey, width, heads, last, *refs):
    lat_refs, refs = refs[:nkey], refs[nkey:]
    tok = lat_refs[0].shape[1]
    rows = heads * tok
    if last:
        q_all_ref, near_ref, delta_ref, s_ref, k_ref, stat_ref, kt = refs
    else:
        q_refs, refs = refs[:GROUP], refs[GROUP:]
        s_ref, k_ref, stat_ref, q_all_ref, kt = refs
        for j in range(GROUP):
            for h in range(heads):
                cols = slice(j * rows + h * tok, j * rows + (h + 1) * tok)
                q_all_ref[:width, cols] = q_refs[j][h * width : (h + 1) * width, :]
                q_all_ref[width : width + EXTRA, cols] = q_refs[j][q_refs[j].shape[0] - EXTRA :, :]
        spare = q_all_ref.shape[0] - width - EXTRA
        q_all_ref[width + EXTRA :, :] = jnp.zeros((spare, GROUP * rows), BF16)
    wide = kt.shape[0]
    for a in range(nkey):
        kt[: width + EXTRA, a * tok : (a + 1) * tok] = lat_refs[a][...]
    kt[width + EXTRA :, :] = jnp.zeros((wide - width - EXTRA, nkey * tok), BF16)
    keys = kt[...].T
    pos = keys[:, wide - 128 :].astype(F32)
    at = width - (wide - 128)
    key_pos = pos[:, at : at + 1] * 64.0 + pos[:, at + 1 : at + 2]
    lane = lax.broadcasted_iota(jnp.int32, keys.shape, 1)
    k_ref[...] = jnp.where(lane < width, keys, jnp.zeros_like(keys))
    stat_ref[...] = jnp.zeros_like(stat_ref)
    if last:
        stat_ref[GROUP * heads : GROUP * heads + heads, :] = delta_ref[:heads, :]
    for j in range(GROUP):
        cols = slice(j * rows, (j + 1) * rows)
        qp = q_all_ref[width : width + EXTRA, cols].astype(F32)
        row_pos = qp[0:1, :] * 64.0 + qp[1:2, :]
        s = mm(k_ref[...], q_all_ref[:, cols]) * factor
        s = jnp.where(key_pos <= row_pos, s, -1e30)
        s_ref[:, cols] = s
        top = jnp.max(s, axis=0, keepdims=True)
        lse = top + jnp.log(jnp.sum(jnp.exp(s - top), axis=0, keepdims=True))
        for h in range(heads):
            at = j * heads + h
            part = lse[:, h * tok : (h + 1) * tok]
            if last:
                near = near_ref[at : at + 1, :]
                most = jnp.maximum(part, near)
                part = most + jnp.log(jnp.exp(part - most) + jnp.exp(near - most))
            stat_ref[at : at + 1, :] = part


def context_kernel(width, heads, *refs):
    q_refs = refs[:GROUP]
    wuv_ref, near_k_ref, last_k_ref, g_ref, near_gp_ref, last_gp_ref = refs[GROUP:]
    lat, all_rows = g_ref.shape
    tok = q_refs[0].shape[1]
    rows = heads * tok
    for j in range(GROUP):
        for h in range(heads):
            at = heads * width + h * HEAD_DIM
            og = q_refs[j][at : at + HEAD_DIM, :]
            col = j * rows + h * tok
            g_ref[:, col : col + tok] = mm(wuv_ref[h], og).astype(BF16)
        cols = slice(j * rows, (j + 1) * rows)
        near_gp_ref[:, cols] = mm(near_k_ref[:, :lat], g_ref[:, cols])
        last_gp_ref[:, cols] = mm(last_k_ref[:, :lat], g_ref[:, cols])


def pair_kernel(heads, *refs):
    stats, (s_ref, gp_ref, gs_ref, p_ref) = refs[:GROUP], refs[GROUP : GROUP + 4]
    all_rows = s_ref.shape[1]
    rows = all_rows // GROUP
    for j in range(GROUP):
        cols = slice(j * rows, (j + 1) * rows)
        lse_parts = []
        for k in range(GROUP):
            at = (j ^ k) * heads
            lse_parts.append(
                jnp.concatenate([stats[k][at + h : at + h + 1, :] for h in range(heads)], axis=1)
            )
        top = functools.reduce(jnp.maximum, lse_parts)
        lse = top + jnp.log(sum(jnp.exp(part - top) for part in lse_parts))
        at = GROUP * heads
        delta = jnp.concatenate([stats[j][at + h : at + h + 1, :] for h in range(heads)], axis=1)
        p = jnp.exp(s_ref[:, cols] - lse)
        gs_ref[:, cols] = (p * (gp_ref[:, cols] - delta)).astype(BF16)
        p_ref[:, cols] = p.astype(BF16)


def partial_kernel(factor, places, width, g_ref, q_all_ref, gs_ref, p_ref, *part_refs):
    lat = g_ref.shape[0]
    for a, at in enumerate(places):
        along = mm_t(q_all_ref[:width, :], gs_ref[at, :]) * factor
        value = mm_t(g_ref[...], p_ref[at, :])
        part_refs[a][:lat, :] = (along[:lat] + value).astype(BF16)
        part_refs[a][lat:, :] = along[lat:].astype(BF16)


def last_kernel(factor, width, heads, *refs):
    stats, refs = refs[:GROUP], refs[GROUP:]
    s_ref, gp_ref, g_ref, q_all_ref, part_ref, gs_ref, p_ref = refs
    pair_kernel(heads, *stats, s_ref, gp_ref, gs_ref, p_ref)
    partial_kernel(factor, [slice(None)], width, g_ref, q_all_ref, gs_ref, p_ref, part_ref)


def query_kernel(factor, nkey, width, heads, *refs):
    stats, refs = refs[:GROUP], refs[GROUP:]
    (s_ref, gp_ref, last_gs_ref), refs = refs[:3], refs[3:]
    lat_refs, refs = refs[:nkey], refs[nkey:]
    gq_refs, far_refs, (gs_ref, p_ref, kt) = refs[: GROUP - 1], refs[GROUP - 1 : -3], refs[-3:]
    tok = lat_refs[0].shape[1]
    keys = s_ref.shape[0]
    rows = heads * tok
    for a in range(nkey):
        kt[:, a * tok : (a + 1) * tok] = lat_refs[a][:width, :]
    pair_kernel(heads, *stats, s_ref, gp_ref, gs_ref, p_ref)
    for j in range(GROUP):
        cols = slice(j * rows, (j + 1) * rows)
        gq = mm(kt[:, :keys], gs_ref[:, cols]) + mm(kt[:, keys:], last_gs_ref[:, cols])
        gq = (gq * factor).astype(BF16)
        for h in range(heads):
            part = gq[:, h * tok : (h + 1) * tok]
            if j < GROUP - 1:
                gq_refs[j][h] = part
            else:
                for c, at, here in segments(h, width, far_refs):
                    far_refs[c][here, :] = part[at]


def segments(head, width, pieces):
    cut = pieces[0].shape[0]
    found = []
    for c in range(len(pieces)):
        low, high = max(head * width, c * cut), min((head + 1) * width, (c + 1) * cut)
        if low < high:
            at = slice(low - head * width, high - head * width)
            found.append((c, at, slice(low - c * cut, high - c * cut)))
    return found


def join_kernel(whole_ref, *refs):
    pieces, out_ref = refs[:-1], refs[-1]
    heads, width, _ = out_ref.shape
    for h in range(heads):
        for c, at, here in segments(h, width, pieces):
            both = whole_ref[h, at, :].astype(F32) + pieces[c][here, :].astype(F32)
            out_ref[h, at, :] = both.astype(BF16)


def sum_kernel(*refs):
    refs[-1][...] = sum(ref[...].astype(F32) for ref in refs[:-1]).astype(BF16)


def spread_kernel(scale, idx_ref, *refs):
    chunks, out_ref = refs[:GROUP], refs[GROUP]
    step = chunks[0].shape[1]
    me = lax.rem(idx_ref[0], GROUP)
    for k in range(GROUP):
        at = pl.multiple_of(jnp.bitwise_xor(me, k) * step, step)
        out_ref[:, pl.ds(at, step), :] = chunks[k][...].astype(F32) * scale


def body(n_ctx, n_dp, positions, queries, latent, out_grad, attn_out, wuv):
    tok, heads, width = queries.shape[1:]
    lat = attn_out.shape[3]
    lines = n_ctx // GROUP
    line_bits = (lines - 1).bit_length()
    rows = heads * tok
    all_rows = GROUP * rows
    keys = lines * tok
    wide = -(-(width + EXTRA) // 128) * 128
    factor = (HEAD_DIM + ROPE) ** (-0.5)

    def swap(x, mask, axis="ctx", size=n_ctx):
        return lax.ppermute(x, axis, [(i, i ^ mask) for i in range(size)])

    def after(x, *done):
        return lax.optimization_barrier((x, done))[0]

    idx = lax.axis_index("ctx").reshape(1)
    step = lat // GROUP
    lat_msg, q_msg, delta, keep, send = call(
        pack_kernel,
        "pack",
        [
            ((width + EXTRA, tok), BF16),
            ((heads * (width + HEAD_DIM) + EXTRA, tok), BF16),
            ((8, tok), F32),
            ((2 * heads, step, HEAD_DIM), BF16),
            ((2 * heads, step, HEAD_DIM), BF16),
        ],
        [
            idx,
            positions,
            jnp.transpose(queries[0], (1, 2, 0)),
            out_grad[0],
            latent[0].T,
            attn_out[0],
            wuv,
        ],
        [
            ((1, tok), jnp.int32),
            (out_grad.shape[1:], BF16),
            (attn_out.shape[1:], BF16),
            (wuv.shape, BF16),
            ((heads, lat, HEAD_DIM), F32),
            ((EXTRA, tok), BF16),
            ((heads, HEAD_DIM, tok), BF16),
            ((8, tok), F32),
            ((2 * heads, step, HEAD_DIM), BF16),
            ((2 * heads, step, HEAD_DIM), BF16),
            ((width, tok), BF16),
            ((heads, width, tok), BF16),
        ],
        smem=(0,),
        hbm=(1, 2, 3, 4, 5, 6),
        copies=11 + 3 * heads,
        out=pltpu.HBM,
        limit=PACK_LIMIT,
    )

    def add(a, b):
        return (a.astype(F32) + b.astype(F32)).astype(BF16)

    dp_hops = [(1 << bit, "dp", n_dp) for bit in range((n_dp - 1).bit_length())]
    line_hops = [(GROUP << bit,) for bit in range(line_bits)]

    q_across = swap(q_msg, 2)
    q_core = swap(q_msg, 1)
    pair = add(keep, swap(send, 1))
    got_pair = swap(pair, *dp_hops[0])
    firsts = [swap(after(lat_msg, q_core) if bit + 1 < line_bits else lat_msg, GROUP << bit) for bit in range(line_bits)]
    own = call(
        hold_kernel,
        "hold_own",
        [(lat_msg.shape, BF16), (q_msg.shape, BF16), (delta.shape, F32)],
        [lat_msg, q_msg, delta],
        share=0,
    )
    q_core, q_across, firsts, got_pair, own = lax.optimization_barrier(
        (q_core, q_across, firsts, got_pair, own)
    )
    held = {0: lat_msg}
    for bit in reversed(range(line_bits)):
        held.update({m | 1 << bit: swap(x, GROUP << bit) for m, x in held.items() if m})
        held[1 << bit] = firsts[bit]
    pair = add(pair, got_pair)
    for step_hop in dp_hops[1:]:
        pair = add(pair, swap(pair, *step_hop))
    lats = [held[m] for m in range(lines)]
    q_far = swap(q_across, 1)
    got_own = swap(pair[heads:], 2)
    lat_own, q_own, delta = own
    lats[0] = lat_own
    qs = [q_own, q_core, q_across, q_far]

    most = lines - 1
    keys = most * tok
    score_flops = 2 * tok * all_rows * wide
    near_s, near_k, near_stat, q_all = call(
        functools.partial(score_kernel, factor, most, width, heads, False),
        "near_scores",
        [((keys, all_rows), F32), ((keys, wide), BF16), ((EXTRA, tok), F32), ((wide, all_rows), BF16)],
        lats[:most] + qs,
        [((wide, keys), BF16)],
        flops=most * score_flops,
        share=0,
    )
    mine = add(pair[:heads], after(got_own, near_stat))
    near = swap(mine, *line_hops[0])
    last_s, last_k, stat = call(
        functools.partial(score_kernel, factor, 1, width, heads, True),
        "last_scores",
        [((tok, all_rows), F32), ((tok, wide), BF16), ((EXTRA, tok), F32)],
        [lats[most], q_all, near_stat, delta],
        [((wide, tok), BF16)],
        flops=score_flops,
    )
    stats = [stat] + [swap(stat, k) for k in range(1, GROUP)]
    g, near_gp, last_gp = call(
        functools.partial(context_kernel, width, heads),
        "context",
        [((lat, all_rows), BF16), ((keys, all_rows), F32), ((tok, all_rows), F32)],
        qs + [wuv, near_k, last_k],
        flops=2 * lines * tok * all_rows * lat + 2 * all_rows * lat * HEAD_DIM,
        share=3,
    )
    mine = add(mine, after(near, stat))
    for step_hop in line_hops[1:-1]:
        mine = add(mine, swap(mine, *step_hop))
    near = swap(mine, *line_hops[-1])
    last_part, last_gs = call(
        functools.partial(last_kernel, factor, width, heads),
        "last_gradients",
        [((width, tok), BF16), ((tok, all_rows), BF16)],
        stats + [last_s, last_gp, g, q_all],
        [((tok, all_rows), BF16)],
        flops=2 * tok * all_rows * (width + lat),
    )
    last_got = swap(last_part, GROUP)
    mine = add(mine, near)
    gq_shape, cut_shape = (heads, width, tok), (heads * width // CUTS, tok)
    gq_own, gq_core, gq_across, *far_cuts, near_gs, near_p = call(
        functools.partial(query_kernel, factor, lines, width, heads),
        "query_gradients",
        [(gq_shape, BF16)] * 3 + [(cut_shape, BF16)] * CUTS + [((keys, all_rows), BF16)] * 2,
        stats + [near_s, near_gp, after(last_gs, mine)] + lats,
        [((width, lines * tok), BF16)],
        flops=2 * lines * tok * all_rows * width,
        share=0,
    )
    across = swap(mine, 2)
    far_cuts = [swap(cut, 1) for cut in far_cuts]
    (gq_sum,) = call(join_kernel, "join", [(gq_shape, BF16)], [after(gq_across, across)] + far_cuts)
    gq_last = swap(gq_sum, 2)
    gq_core = swap(after(gq_core, gq_sum), 1)
    def partials(name, blocks, gs, p, share=1):
        rows = [slice(m * tok, (m + 1) * tok) for m in blocks]
        made = call(
            functools.partial(partial_kernel, factor, rows, width),
            name,
            [((width, tok), BF16)] * len(blocks),
            [g, q_all, gs, p],
            flops=2 * len(blocks) * tok * all_rows * (width + lat),
            share=share,
        )
        return dict(zip(blocks, made))

    middle = lines // 2
    made = partials("middle_gradients", [middle], near_gs, near_p, 3)
    made.update(partials("near_gradients", [m for m in range(most) if m != middle], near_gs, after(near_p, *far_cuts)))
    near_parts = [made[m] for m in range(most)]
    parts = list(near_parts) + [last_part]
    kept = [parts[0]]
    for bit in range(line_bits):
        for m in range(3 << bit, lines, 2 << bit):
            got = last_got if m == most and bit == 0 else swap(parts[m], GROUP << bit)
            parts[m ^ 1 << bit] = add(parts[m ^ 1 << bit], got)
    mine_two = jnp.concatenate([mine, across], axis=0)
    other_two = swap(mine_two, 1)
    pieces = [mine_two[:heads], other_two[:heads], mine_two[heads:], other_two[heads:]]
    parts[1] = after(parts[1], gq_sum)
    kept += [swap(parts[1 << bit], GROUP << bit) for bit in reversed(range(line_bits))]
    scale = 1.0 / math.sqrt(tok * n_ctx * n_dp)
    (grad_w,) = call(
        functools.partial(spread_kernel, scale),
        "spread",
        [((heads, lat, HEAD_DIM), F32)],
        [idx] + pieces,
        smem=(0,),
    )
    gq_pieces = [gq_own, gq_core, gq_last]
    (grad_q,) = call(sum_kernel, "query_sum", [((heads, width, tok), BF16)], gq_pieces)
    kept[0] = after(kept[0], grad_q)
    (grad_lat,) = call(sum_kernel, "latent_sum", [((width, tok), BF16)], kept)
    return (jnp.transpose(grad_q, (2, 0, 1))[None], grad_lat.T[None], grad_w)


def solution(mesh):
    placed = (
        P("dp", "ctx"),
        P("dp", "ctx", None, None),
        P("dp", "ctx", None),
        P("dp", "ctx", None, None),
        P("dp", "ctx", None, None),
        P(),
    )
    return jax.shard_map(
        functools.partial(body, mesh.shape["ctx"], mesh.shape["dp"]),
        mesh=mesh,
        in_specs=placed,
        out_specs=(P("dp", "ctx", None, None), P("dp", "ctx", None), P()),
        check_vma=False,
    )
```

```python
import functools
import math

import jax
import jax.numpy as jnp
from jax import lax
from jax.experimental import pallas as pl
from jax.experimental.pallas import tpu as pltpu
from jax.sharding import PartitionSpec as P

ROPE = 64
HEAD_DIM = 128
GROUP = 4
EXTRA = 16
CUTS = 2
PACK_LIMIT = 63 << 20
F32 = jnp.float32
BF16 = jnp.bfloat16


def mm(a, b):
    return jnp.dot(a, b, preferred_element_type=F32)


def mm_t(a, b):
    return lax.dot_general(a, b, (((1,), (1,)), ((), ())), preferred_element_type=F32)


def size_of(shape, dtype):
    return math.prod(shape) * jnp.dtype(dtype).itemsize


def call(kernel, name, outs, args, scratch=(), flops=0, smem=(), hbm=(), copies=0, limit=None, share=1, out=pltpu.VMEM):
    def place(i):
        return pltpu.SMEM if i in smem else pltpu.HBM if i in hbm else pltpu.VMEM

    moved = sum(size_of(a.shape, a.dtype) for a in args) + sum(size_of(*o) for o in outs)
    held = moved + sum(size_of(*s) for s in scratch)
    semaphores = [pltpu.SemaphoreType.DMA((copies,))] if copies else []
    return pl.pallas_call(
        kernel,
        out_shape=[jax.ShapeDtypeStruct(s, d) for s, d in outs],
        in_specs=[pl.BlockSpec(memory_space=place(i)) for i in range(len(args))],
        out_specs=[pl.BlockSpec(memory_space=out) for _ in outs],
        scratch_shapes=[pltpu.VMEM(s, d) for s, d in scratch] + semaphores,
        compiler_params=pltpu.CompilerParams(vmem_limit_bytes=limit or int(1.2 * held) + (8 << 20)),
        cost_estimate=pl.CostEstimate(flops=flops * share, bytes_accessed=moved * share, transcendentals=0),
        name=name,
    )(*args)


def fetch(pairs, sems):
    copies = [pltpu.make_async_copy(src, dst, sems.at[i]) for i, (src, dst) in enumerate(pairs)]
    for copy in copies:
        copy.start()
    return copies


def pack_kernel(
    idx_ref, pos_hbm, q_hbm, og_hbm, lat_hbm, attn_hbm, wuv_hbm,
    lat_msg, q_msg, delta_hbm, keep_hbm, send_hbm,
    pos_ref, og_ref, attn_ref, wuv_ref, term, rows_ref, og_t_ref, delta_ref, keep_ref, send_ref,
    lat_ref, q_ref, sems,
):
    heads, width, tok = q_hbm.shape
    _, lat, _ = wuv_ref.shape
    started = []

    def send_off(src, dst):
        copy = pltpu.make_async_copy(src, dst, sems.at[len(started)])
        copy.start()
        started.append(copy)

    send_off(og_hbm, og_ref)
    send_off(pos_hbm, pos_ref)
    send_off(attn_hbm, attn_ref)
    send_off(wuv_hbm, wuv_ref)
    send_off(lat_hbm, lat_ref)
    for h in range(heads):
        send_off(q_hbm.at[h], q_ref.at[h])
    started[0].wait()
    for h in range(heads):
        og_t_ref[h] = og_ref[:, h, :].T
        send_off(og_t_ref.at[h], q_msg.at[pl.ds(heads * width + h * HEAD_DIM, HEAD_DIM), :])
    started[1].wait()
    pos = jnp.broadcast_to(pos_ref[...], (EXTRA, tok))
    row = lax.broadcasted_iota(jnp.int32, (EXTRA, tok), 0)
    high = lax.shift_right_logical(pos, 6)
    both = jnp.where(row == 0, high, jnp.where(row == 1, pos - high * 64, 0))
    rows_ref[...] = both.astype(F32).astype(BF16)
    send_off(rows_ref, lat_msg.at[pl.ds(width, EXTRA), :])
    send_off(rows_ref, q_msg.at[pl.ds(heads * (width + HEAD_DIM), EXTRA), :])
    started[4].wait()
    send_off(lat_ref, lat_msg.at[pl.ds(0, width), :])
    for h in range(heads):
        started[5 + h].wait()
        send_off(q_ref.at[h], q_msg.at[pl.ds(h * width, width), :])
    delta_ref[...] = jnp.zeros_like(delta_ref)
    started[2].wait()
    attn = [attn_ref[:, h, :].T for h in range(heads)]
    for h in range(heads):
        term[h] = mm_t(attn[h], og_t_ref[h])
    step = lat // GROUP
    me = lax.rem(idx_ref[0], GROUP)
    for k in range(GROUP):
        at = pl.multiple_of(jnp.bitwise_xor(me, k) * step, step)
        target = send_ref if k % 2 else keep_ref
        target[k // 2 * heads : (k // 2 + 1) * heads] = term[:, pl.ds(at, step), :].astype(BF16)
    send_off(send_ref, send_hbm)
    send_off(keep_ref, keep_hbm)
    started[3].wait()
    for h in range(heads):
        g = mm(wuv_ref[h], og_t_ref[h]).astype(BF16).astype(F32)
        delta_ref[h : h + 1, :] = jnp.sum(g * attn[h].astype(F32), axis=0, keepdims=True)
    send_off(delta_ref, delta_hbm)
    for copy in started[5 + heads :]:
        copy.wait()


def hold_kernel(*refs):
    half = len(refs) // 2
    for source, target in zip(refs[:half], refs[half:]):
        target[...] = source[...]


def score_kernel(factor, nkey, width, heads, last, *refs):
    lat_refs, refs = refs[:nkey], refs[nkey:]
    tok = lat_refs[0].shape[1]
    rows = heads * tok
    if last:
        q_all_ref, near_ref, delta_ref, s_ref, k_ref, stat_ref, kt = refs
    else:
        q_refs, refs = refs[:GROUP], refs[GROUP:]
        s_ref, k_ref, stat_ref, q_all_ref, kt = refs
        for j in range(GROUP):
            for h in range(heads):
                cols = slice(j * rows + h * tok, j * rows + (h + 1) * tok)
                q_all_ref[:width, cols] = q_refs[j][h * width : (h + 1) * width, :]
                q_all_ref[width : width + EXTRA, cols] = q_refs[j][q_refs[j].shape[0] - EXTRA :, :]
        spare = q_all_ref.shape[0] - width - EXTRA
        q_all_ref[width + EXTRA :, :] = jnp.zeros((spare, GROUP * rows), BF16)
    wide = kt.shape[0]
    for a in range(nkey):
        kt[: width + EXTRA, a * tok : (a + 1) * tok] = lat_refs[a][...]
    kt[width + EXTRA :, :] = jnp.zeros((wide - width - EXTRA, nkey * tok), BF16)
    keys = kt[...].T
    pos = keys[:, wide - 128 :].astype(F32)
    at = width - (wide - 128)
    key_pos = pos[:, at : at + 1] * 64.0 + pos[:, at + 1 : at + 2]
    lane = lax.broadcasted_iota(jnp.int32, keys.shape, 1)
    k_ref[...] = jnp.where(lane < width, keys, jnp.zeros_like(keys))
    stat_ref[...] = jnp.zeros_like(stat_ref)
    if last:
        stat_ref[GROUP * heads : GROUP * heads + heads, :] = delta_ref[:heads, :]
    for j in range(GROUP):
        cols = slice(j * rows, (j + 1) * rows)
        qp = q_all_ref[width : width + EXTRA, cols].astype(F32)
        row_pos = qp[0:1, :] * 64.0 + qp[1:2, :]
        s = mm(k_ref[...], q_all_ref[:, cols]) * factor
        s = jnp.where(key_pos <= row_pos, s, -1e30)
        s_ref[:, cols] = s
        top = jnp.max(s, axis=0, keepdims=True)
        lse = top + jnp.log(jnp.sum(jnp.exp(s - top), axis=0, keepdims=True))
        for h in range(heads):
            at = j * heads + h
            part = lse[:, h * tok : (h + 1) * tok]
            if last:
                near = near_ref[at : at + 1, :]
                most = jnp.maximum(part, near)
                part = most + jnp.log(jnp.exp(part - most) + jnp.exp(near - most))
            stat_ref[at : at + 1, :] = part


def context_kernel(width, heads, *refs):
    q_refs = refs[:GROUP]
    wuv_ref, near_k_ref, last_k_ref, g_ref, near_gp_ref, last_gp_ref = refs[GROUP:]
    lat, all_rows = g_ref.shape
    tok = q_refs[0].shape[1]
    rows = heads * tok
    for j in range(GROUP):
        for h in range(heads):
            at = heads * width + h * HEAD_DIM
            og = q_refs[j][at : at + HEAD_DIM, :]
            col = j * rows + h * tok
            g_ref[:, col : col + tok] = mm(wuv_ref[h], og).astype(BF16)
        cols = slice(j * rows, (j + 1) * rows)
        near_gp_ref[:, cols] = mm(near_k_ref[:, :lat], g_ref[:, cols])
        last_gp_ref[:, cols] = mm(last_k_ref[:, :lat], g_ref[:, cols])


def pair_kernel(heads, keys, *refs):
    stats, (s_ref, gp_ref, gs_ref, p_ref) = refs[:GROUP], refs[GROUP : GROUP + 4]
    all_rows = s_ref.shape[1]
    rows = all_rows // GROUP
    for j in range(GROUP):
        cols = slice(j * rows, (j + 1) * rows)
        lse_parts = []
        for k in range(GROUP):
            at = (j ^ k) * heads
            lse_parts.append(
                jnp.concatenate([stats[k][at + h : at + h + 1, :] for h in range(heads)], axis=1)
            )
        top = functools.reduce(jnp.maximum, lse_parts)
        lse = top + jnp.log(sum(jnp.exp(part - top) for part in lse_parts))
        at = GROUP * heads
        delta = jnp.concatenate([stats[j][at + h : at + h + 1, :] for h in range(heads)], axis=1)
        p = jnp.exp(s_ref[keys, cols] - lse)
        gs_ref[:, cols] = (p * (gp_ref[keys, cols] - delta)).astype(BF16)
        p_ref[:, cols] = p.astype(BF16)


def partial_kernel(factor, places, width, g_ref, q_all_ref, gs_ref, p_ref, *part_refs):
    lat = g_ref.shape[0]
    for a, at in enumerate(places):
        along = mm_t(q_all_ref[:width, :], gs_ref[at, :]) * factor
        value = mm_t(g_ref[...], p_ref[at, :])
        part_refs[a][:lat, :] = (along[:lat] + value).astype(BF16)
        part_refs[a][lat:, :] = along[lat:].astype(BF16)


def block_kernel(factor, keys, width, heads, *refs):
    stats, refs = refs[:GROUP], refs[GROUP:]
    s_ref, gp_ref, g_ref, q_all_ref, part_ref, gs_ref, p_ref = refs
    pair_kernel(heads, keys, *stats, s_ref, gp_ref, gs_ref, p_ref)
    partial_kernel(factor, [slice(None)], width, g_ref, q_all_ref, gs_ref, p_ref, part_ref)


def query_kernel(factor, nkey, width, heads, *refs):
    stats, refs = refs[:GROUP], refs[GROUP:]
    (s_ref, gp_ref, last_gs_ref), refs = refs[:3], refs[3:]
    lat_refs, refs = refs[:nkey], refs[nkey:]
    gq_refs, far_refs, (gs_ref, p_ref, kt) = refs[: GROUP - 1], refs[GROUP - 1 : -3], refs[-3:]
    tok = lat_refs[0].shape[1]
    keys = s_ref.shape[0]
    rows = heads * tok
    for a in range(nkey):
        kt[:, a * tok : (a + 1) * tok] = lat_refs[a][:width, :]
    pair_kernel(heads, slice(None), *stats, s_ref, gp_ref, gs_ref, p_ref)
    for j in range(GROUP):
        cols = slice(j * rows, (j + 1) * rows)
        gq = mm(kt[:, :keys], gs_ref[:, cols]) + mm(kt[:, keys:], last_gs_ref[:, cols])
        gq = (gq * factor).astype(BF16)
        for h in range(heads):
            part = gq[:, h * tok : (h + 1) * tok]
            if j < GROUP - 1:
                gq_refs[j][h] = part
            else:
                for c, at, here in segments(h, width, far_refs):
                    far_refs[c][here, :] = part[at]


def segments(head, width, pieces):
    cut = pieces[0].shape[0]
    found = []
    for c in range(len(pieces)):
        low, high = max(head * width, c * cut), min((head + 1) * width, (c + 1) * cut)
        if low < high:
            at = slice(low - head * width, high - head * width)
            found.append((c, at, slice(low - c * cut, high - c * cut)))
    return found


def join_kernel(whole_ref, *refs):
    pieces, out_ref = refs[:-1], refs[-1]
    heads, width, _ = out_ref.shape
    for h in range(heads):
        for c, at, here in segments(h, width, pieces):
            both = whole_ref[h, at, :].astype(F32) + pieces[c][here, :].astype(F32)
            out_ref[h, at, :] = both.astype(BF16)


def sum_kernel(*refs):
    refs[-1][...] = sum(ref[...].astype(F32) for ref in refs[:-1]).astype(BF16)


def spread_kernel(scale, idx_ref, *refs):
    chunks, out_ref = refs[:GROUP], refs[GROUP]
    step = chunks[0].shape[1]
    me = lax.rem(idx_ref[0], GROUP)
    for k in range(GROUP):
        at = pl.multiple_of(jnp.bitwise_xor(me, k) * step, step)
        out_ref[:, pl.ds(at, step), :] = chunks[k][...].astype(F32) * scale


def body(n_ctx, n_dp, positions, queries, latent, out_grad, attn_out, wuv):
    tok, heads, width = queries.shape[1:]
    lat = attn_out.shape[3]
    lines = n_ctx // GROUP
    line_bits = (lines - 1).bit_length()
    rows = heads * tok
    all_rows = GROUP * rows
    keys = lines * tok
    wide = -(-(width + EXTRA) // 128) * 128
    factor = (HEAD_DIM + ROPE) ** (-0.5)

    def swap(x, mask, axis="ctx", size=n_ctx):
        return lax.ppermute(x, axis, [(i, i ^ mask) for i in range(size)])

    def after(x, *done):
        return lax.optimization_barrier((x, done))[0]

    idx = lax.axis_index("ctx").reshape(1)
    step = lat // GROUP
    lat_msg, q_msg, delta, keep, send = call(
        pack_kernel,
        "pack",
        [
            ((width + EXTRA, tok), BF16),
            ((heads * (width + HEAD_DIM) + EXTRA, tok), BF16),
            ((8, tok), F32),
            ((2 * heads, step, HEAD_DIM), BF16),
            ((2 * heads, step, HEAD_DIM), BF16),
        ],
        [
            idx,
            positions,
            jnp.transpose(queries[0], (1, 2, 0)),
            out_grad[0],
            latent[0].T,
            attn_out[0],
            wuv,
        ],
        [
            ((1, tok), jnp.int32),
            (out_grad.shape[1:], BF16),
            (attn_out.shape[1:], BF16),
            (wuv.shape, BF16),
            ((heads, lat, HEAD_DIM), F32),
            ((EXTRA, tok), BF16),
            ((heads, HEAD_DIM, tok), BF16),
            ((8, tok), F32),
            ((2 * heads, step, HEAD_DIM), BF16),
            ((2 * heads, step, HEAD_DIM), BF16),
            ((width, tok), BF16),
            ((heads, width, tok), BF16),
        ],
        smem=(0,),
        hbm=(1, 2, 3, 4, 5, 6),
        copies=11 + 3 * heads,
        out=pltpu.HBM,
        limit=PACK_LIMIT,
    )

    def add(a, b):
        return (a.astype(F32) + b.astype(F32)).astype(BF16)

    dp_hops = [(1 << bit, "dp", n_dp) for bit in range((n_dp - 1).bit_length())]
    line_hops = [(GROUP << bit,) for bit in range(line_bits)]

    q_across = swap(q_msg, 2)
    q_core = swap(q_msg, 1)
    pair = add(keep, swap(send, 1))
    got_pair = swap(pair, *dp_hops[0])
    firsts = [swap(after(lat_msg, q_core) if bit + 1 < line_bits else lat_msg, GROUP << bit) for bit in range(line_bits)]
    own = call(
        hold_kernel,
        "hold_own",
        [(lat_msg.shape, BF16), (q_msg.shape, BF16), (delta.shape, F32)],
        [lat_msg, q_msg, delta],
        share=0,
    )
    q_core, q_across, firsts, got_pair, own = lax.optimization_barrier(
        (q_core, q_across, firsts, got_pair, own)
    )
    held = {0: lat_msg}
    for bit in reversed(range(line_bits)):
        held.update({m | 1 << bit: swap(x, GROUP << bit) for m, x in held.items() if m})
        held[1 << bit] = firsts[bit]
    pair = add(pair, got_pair)
    for step_hop in dp_hops[1:]:
        pair = add(pair, swap(pair, *step_hop))
    lats = [held[m] for m in range(lines)]
    q_far = swap(q_across, 1)
    got_own = swap(pair[heads:], 2)
    lat_own, q_own, delta = own
    lats[0] = lat_own
    qs = [q_own, q_core, q_across, q_far]

    most = lines - 1
    keys = most * tok
    score_flops = 2 * tok * all_rows * wide
    near_s, near_k, near_stat, q_all = call(
        functools.partial(score_kernel, factor, most, width, heads, False),
        "near_scores",
        [((keys, all_rows), F32), ((keys, wide), BF16), ((EXTRA, tok), F32), ((wide, all_rows), BF16)],
        lats[:most] + qs,
        [((wide, keys), BF16)],
        flops=most * score_flops,
        share=0,
    )
    mine = add(pair[:heads], after(got_own, near_stat))
    near = swap(mine, *line_hops[0])
    last_s, last_k, stat = call(
        functools.partial(score_kernel, factor, 1, width, heads, True),
        "last_scores",
        [((tok, all_rows), F32), ((tok, wide), BF16), ((EXTRA, tok), F32)],
        [lats[most], q_all, near_stat, delta],
        [((wide, tok), BF16)],
        flops=score_flops,
    )
    stats = [stat] + [swap(stat, k) for k in range(1, GROUP)]
    g, near_gp, last_gp = call(
        functools.partial(context_kernel, width, heads),
        "context",
        [((lat, all_rows), BF16), ((keys, all_rows), F32), ((tok, all_rows), F32)],
        qs + [wuv, near_k, last_k],
        flops=2 * lines * tok * all_rows * lat + 2 * all_rows * lat * HEAD_DIM,
        share=3,
    )
    mine = add(mine, after(near, stat))
    for step_hop in line_hops[1:-1]:
        mine = add(mine, swap(mine, *step_hop))
    near = swap(mine, *line_hops[-1])
    def block(name, keys_at, s, gp):
        return call(
            functools.partial(block_kernel, factor, keys_at, width, heads),
            name,
            [((width, tok), BF16), ((tok, all_rows), BF16)],
            stats + [s, gp, g, q_all],
            [((tok, all_rows), BF16)],
            flops=2 * tok * all_rows * (width + lat),
        )

    last_part, last_gs = block("last_gradients", slice(None), last_s, last_gp)
    last_got = swap(last_part, GROUP)
    next_part, _ = block("next_gradients", slice(tok, 2 * tok), near_s, near_gp)
    next_got = swap(next_part, GROUP)
    mine = add(mine, near)
    gq_shape, cut_shape = (heads, width, tok), (heads * width // CUTS, tok)
    gq_own, gq_core, gq_across, *far_cuts, near_gs, near_p = call(
        functools.partial(query_kernel, factor, lines, width, heads),
        "query_gradients",
        [(gq_shape, BF16)] * 3 + [(cut_shape, BF16)] * CUTS + [((keys, all_rows), BF16)] * 2,
        stats + [near_s, near_gp, after(last_gs, mine)] + lats,
        [((width, lines * tok), BF16)],
        flops=2 * lines * tok * all_rows * width,
        share=0,
    )
    across = swap(mine, 2)
    far_cuts = [swap(cut, 1) for cut in far_cuts]
    (gq_sum,) = call(join_kernel, "join", [(gq_shape, BF16)], [after(gq_across, across)] + far_cuts)
    gq_last = swap(gq_sum, 2)
    gq_core = swap(after(gq_core, gq_sum), 1)
    def partials(name, blocks, gs, p, share=1):
        rows = [slice(m * tok, (m + 1) * tok) for m in blocks]
        made = call(
            functools.partial(partial_kernel, factor, rows, width),
            name,
            [((width, tok), BF16)] * len(blocks),
            [g, q_all, gs, p],
            flops=2 * len(blocks) * tok * all_rows * (width + lat),
            share=share,
        )
        return dict(zip(blocks, made))

    middle = lines // 2
    made = partials("middle_gradients", [middle], near_gs, near_p, 3)
    made.update(partials("near_gradients", [m for m in range(most) if m not in (1, middle)], near_gs, after(near_p, *far_cuts)))
    made[1] = next_part
    near_parts = [made[m] for m in range(most)]
    parts = list(near_parts) + [last_part]
    kept = [parts[0]]
    for bit in range(line_bits):
        for m in range(3 << bit, lines, 2 << bit):
            got = last_got if m == most and bit == 0 else swap(parts[m], GROUP << bit)
            parts[m ^ 1 << bit] = add(parts[m ^ 1 << bit], got)
    mine_two = jnp.concatenate([mine, across], axis=0)
    other_two = swap(mine_two, 1)
    pieces = [mine_two[:heads], other_two[:heads], mine_two[heads:], other_two[heads:]]
    kept += [swap(parts[1 << bit], GROUP << bit) for bit in range(1, line_bits)] + [next_got]
    scale = 1.0 / math.sqrt(tok * n_ctx * n_dp)
    (grad_w,) = call(
        functools.partial(spread_kernel, scale),
        "spread",
        [((heads, lat, HEAD_DIM), F32)],
        [idx] + pieces,
        smem=(0,),
    )
    gq_pieces = [gq_own, gq_core, gq_last]
    (grad_q,) = call(sum_kernel, "query_sum", [((heads, width, tok), BF16)], gq_pieces)
    kept[0] = after(kept[0], grad_q)
    (grad_lat,) = call(sum_kernel, "latent_sum", [((width, tok), BF16)], kept)
    return (jnp.transpose(grad_q, (2, 0, 1))[None], grad_lat.T[None], grad_w)


def solution(mesh):
    placed = (
        P("dp", "ctx"),
        P("dp", "ctx", None, None),
        P("dp", "ctx", None),
        P("dp", "ctx", None, None),
        P("dp", "ctx", None, None),
        P(),
    )
    return jax.shard_map(
        functools.partial(body, mesh.shape["ctx"], mesh.shape["dp"]),
        mesh=mesh,
        in_specs=placed,
        out_specs=(P("dp", "ctx", None, None), P("dp", "ctx", None), P()),
        check_vma=False,
    )
```

```python
import functools
import math

import jax
import jax.numpy as jnp
from jax import lax
from jax.experimental import pallas as pl
from jax.experimental.pallas import tpu as pltpu
from jax.sharding import PartitionSpec as P

ROPE = 64
HEAD_DIM = 128
GROUP = 4
EXTRA = 16
CUTS = 2
PACK_LIMIT = 63 << 20
F32 = jnp.float32
BF16 = jnp.bfloat16


def mm(a, b):
    return jnp.dot(a, b, preferred_element_type=F32)


def mm_t(a, b):
    return lax.dot_general(a, b, (((1,), (1,)), ((), ())), preferred_element_type=F32)


def size_of(shape, dtype):
    return math.prod(shape) * jnp.dtype(dtype).itemsize


def call(kernel, name, outs, args, scratch=(), flops=0, smem=(), hbm=(), copies=0, limit=None, share=1, out=pltpu.VMEM):
    def place(i):
        return pltpu.SMEM if i in smem else pltpu.HBM if i in hbm else pltpu.VMEM

    moved = sum(size_of(a.shape, a.dtype) for a in args) + sum(size_of(*o) for o in outs)
    held = moved + sum(size_of(*s) for s in scratch)
    semaphores = [pltpu.SemaphoreType.DMA((copies,))] if copies else []
    return pl.pallas_call(
        kernel,
        out_shape=[jax.ShapeDtypeStruct(s, d) for s, d in outs],
        in_specs=[pl.BlockSpec(memory_space=place(i)) for i in range(len(args))],
        out_specs=[pl.BlockSpec(memory_space=out) for _ in outs],
        scratch_shapes=[pltpu.VMEM(s, d) for s, d in scratch] + semaphores,
        compiler_params=pltpu.CompilerParams(vmem_limit_bytes=limit or int(1.2 * held) + (8 << 20)),
        cost_estimate=pl.CostEstimate(flops=flops * share, bytes_accessed=moved * share, transcendentals=0),
        name=name,
    )(*args)


def fetch(pairs, sems):
    copies = [pltpu.make_async_copy(src, dst, sems.at[i]) for i, (src, dst) in enumerate(pairs)]
    for copy in copies:
        copy.start()
    return copies


def pack_kernel(
    idx_ref, pos_hbm, q_hbm, og_hbm, lat_hbm, attn_hbm, wuv_hbm,
    lat_msg, q_msg, delta_hbm, keep_hbm, send_hbm,
    pos_ref, og_ref, attn_ref, wuv_ref, term, rows_ref, og_t_ref, delta_ref, keep_ref, send_ref,
    lat_ref, q_ref, sems,
):
    heads, width, tok = q_hbm.shape
    _, lat, _ = wuv_ref.shape
    started = []

    def send_off(src, dst):
        copy = pltpu.make_async_copy(src, dst, sems.at[len(started)])
        copy.start()
        started.append(copy)

    send_off(og_hbm, og_ref)
    send_off(pos_hbm, pos_ref)
    send_off(attn_hbm, attn_ref)
    send_off(wuv_hbm, wuv_ref)
    send_off(lat_hbm, lat_ref)
    for h in range(heads):
        send_off(q_hbm.at[h], q_ref.at[h])
    started[0].wait()
    for h in range(heads):
        og_t_ref[h] = og_ref[:, h, :].T
        send_off(og_t_ref.at[h], q_msg.at[pl.ds(heads * width + h * HEAD_DIM, HEAD_DIM), :])
    started[1].wait()
    pos = jnp.broadcast_to(pos_ref[...], (EXTRA, tok))
    row = lax.broadcasted_iota(jnp.int32, (EXTRA, tok), 0)
    high = lax.shift_right_logical(pos, 6)
    both = jnp.where(row == 0, high, jnp.where(row == 1, pos - high * 64, 0))
    rows_ref[...] = both.astype(F32).astype(BF16)
    send_off(rows_ref, lat_msg.at[pl.ds(width, EXTRA), :])
    send_off(rows_ref, q_msg.at[pl.ds(heads * (width + HEAD_DIM), EXTRA), :])
    started[4].wait()
    send_off(lat_ref, lat_msg.at[pl.ds(0, width), :])
    for h in range(heads):
        started[5 + h].wait()
        send_off(q_ref.at[h], q_msg.at[pl.ds(h * width, width), :])
    delta_ref[...] = jnp.zeros_like(delta_ref)
    started[2].wait()
    attn = [attn_ref[:, h, :].T for h in range(heads)]
    for h in range(heads):
        term[h] = mm_t(attn[h], og_t_ref[h])
    step = lat // GROUP
    me = lax.rem(idx_ref[0], GROUP)
    for k in range(GROUP):
        at = pl.multiple_of(jnp.bitwise_xor(me, k) * step, step)
        target = send_ref if k % 2 else keep_ref
        target[k // 2 * heads : (k // 2 + 1) * heads] = term[:, pl.ds(at, step), :].astype(BF16)
    send_off(send_ref, send_hbm)
    send_off(keep_ref, keep_hbm)
    started[3].wait()
    for h in range(heads):
        g = mm(wuv_ref[h], og_t_ref[h]).astype(BF16).astype(F32)
        delta_ref[h : h + 1, :] = jnp.sum(g * attn[h].astype(F32), axis=0, keepdims=True)
    send_off(delta_ref, delta_hbm)
    for copy in started[5 + heads :]:
        copy.wait()


def hold_kernel(*refs):
    half = len(refs) // 2
    for source, target in zip(refs[:half], refs[half:]):
        target[...] = source[...]


def score_kernel(factor, nkey, width, heads, last, *refs):
    lat_refs, refs = refs[:nkey], refs[nkey:]
    tok = lat_refs[0].shape[1]
    rows = heads * tok
    if last:
        q_all_ref, near_ref, delta_ref, s_ref, k_ref, stat_ref, kt = refs
    else:
        q_refs, refs = refs[:GROUP], refs[GROUP:]
        s_ref, k_ref, stat_ref, q_all_ref, kt = refs
        for j in range(GROUP):
            for h in range(heads):
                cols = slice(j * rows + h * tok, j * rows + (h + 1) * tok)
                q_all_ref[:width, cols] = q_refs[j][h * width : (h + 1) * width, :]
                q_all_ref[width : width + EXTRA, cols] = q_refs[j][q_refs[j].shape[0] - EXTRA :, :]
        spare = q_all_ref.shape[0] - width - EXTRA
        q_all_ref[width + EXTRA :, :] = jnp.zeros((spare, GROUP * rows), BF16)
    wide = kt.shape[0]
    for a in range(nkey):
        kt[: width + EXTRA, a * tok : (a + 1) * tok] = lat_refs[a][...]
    kt[width + EXTRA :, :] = jnp.zeros((wide - width - EXTRA, nkey * tok), BF16)
    keys = kt[...].T
    pos = keys[:, wide - 128 :].astype(F32)
    at = width - (wide - 128)
    key_pos = pos[:, at : at + 1] * 64.0 + pos[:, at + 1 : at + 2]
    lane = lax.broadcasted_iota(jnp.int32, keys.shape, 1)
    k_ref[...] = jnp.where(lane < width, keys, jnp.zeros_like(keys))
    stat_ref[...] = jnp.zeros_like(stat_ref)
    if last:
        stat_ref[GROUP * heads : GROUP * heads + heads, :] = delta_ref[:heads, :]
    for j in range(GROUP):
        cols = slice(j * rows, (j + 1) * rows)
        qp = q_all_ref[width : width + EXTRA, cols].astype(F32)
        row_pos = qp[0:1, :] * 64.0 + qp[1:2, :]
        s = mm(k_ref[...], q_all_ref[:, cols]) * factor
        s = jnp.where(key_pos <= row_pos, s, -1e30)
        s_ref[:, cols] = s
        top = jnp.max(s, axis=0, keepdims=True)
        lse = top + jnp.log(jnp.sum(jnp.exp(s - top), axis=0, keepdims=True))
        for h in range(heads):
            at = j * heads + h
            part = lse[:, h * tok : (h + 1) * tok]
            if last:
                near = near_ref[at : at + 1, :]
                most = jnp.maximum(part, near)
                part = most + jnp.log(jnp.exp(part - most) + jnp.exp(near - most))
            stat_ref[at : at + 1, :] = part


def context_kernel(width, heads, *refs):
    q_refs = refs[:GROUP]
    wuv_ref, near_k_ref, last_k_ref, g_ref, near_gp_ref, last_gp_ref = refs[GROUP:]
    lat, all_rows = g_ref.shape
    tok = q_refs[0].shape[1]
    rows = heads * tok
    for j in range(GROUP):
        for h in range(heads):
            at = heads * width + h * HEAD_DIM
            og = q_refs[j][at : at + HEAD_DIM, :]
            col = j * rows + h * tok
            g_ref[:, col : col + tok] = mm(wuv_ref[h], og).astype(BF16)
        cols = slice(j * rows, (j + 1) * rows)
        near_gp_ref[:, cols] = mm(near_k_ref[:, :lat], g_ref[:, cols])
        last_gp_ref[:, cols] = mm(last_k_ref[:, :lat], g_ref[:, cols])


def pair_kernel(heads, keys, *refs):
    stats, (s_ref, gp_ref, gs_ref, p_ref) = refs[:GROUP], refs[GROUP : GROUP + 4]
    all_rows = s_ref.shape[1]
    rows = all_rows // GROUP
    for j in range(GROUP):
        cols = slice(j * rows, (j + 1) * rows)
        lse_parts = []
        for k in range(GROUP):
            at = (j ^ k) * heads
            lse_parts.append(
                jnp.concatenate([stats[k][at + h : at + h + 1, :] for h in range(heads)], axis=1)
            )
        top = functools.reduce(jnp.maximum, lse_parts)
        lse = top + jnp.log(sum(jnp.exp(part - top) for part in lse_parts))
        at = GROUP * heads
        delta = jnp.concatenate([stats[j][at + h : at + h + 1, :] for h in range(heads)], axis=1)
        p = jnp.exp(s_ref[keys, cols] - lse)
        gs_ref[:, cols] = (p * (gp_ref[keys, cols] - delta)).astype(BF16)
        p_ref[:, cols] = p.astype(BF16)


def partial_kernel(factor, places, width, g_ref, q_all_ref, gs_ref, p_ref, *part_refs):
    lat = g_ref.shape[0]
    for a, at in enumerate(places):
        along = mm_t(q_all_ref[:width, :], gs_ref[at, :]) * factor
        value = mm_t(g_ref[...], p_ref[at, :])
        part_refs[a][:lat, :] = (along[:lat] + value).astype(BF16)
        part_refs[a][lat:, :] = along[lat:].astype(BF16)


def block_kernel(factor, keys, width, heads, *refs):
    stats, refs = refs[:GROUP], refs[GROUP:]
    s_ref, gp_ref, g_ref, q_all_ref, part_ref, gs_ref, p_ref = refs
    pair_kernel(heads, keys, *stats, s_ref, gp_ref, gs_ref, p_ref)
    partial_kernel(factor, [slice(None)], width, g_ref, q_all_ref, gs_ref, p_ref, part_ref)


def query_kernel(factor, nkey, width, heads, *refs):
    stats, refs = refs[:GROUP], refs[GROUP:]
    (s_ref, gp_ref, last_gs_ref), refs = refs[:3], refs[3:]
    lat_refs, refs = refs[:nkey], refs[nkey:]
    gq_refs, far_refs, (gs_ref, p_ref, kt) = refs[: GROUP - 1], refs[GROUP - 1 : -3], refs[-3:]
    tok = lat_refs[0].shape[1]
    keys = s_ref.shape[0]
    rows = heads * tok
    for a in range(nkey):
        kt[:, a * tok : (a + 1) * tok] = lat_refs[a][:width, :]
    pair_kernel(heads, slice(None), *stats, s_ref, gp_ref, gs_ref, p_ref)
    for j in range(GROUP):
        cols = slice(j * rows, (j + 1) * rows)
        gq = mm(kt[:, :keys], gs_ref[:, cols]) + mm(kt[:, keys:], last_gs_ref[:, cols])
        gq = (gq * factor).astype(BF16)
        for h in range(heads):
            part = gq[:, h * tok : (h + 1) * tok]
            if j < GROUP - 1:
                gq_refs[j][h] = part
            else:
                for c, at, here in segments(h, width, far_refs):
                    far_refs[c][here, :] = part[at]


def segments(head, width, pieces):
    cut = pieces[0].shape[0]
    found = []
    for c in range(len(pieces)):
        low, high = max(head * width, c * cut), min((head + 1) * width, (c + 1) * cut)
        if low < high:
            at = slice(low - head * width, high - head * width)
            found.append((c, at, slice(low - c * cut, high - c * cut)))
    return found


def join_kernel(whole_ref, *refs):
    pieces, out_ref = refs[:-1], refs[-1]
    heads, width, _ = out_ref.shape
    for h in range(heads):
        for c, at, here in segments(h, width, pieces):
            both = whole_ref[h, at, :].astype(F32) + pieces[c][here, :].astype(F32)
            out_ref[h, at, :] = both.astype(BF16)


def sum_kernel(*refs):
    refs[-1][...] = sum(ref[...].astype(F32) for ref in refs[:-1]).astype(BF16)


def spread_kernel(scale, idx_ref, *refs):
    chunks, out_ref = refs[:GROUP], refs[GROUP]
    step = chunks[0].shape[1]
    me = lax.rem(idx_ref[0], GROUP)
    for k in range(GROUP):
        at = pl.multiple_of(jnp.bitwise_xor(me, k) * step, step)
        out_ref[:, pl.ds(at, step), :] = chunks[k][...].astype(F32) * scale


def body(n_ctx, n_dp, positions, queries, latent, out_grad, attn_out, wuv):
    tok, heads, width = queries.shape[1:]
    lat = attn_out.shape[3]
    lines = n_ctx // GROUP
    line_bits = (lines - 1).bit_length()
    rows = heads * tok
    all_rows = GROUP * rows
    keys = lines * tok
    wide = -(-(width + EXTRA) // 128) * 128
    factor = (HEAD_DIM + ROPE) ** (-0.5)

    def swap(x, mask, axis="ctx", size=n_ctx):
        return lax.ppermute(x, axis, [(i, i ^ mask) for i in range(size)])

    def after(x, *done):
        return lax.optimization_barrier((x, done))[0]

    idx = lax.axis_index("ctx").reshape(1)
    step = lat // GROUP
    lat_msg, q_msg, delta, keep, send = call(
        pack_kernel,
        "pack",
        [
            ((width + EXTRA, tok), BF16),
            ((heads * (width + HEAD_DIM) + EXTRA, tok), BF16),
            ((8, tok), F32),
            ((2 * heads, step, HEAD_DIM), BF16),
            ((2 * heads, step, HEAD_DIM), BF16),
        ],
        [
            idx,
            positions,
            jnp.transpose(queries[0], (1, 2, 0)),
            out_grad[0],
            latent[0].T,
            attn_out[0],
            wuv,
        ],
        [
            ((1, tok), jnp.int32),
            (out_grad.shape[1:], BF16),
            (attn_out.shape[1:], BF16),
            (wuv.shape, BF16),
            ((heads, lat, HEAD_DIM), F32),
            ((EXTRA, tok), BF16),
            ((heads, HEAD_DIM, tok), BF16),
            ((8, tok), F32),
            ((2 * heads, step, HEAD_DIM), BF16),
            ((2 * heads, step, HEAD_DIM), BF16),
            ((width, tok), BF16),
            ((heads, width, tok), BF16),
        ],
        smem=(0,),
        hbm=(1, 2, 3, 4, 5, 6),
        copies=11 + 3 * heads,
        out=pltpu.HBM,
        limit=PACK_LIMIT,
    )

    def add(a, b):
        return (a.astype(F32) + b.astype(F32)).astype(BF16)

    dp_hops = [(1 << bit, "dp", n_dp) for bit in range((n_dp - 1).bit_length())]
    line_hops = [(GROUP << bit,) for bit in range(line_bits)]

    q_across = swap(q_msg, 2)
    q_core = swap(q_msg, 1)
    pair = add(keep, swap(send, 1))
    got_pair = swap(pair, *dp_hops[0])
    firsts = [swap(after(lat_msg, q_core) if bit + 1 < line_bits else lat_msg, GROUP << bit) for bit in range(line_bits)]
    own = call(
        hold_kernel,
        "hold_own",
        [(lat_msg.shape, BF16), (q_msg.shape, BF16), (delta.shape, F32)],
        [lat_msg, q_msg, delta],
        share=0,
    )
    q_core, q_across, firsts, got_pair, own = lax.optimization_barrier(
        (q_core, q_across, firsts, got_pair, own)
    )
    held = {0: lat_msg}
    for bit in reversed(range(line_bits)):
        held.update({m | 1 << bit: swap(x, GROUP << bit) for m, x in held.items() if m})
        held[1 << bit] = firsts[bit]
    pair = add(pair, got_pair)
    for step_hop in dp_hops[1:]:
        pair = add(pair, swap(pair, *step_hop))
    lats = [held[m] for m in range(lines)]
    q_far = swap(q_across, 1)
    got_own = swap(pair[heads:], 2)
    lat_own, q_own, delta = own
    lats[0] = lat_own
    qs = [q_own, q_core, q_across, q_far]

    most = lines - 1
    keys = most * tok
    score_flops = 2 * tok * all_rows * wide
    near_s, near_k, near_stat, q_all = call(
        functools.partial(score_kernel, factor, most, width, heads, False),
        "near_scores",
        [((keys, all_rows), F32), ((keys, wide), BF16), ((EXTRA, tok), F32), ((wide, all_rows), BF16)],
        lats[:most] + qs,
        [((wide, keys), BF16)],
        flops=most * score_flops,
        share=0,
    )
    mine = add(pair[:heads], after(got_own, near_stat))
    near = swap(mine, *line_hops[0])
    last_s, last_k, stat = call(
        functools.partial(score_kernel, factor, 1, width, heads, True),
        "last_scores",
        [((tok, all_rows), F32), ((tok, wide), BF16), ((EXTRA, tok), F32)],
        [lats[most], q_all, near_stat, delta],
        [((wide, tok), BF16)],
        flops=score_flops,
    )
    stats = [stat] + [swap(stat, k) for k in range(1, GROUP)]
    g, near_gp, last_gp = call(
        functools.partial(context_kernel, width, heads),
        "context",
        [((lat, all_rows), BF16), ((keys, all_rows), F32), ((tok, all_rows), F32)],
        qs + [wuv, near_k, last_k],
        flops=2 * lines * tok * all_rows * lat + 2 * all_rows * lat * HEAD_DIM,
        share=3,
    )
    mine = add(mine, after(near, stat))
    for step_hop in line_hops[1:-1]:
        mine = add(mine, swap(mine, *step_hop))
    near = swap(mine, *line_hops[-1])
    def block(name, keys_at, s, gp, keep):
        part, pairs = ((width, tok), BF16), ((tok, all_rows), BF16)
        return call(
            functools.partial(block_kernel, factor, keys_at, width, heads),
            name,
            [part, pairs] if keep else [part],
            stats + [s, gp, g, q_all],
            [pairs] if keep else [pairs] * 2,
            flops=2 * tok * all_rows * (width + lat),
        )

    last_part, last_gs = block("last_gradients", slice(None), last_s, last_gp, True)
    last_got = swap(last_part, GROUP)
    (next_part,) = block("next_gradients", slice(tok, 2 * tok), near_s, after(near_gp, last_part), False)
    next_got = swap(next_part, GROUP)
    mine = add(mine, near)
    gq_shape, cut_shape = (heads, width, tok), (heads * width // CUTS, tok)
    gq_own, gq_core, gq_across, *far_cuts, near_gs, near_p = call(
        functools.partial(query_kernel, factor, lines, width, heads),
        "query_gradients",
        [(gq_shape, BF16)] * 3 + [(cut_shape, BF16)] * CUTS + [((keys, all_rows), BF16)] * 2,
        stats + [near_s, near_gp, after(last_gs, mine)] + lats,
        [((width, lines * tok), BF16)],
        flops=2 * lines * tok * all_rows * width,
        share=0,
    )
    across = swap(mine, 2)
    far_cuts = [swap(cut, 1) for cut in far_cuts]
    (gq_sum,) = call(join_kernel, "join", [(gq_shape, BF16)], [after(gq_across, across)] + far_cuts)
    gq_last = swap(gq_sum, 2)
    gq_core = swap(after(gq_core, gq_sum), 1)
    def partials(name, blocks, gs, p, share=1):
        rows = [slice(m * tok, (m + 1) * tok) for m in blocks]
        made = call(
            functools.partial(partial_kernel, factor, rows, width),
            name,
            [((width, tok), BF16)] * len(blocks),
            [g, q_all, gs, p],
            flops=2 * len(blocks) * tok * all_rows * (width + lat),
            share=share,
        )
        return dict(zip(blocks, made))

    middle = lines // 2
    made = partials("middle_gradients", [middle], near_gs, near_p, 3)
    made.update(partials("near_gradients", [m for m in range(most) if m not in (1, middle)], near_gs, after(near_p, *far_cuts)))
    made[1] = next_part
    near_parts = [made[m] for m in range(most)]
    parts = list(near_parts) + [last_part]
    kept = [parts[0]]
    for bit in range(line_bits):
        for m in range(3 << bit, lines, 2 << bit):
            got = last_got if m == most and bit == 0 else swap(parts[m], GROUP << bit)
            parts[m ^ 1 << bit] = add(parts[m ^ 1 << bit], got)
    mine_two = jnp.concatenate([mine, across], axis=0)
    other_two = swap(mine_two, 1)
    pieces = [mine_two[:heads], other_two[:heads], mine_two[heads:], other_two[heads:]]
    kept += [swap(parts[1 << bit], GROUP << bit) for bit in range(1, line_bits)] + [next_got]
    scale = 1.0 / math.sqrt(tok * n_ctx * n_dp)
    (grad_w,) = call(
        functools.partial(spread_kernel, scale),
        "spread",
        [((heads, lat, HEAD_DIM), F32)],
        [idx] + pieces,
        smem=(0,),
    )
    kept[0] = after(kept[0], grad_w)
    (grad_lat,) = call(sum_kernel, "latent_sum", [((width, tok), BF16)], kept, flops=3 * 10**9)
    gq_pieces = [gq_own, gq_core, after(gq_last, grad_lat)]
    (grad_q,) = call(sum_kernel, "query_sum", [((heads, width, tok), BF16)], gq_pieces)
    return (jnp.transpose(grad_q, (2, 0, 1))[None], grad_lat.T[None], grad_w)


def solution(mesh):
    placed = (
        P("dp", "ctx"),
        P("dp", "ctx", None, None),
        P("dp", "ctx", None),
        P("dp", "ctx", None, None),
        P("dp", "ctx", None, None),
        P(),
    )
    return jax.shard_map(
        functools.partial(body, mesh.shape["ctx"], mesh.shape["dp"]),
        mesh=mesh,
        in_specs=placed,
        out_specs=(P("dp", "ctx", None, None), P("dp", "ctx", None), P()),
        check_vma=False,
    )
```

```python
import functools
import math

import jax
import jax.numpy as jnp
from jax import lax
from jax.experimental import pallas as pl
from jax.experimental.pallas import tpu as pltpu
from jax.sharding import PartitionSpec as P

ROPE = 64
HEAD_DIM = 128
GROUP = 4
EXTRA = 16
CUTS = 2
PACK_LIMIT = 63 << 20
F32 = jnp.float32
BF16 = jnp.bfloat16


def mm(a, b):
    return jnp.dot(a, b, preferred_element_type=F32)


def mm_t(a, b):
    return lax.dot_general(a, b, (((1,), (1,)), ((), ())), preferred_element_type=F32)


def size_of(shape, dtype):
    return math.prod(shape) * jnp.dtype(dtype).itemsize


def call(kernel, name, outs, args, scratch=(), flops=0, smem=(), hbm=(), copies=0, limit=None, share=1, out=pltpu.VMEM):
    def place(i):
        return pltpu.SMEM if i in smem else pltpu.HBM if i in hbm else pltpu.VMEM

    moved = sum(size_of(a.shape, a.dtype) for a in args) + sum(size_of(*o) for o in outs)
    held = moved + sum(size_of(*s) for s in scratch)
    semaphores = [pltpu.SemaphoreType.DMA((copies,))] if copies else []
    return pl.pallas_call(
        kernel,
        out_shape=[jax.ShapeDtypeStruct(s, d) for s, d in outs],
        in_specs=[pl.BlockSpec(memory_space=place(i)) for i in range(len(args))],
        out_specs=[pl.BlockSpec(memory_space=out) for _ in outs],
        scratch_shapes=[pltpu.VMEM(s, d) for s, d in scratch] + semaphores,
        compiler_params=pltpu.CompilerParams(vmem_limit_bytes=limit or int(1.2 * held) + (8 << 20)),
        cost_estimate=pl.CostEstimate(flops=flops * share, bytes_accessed=moved * share, transcendentals=0),
        name=name,
    )(*args)


def fetch(pairs, sems):
    copies = [pltpu.make_async_copy(src, dst, sems.at[i]) for i, (src, dst) in enumerate(pairs)]
    for copy in copies:
        copy.start()
    return copies


def pack_kernel(
    idx_ref, pos_hbm, q_hbm, og_hbm, lat_hbm, attn_hbm, wuv_hbm,
    lat_msg, q_msg, delta_hbm, keep_hbm, send_hbm,
    pos_ref, og_ref, attn_ref, wuv_ref, term, rows_ref, og_t_ref, delta_ref, keep_ref, send_ref,
    lat_ref, q_ref, sems,
):
    heads, width, tok = q_hbm.shape
    _, lat, _ = wuv_ref.shape
    started = []

    def send_off(src, dst):
        copy = pltpu.make_async_copy(src, dst, sems.at[len(started)])
        copy.start()
        started.append(copy)

    send_off(og_hbm, og_ref)
    send_off(pos_hbm, pos_ref)
    send_off(attn_hbm, attn_ref)
    send_off(wuv_hbm, wuv_ref)
    send_off(lat_hbm, lat_ref)
    for h in range(heads):
        send_off(q_hbm.at[h], q_ref.at[h])
    started[0].wait()
    for h in range(heads):
        og_t_ref[h] = og_ref[:, h, :].T
        send_off(og_t_ref.at[h], q_msg.at[pl.ds(heads * width + h * HEAD_DIM, HEAD_DIM), :])
    started[1].wait()
    pos = jnp.broadcast_to(pos_ref[...], (EXTRA, tok))
    row = lax.broadcasted_iota(jnp.int32, (EXTRA, tok), 0)
    high = lax.shift_right_logical(pos, 6)
    both = jnp.where(row == 0, high, jnp.where(row == 1, pos - high * 64, 0))
    rows_ref[...] = both.astype(F32).astype(BF16)
    send_off(rows_ref, lat_msg.at[pl.ds(width, EXTRA), :])
    send_off(rows_ref, q_msg.at[pl.ds(heads * (width + HEAD_DIM), EXTRA), :])
    started[4].wait()
    send_off(lat_ref, lat_msg.at[pl.ds(0, width), :])
    for h in range(heads):
        started[5 + h].wait()
        send_off(q_ref.at[h], q_msg.at[pl.ds(h * width, width), :])
    delta_ref[...] = jnp.zeros_like(delta_ref)
    started[2].wait()
    attn = [attn_ref[:, h, :].T for h in range(heads)]
    for h in range(heads):
        term[h] = mm_t(attn[h], og_t_ref[h])
    step = lat // GROUP
    me = lax.rem(idx_ref[0], GROUP)
    for k in range(GROUP):
        at = pl.multiple_of(jnp.bitwise_xor(me, k) * step, step)
        target = send_ref if k % 2 else keep_ref
        target[k // 2 * heads : (k // 2 + 1) * heads] = term[:, pl.ds(at, step), :].astype(BF16)
    send_off(send_ref, send_hbm)
    send_off(keep_ref, keep_hbm)
    started[3].wait()
    for h in range(heads):
        g = mm(wuv_ref[h], og_t_ref[h]).astype(BF16).astype(F32)
        delta_ref[h : h + 1, :] = jnp.sum(g * attn[h].astype(F32), axis=0, keepdims=True)
    send_off(delta_ref, delta_hbm)
    for copy in started[5 + heads :]:
        copy.wait()


def hold_kernel(*refs):
    half = len(refs) // 2
    for source, target in zip(refs[:half], refs[half:]):
        target[...] = source[...]


def score_kernel(factor, nkey, width, heads, last, *refs):
    lat_refs, refs = refs[:nkey], refs[nkey:]
    tok = lat_refs[0].shape[1]
    rows = heads * tok
    if last:
        q_all_ref, near_ref, delta_ref, s_ref, k_ref, stat_ref, kt = refs
    else:
        q_refs, refs = refs[:GROUP], refs[GROUP:]
        s_ref, k_ref, stat_ref, q_all_ref, kt = refs
        for j in range(GROUP):
            for h in range(heads):
                cols = slice(j * rows + h * tok, j * rows + (h + 1) * tok)
                q_all_ref[:width, cols] = q_refs[j][h * width : (h + 1) * width, :]
                q_all_ref[width : width + EXTRA, cols] = q_refs[j][q_refs[j].shape[0] - EXTRA :, :]
        spare = q_all_ref.shape[0] - width - EXTRA
        q_all_ref[width + EXTRA :, :] = jnp.zeros((spare, GROUP * rows), BF16)
    wide = kt.shape[0]
    for a in range(nkey):
        kt[: width + EXTRA, a * tok : (a + 1) * tok] = lat_refs[a][...]
    kt[width + EXTRA :, :] = jnp.zeros((wide - width - EXTRA, nkey * tok), BF16)
    keys = kt[...].T
    pos = keys[:, wide - 128 :].astype(F32)
    at = width - (wide - 128)
    key_pos = pos[:, at : at + 1] * 64.0 + pos[:, at + 1 : at + 2]
    lane = lax.broadcasted_iota(jnp.int32, keys.shape, 1)
    k_ref[...] = jnp.where(lane < width, keys, jnp.zeros_like(keys))
    stat_ref[...] = jnp.zeros_like(stat_ref)
    if last:
        stat_ref[GROUP * heads : GROUP * heads + heads, :] = delta_ref[:heads, :]
    for j in range(GROUP):
        cols = slice(j * rows, (j + 1) * rows)
        qp = q_all_ref[width : width + EXTRA, cols].astype(F32)
        row_pos = qp[0:1, :] * 64.0 + qp[1:2, :]
        s = mm(k_ref[...], q_all_ref[:, cols]) * factor
        s = jnp.where(key_pos <= row_pos, s, -1e30)
        s_ref[:, cols] = s
        top = jnp.max(s, axis=0, keepdims=True)
        lse = top + jnp.log(jnp.sum(jnp.exp(s - top), axis=0, keepdims=True))
        for h in range(heads):
            at = j * heads + h
            part = lse[:, h * tok : (h + 1) * tok]
            if last:
                near = near_ref[at : at + 1, :]
                most = jnp.maximum(part, near)
                part = most + jnp.log(jnp.exp(part - most) + jnp.exp(near - most))
            stat_ref[at : at + 1, :] = part


def context_kernel(width, heads, *refs):
    q_refs = refs[:GROUP]
    wuv_ref, near_k_ref, last_k_ref, g_ref, near_gp_ref, last_gp_ref = refs[GROUP:]
    lat, all_rows = g_ref.shape
    tok = q_refs[0].shape[1]
    rows = heads * tok
    for j in range(GROUP):
        for h in range(heads):
            at = heads * width + h * HEAD_DIM
            og = q_refs[j][at : at + HEAD_DIM, :]
            col = j * rows + h * tok
            g_ref[:, col : col + tok] = mm(wuv_ref[h], og).astype(BF16)
        cols = slice(j * rows, (j + 1) * rows)
        near_gp_ref[:, cols] = mm(near_k_ref[:, :lat], g_ref[:, cols])
        last_gp_ref[:, cols] = mm(last_k_ref[:, :lat], g_ref[:, cols])


def pair_kernel(heads, keys, *refs):
    stats, (s_ref, gp_ref, gs_ref, p_ref) = refs[:GROUP], refs[GROUP : GROUP + 4]
    all_rows = s_ref.shape[1]
    rows = all_rows // GROUP
    for j in range(GROUP):
        cols = slice(j * rows, (j + 1) * rows)
        lse_parts = []
        for k in range(GROUP):
            at = (j ^ k) * heads
            lse_parts.append(
                jnp.concatenate([stats[k][at + h : at + h + 1, :] for h in range(heads)], axis=1)
            )
        top = functools.reduce(jnp.maximum, lse_parts)
        lse = top + jnp.log(sum(jnp.exp(part - top) for part in lse_parts))
        at = GROUP * heads
        delta = jnp.concatenate([stats[j][at + h : at + h + 1, :] for h in range(heads)], axis=1)
        p = jnp.exp(s_ref[keys, cols] - lse)
        gs_ref[:, cols] = (p * (gp_ref[keys, cols] - delta)).astype(BF16)
        p_ref[:, cols] = p.astype(BF16)


def partial_kernel(factor, places, width, g_ref, q_all_ref, gs_ref, p_ref, *part_refs):
    lat = g_ref.shape[0]
    for a, at in enumerate(places):
        along = mm_t(q_all_ref[:width, :], gs_ref[at, :]) * factor
        value = mm_t(g_ref[...], p_ref[at, :])
        part_refs[a][:lat, :] = (along[:lat] + value).astype(BF16)
        part_refs[a][lat:, :] = along[lat:].astype(BF16)


def block_kernel(factor, keys, width, heads, *refs):
    stats, refs = refs[:GROUP], refs[GROUP:]
    s_ref, gp_ref, g_ref, q_all_ref, part_ref, gs_ref, p_ref = refs
    pair_kernel(heads, keys, *stats, s_ref, gp_ref, gs_ref, p_ref)
    partial_kernel(factor, [slice(None)], width, g_ref, q_all_ref, gs_ref, p_ref, part_ref)


def query_kernel(factor, nkey, width, heads, *refs):
    stats, refs = refs[:GROUP], refs[GROUP:]
    (s_ref, gp_ref, last_gs_ref), refs = refs[:3], refs[3:]
    lat_refs, refs = refs[:nkey], refs[nkey:]
    gq_refs, far_refs, (gs_ref, p_ref, kt) = refs[: GROUP - 1], refs[GROUP - 1 : -3], refs[-3:]
    tok = lat_refs[0].shape[1]
    keys = s_ref.shape[0]
    rows = heads * tok
    for a in range(nkey):
        kt[:, a * tok : (a + 1) * tok] = lat_refs[a][:width, :]
    pair_kernel(heads, slice(None), *stats, s_ref, gp_ref, gs_ref, p_ref)
    for j in range(GROUP):
        cols = slice(j * rows, (j + 1) * rows)
        gq = mm(kt[:, :keys], gs_ref[:, cols]) + mm(kt[:, keys:], last_gs_ref[:, cols])
        gq = (gq * factor).astype(BF16)
        for h in range(heads):
            part = gq[:, h * tok : (h + 1) * tok]
            if j < GROUP - 1:
                gq_refs[j][h] = part
            else:
                for c, at, here in segments(h, width, far_refs):
                    far_refs[c][here, :] = part[at]


def segments(head, width, pieces):
    cut = pieces[0].shape[0]
    found = []
    for c in range(len(pieces)):
        low, high = max(head * width, c * cut), min((head + 1) * width, (c + 1) * cut)
        if low < high:
            at = slice(low - head * width, high - head * width)
            found.append((c, at, slice(low - c * cut, high - c * cut)))
    return found


def join_kernel(whole_ref, *refs):
    pieces, out_ref = refs[:-1], refs[-1]
    heads, width, _ = out_ref.shape
    for h in range(heads):
        for c, at, here in segments(h, width, pieces):
            both = whole_ref[h, at, :].astype(F32) + pieces[c][here, :].astype(F32)
            out_ref[h, at, :] = both.astype(BF16)


def sum_kernel(*refs):
    refs[-1][...] = sum(ref[...].astype(F32) for ref in refs[:-1])


def finish_kernel(lat_sum_ref, *refs):
    pieces, lat_out_ref, q_out_ref = refs[:-2], refs[-2], refs[-1]
    lat_out_ref[...] = lat_sum_ref[...].astype(BF16)
    q_out_ref[...] = sum(piece[...].astype(F32) for piece in pieces).astype(BF16)


def spread_kernel(scale, idx_ref, *refs):
    chunks, out_ref = refs[:GROUP], refs[GROUP]
    step = chunks[0].shape[1]
    me = lax.rem(idx_ref[0], GROUP)
    for k in range(GROUP):
        at = pl.multiple_of(jnp.bitwise_xor(me, k) * step, step)
        out_ref[:, pl.ds(at, step), :] = chunks[k][...].astype(F32) * scale


def body(n_ctx, n_dp, positions, queries, latent, out_grad, attn_out, wuv):
    tok, heads, width = queries.shape[1:]
    lat = attn_out.shape[3]
    lines = n_ctx // GROUP
    line_bits = (lines - 1).bit_length()
    rows = heads * tok
    all_rows = GROUP * rows
    keys = lines * tok
    wide = -(-(width + EXTRA) // 128) * 128
    factor = (HEAD_DIM + ROPE) ** (-0.5)

    def swap(x, mask, axis="ctx", size=n_ctx):
        return lax.ppermute(x, axis, [(i, i ^ mask) for i in range(size)])

    def after(x, *done):
        return lax.optimization_barrier((x, done))[0]

    idx = lax.axis_index("ctx").reshape(1)
    step = lat // GROUP
    lat_msg, q_msg, delta, keep, send = call(
        pack_kernel,
        "pack",
        [
            ((width + EXTRA, tok), BF16),
            ((heads * (width + HEAD_DIM) + EXTRA, tok), BF16),
            ((8, tok), F32),
            ((2 * heads, step, HEAD_DIM), BF16),
            ((2 * heads, step, HEAD_DIM), BF16),
        ],
        [
            idx,
            positions,
            jnp.transpose(queries[0], (1, 2, 0)),
            out_grad[0],
            latent[0].T,
            attn_out[0],
            wuv,
        ],
        [
            ((1, tok), jnp.int32),
            (out_grad.shape[1:], BF16),
            (attn_out.shape[1:], BF16),
            (wuv.shape, BF16),
            ((heads, lat, HEAD_DIM), F32),
            ((EXTRA, tok), BF16),
            ((heads, HEAD_DIM, tok), BF16),
            ((8, tok), F32),
            ((2 * heads, step, HEAD_DIM), BF16),
            ((2 * heads, step, HEAD_DIM), BF16),
            ((width, tok), BF16),
            ((heads, width, tok), BF16),
        ],
        smem=(0,),
        hbm=(1, 2, 3, 4, 5, 6),
        copies=11 + 3 * heads,
        out=pltpu.HBM,
        limit=PACK_LIMIT,
    )

    def add(a, b):
        return (a.astype(F32) + b.astype(F32)).astype(BF16)

    dp_hops = [(1 << bit, "dp", n_dp) for bit in range((n_dp - 1).bit_length())]
    line_hops = [(GROUP << bit,) for bit in range(line_bits)]

    q_across = swap(q_msg, 2)
    q_core = swap(q_msg, 1)
    pair = add(keep, swap(send, 1))
    got_pair = swap(pair, *dp_hops[0])
    firsts = [swap(after(lat_msg, q_core) if bit + 1 < line_bits else lat_msg, GROUP << bit) for bit in range(line_bits)]
    own = call(
        hold_kernel,
        "hold_own",
        [(lat_msg.shape, BF16), (q_msg.shape, BF16), (delta.shape, F32)],
        [lat_msg, q_msg, delta],
        share=0,
    )
    q_core, q_across, firsts, got_pair, own = lax.optimization_barrier(
        (q_core, q_across, firsts, got_pair, own)
    )
    held = {0: lat_msg}
    for bit in reversed(range(line_bits)):
        held.update({m | 1 << bit: swap(x, GROUP << bit) for m, x in held.items() if m})
        held[1 << bit] = firsts[bit]
    pair = add(pair, got_pair)
    for step_hop in dp_hops[1:]:
        pair = add(pair, swap(pair, *step_hop))
    lats = [held[m] for m in range(lines)]
    q_far = swap(q_across, 1)
    got_own = swap(pair[heads:], 2)
    lat_own, q_own, delta = own
    lats[0] = lat_own
    qs = [q_own, q_core, q_across, q_far]

    most = lines - 1
    keys = most * tok
    score_flops = 2 * tok * all_rows * wide
    near_s, near_k, near_stat, q_all = call(
        functools.partial(score_kernel, factor, most, width, heads, False),
        "near_scores",
        [((keys, all_rows), F32), ((keys, wide), BF16), ((EXTRA, tok), F32), ((wide, all_rows), BF16)],
        lats[:most] + qs,
        [((wide, keys), BF16)],
        flops=most * score_flops,
        share=0,
    )
    mine = add(pair[:heads], after(got_own, near_stat))
    near = swap(mine, *line_hops[0])
    last_s, last_k, stat = call(
        functools.partial(score_kernel, factor, 1, width, heads, True),
        "last_scores",
        [((tok, all_rows), F32), ((tok, wide), BF16), ((EXTRA, tok), F32)],
        [lats[most], q_all, near_stat, delta],
        [((wide, tok), BF16)],
        flops=score_flops,
    )
    stats = [stat] + [swap(stat, k) for k in range(1, GROUP)]
    g, near_gp, last_gp = call(
        functools.partial(context_kernel, width, heads),
        "context",
        [((lat, all_rows), BF16), ((keys, all_rows), F32), ((tok, all_rows), F32)],
        qs + [wuv, near_k, last_k],
        flops=2 * lines * tok * all_rows * lat + 2 * all_rows * lat * HEAD_DIM,
        share=3,
    )
    mine = add(mine, after(near, stat))
    for step_hop in line_hops[1:-1]:
        mine = add(mine, swap(mine, *step_hop))
    near = swap(mine, *line_hops[-1])
    def block(name, keys_at, s, gp, keep):
        part, pairs = ((width, tok), BF16), ((tok, all_rows), BF16)
        return call(
            functools.partial(block_kernel, factor, keys_at, width, heads),
            name,
            [part, pairs] if keep else [part],
            stats + [s, gp, g, q_all],
            [pairs] if keep else [pairs] * 2,
            flops=2 * tok * all_rows * (width + lat),
        )

    last_part, last_gs = block("last_gradients", slice(None), last_s, last_gp, True)
    last_got = swap(last_part, GROUP)
    (next_part,) = block("next_gradients", slice(tok, 2 * tok), near_s, after(near_gp, last_part), False)
    next_got = swap(next_part, GROUP)
    mine = add(mine, near)
    gq_shape, cut_shape = (heads, width, tok), (heads * width // CUTS, tok)
    gq_own, gq_core, gq_across, *far_cuts, near_gs, near_p = call(
        functools.partial(query_kernel, factor, lines, width, heads),
        "query_gradients",
        [(gq_shape, BF16)] * 3 + [(cut_shape, BF16)] * CUTS + [((keys, all_rows), BF16)] * 2,
        stats + [near_s, near_gp, after(last_gs, mine)] + lats,
        [((width, lines * tok), BF16)],
        flops=2 * lines * tok * all_rows * width,
        share=0,
    )
    across = swap(mine, 2)
    far_cuts = [swap(cut, 1) for cut in far_cuts]
    (gq_sum,) = call(join_kernel, "join", [(gq_shape, BF16)], [after(gq_across, across)] + far_cuts)
    gq_last = swap(gq_sum, 2)
    gq_core = swap(after(gq_core, gq_sum), 1)
    def partials(name, blocks, gs, p, share=1):
        rows = [slice(m * tok, (m + 1) * tok) for m in blocks]
        made = call(
            functools.partial(partial_kernel, factor, rows, width),
            name,
            [((width, tok), BF16)] * len(blocks),
            [g, q_all, gs, p],
            flops=2 * len(blocks) * tok * all_rows * (width + lat),
            share=share,
        )
        return dict(zip(blocks, made))

    middle = lines // 2
    made = partials("middle_gradients", [middle], near_gs, near_p, 3)
    made.update(partials("near_gradients", [m for m in range(most) if m not in (1, middle)], near_gs, after(near_p, *far_cuts)))
    made[1] = next_part
    near_parts = [made[m] for m in range(most)]
    parts = list(near_parts) + [last_part]
    kept = [parts[0]]
    for bit in range(line_bits):
        for m in range(3 << bit, lines, 2 << bit):
            got = last_got if m == most and bit == 0 else swap(parts[m], GROUP << bit)
            parts[m ^ 1 << bit] = add(parts[m ^ 1 << bit], got)
    mine_two = jnp.concatenate([mine, across], axis=0)
    other_two = swap(mine_two, 1)
    pieces = [mine_two[:heads], other_two[:heads], mine_two[heads:], other_two[heads:]]
    kept += [swap(parts[1 << bit], GROUP << bit) for bit in range(1, line_bits)] + [next_got]
    scale = 1.0 / math.sqrt(tok * n_ctx * n_dp)
    (grad_w,) = call(
        functools.partial(spread_kernel, scale),
        "spread",
        [((heads, lat, HEAD_DIM), F32)],
        [idx] + pieces,
        smem=(0,),
    )
    kept[0] = after(kept[0], grad_w)
    (lat_sum,) = call(sum_kernel, "latent_sum", [((width, tok), F32)], kept, flops=3 * 10**9)
    grad_lat, grad_q = call(
        finish_kernel,
        "finish",
        [((width, tok), BF16), ((heads, width, tok), BF16)],
        [lat_sum, gq_own, gq_core, gq_last],
    )
    return (jnp.transpose(grad_q, (2, 0, 1))[None], grad_lat.T[None], grad_w)


def solution(mesh):
    placed = (
        P("dp", "ctx"),
        P("dp", "ctx", None, None),
        P("dp", "ctx", None),
        P("dp", "ctx", None, None),
        P("dp", "ctx", None, None),
        P(),
    )
    return jax.shard_map(
        functools.partial(body, mesh.shape["ctx"], mesh.shape["dp"]),
        mesh=mesh,
        in_specs=placed,
        out_specs=(P("dp", "ctx", None, None), P("dp", "ctx", None), P()),
        check_vma=False,
    )
```

```python
import functools
import math

import jax
import jax.numpy as jnp
from jax import lax
from jax.experimental import pallas as pl
from jax.experimental.pallas import tpu as pltpu
from jax.sharding import PartitionSpec as P

ROPE = 64
HEAD_DIM = 128
GROUP = 4
EXTRA = 16
CUTS = 2
PACK_LIMIT = 63 << 20
F32 = jnp.float32
BF16 = jnp.bfloat16


def mm(a, b):
    return jnp.dot(a, b, preferred_element_type=F32)


def mm_t(a, b):
    return lax.dot_general(a, b, (((1,), (1,)), ((), ())), preferred_element_type=F32)


def size_of(shape, dtype):
    return math.prod(shape) * jnp.dtype(dtype).itemsize


def call(kernel, name, outs, args, scratch=(), flops=0, smem=(), hbm=(), copies=0, limit=None, share=1, out=pltpu.VMEM):
    def place(i):
        return pltpu.SMEM if i in smem else pltpu.HBM if i in hbm else pltpu.VMEM

    moved = sum(size_of(a.shape, a.dtype) for a in args) + sum(size_of(*o) for o in outs)
    held = moved + sum(size_of(*s) for s in scratch)
    semaphores = [pltpu.SemaphoreType.DMA((copies,))] if copies else []
    return pl.pallas_call(
        kernel,
        out_shape=[jax.ShapeDtypeStruct(s, d) for s, d in outs],
        in_specs=[pl.BlockSpec(memory_space=place(i)) for i in range(len(args))],
        out_specs=[pl.BlockSpec(memory_space=out) for _ in outs],
        scratch_shapes=[pltpu.VMEM(s, d) for s, d in scratch] + semaphores,
        compiler_params=pltpu.CompilerParams(vmem_limit_bytes=limit or int(1.2 * held) + (8 << 20)),
        cost_estimate=pl.CostEstimate(flops=flops * share, bytes_accessed=moved * share, transcendentals=0),
        name=name,
    )(*args)


def fetch(pairs, sems):
    copies = [pltpu.make_async_copy(src, dst, sems.at[i]) for i, (src, dst) in enumerate(pairs)]
    for copy in copies:
        copy.start()
    return copies


def pack_kernel(
    idx_ref, pos_hbm, q_hbm, og_hbm, lat_hbm, attn_hbm, wuv_hbm,
    lat_msg, q_msg, delta_hbm, keep_hbm, send_hbm,
    pos_ref, og_ref, attn_ref, wuv_ref, term, rows_ref, og_t_ref, delta_ref, keep_ref, send_ref,
    lat_ref, q_ref, sems,
):
    heads, width, tok = q_hbm.shape
    _, lat, _ = wuv_ref.shape
    started = []

    def send_off(src, dst):
        copy = pltpu.make_async_copy(src, dst, sems.at[len(started)])
        copy.start()
        started.append(copy)

    send_off(og_hbm, og_ref)
    send_off(pos_hbm, pos_ref)
    send_off(attn_hbm, attn_ref)
    send_off(wuv_hbm, wuv_ref)
    send_off(lat_hbm, lat_ref)
    for h in range(heads):
        send_off(q_hbm.at[h], q_ref.at[h])
    started[0].wait()
    for h in range(heads):
        og_t_ref[h] = og_ref[:, h, :].T
        send_off(og_t_ref.at[h], q_msg.at[pl.ds(heads * width + h * HEAD_DIM, HEAD_DIM), :])
    started[1].wait()
    pos = jnp.broadcast_to(pos_ref[...], (EXTRA, tok))
    row = lax.broadcasted_iota(jnp.int32, (EXTRA, tok), 0)
    high = lax.shift_right_logical(pos, 6)
    both = jnp.where(row == 0, high, jnp.where(row == 1, pos - high * 64, 0))
    rows_ref[...] = both.astype(F32).astype(BF16)
    send_off(rows_ref, lat_msg.at[pl.ds(width, EXTRA), :])
    send_off(rows_ref, q_msg.at[pl.ds(heads * (width + HEAD_DIM), EXTRA), :])
    delta_ref[...] = jnp.zeros_like(delta_ref)
    started[2].wait()
    attn = [attn_ref[:, h, :].T for h in range(heads)]
    for h in range(heads):
        term[h] = mm_t(attn[h], og_t_ref[h])
    step = lat // GROUP
    me = lax.rem(idx_ref[0], GROUP)
    for k in range(GROUP):
        at = pl.multiple_of(jnp.bitwise_xor(me, k) * step, step)
        target = send_ref if k % 2 else keep_ref
        target[k // 2 * heads : (k // 2 + 1) * heads] = term[:, pl.ds(at, step), :].astype(BF16)
    send_off(send_ref, send_hbm)
    send_off(keep_ref, keep_hbm)
    started[4].wait()
    send_off(lat_ref, lat_msg.at[pl.ds(0, width), :])
    for h in range(heads):
        started[5 + h].wait()
        send_off(q_ref.at[h], q_msg.at[pl.ds(h * width, width), :])
    started[3].wait()
    for h in range(heads):
        g = mm(wuv_ref[h], og_t_ref[h]).astype(BF16).astype(F32)
        delta_ref[h : h + 1, :] = jnp.sum(g * attn[h].astype(F32), axis=0, keepdims=True)
    send_off(delta_ref, delta_hbm)
    for copy in started[5 + heads :]:
        copy.wait()


def hold_kernel(*refs):
    half = len(refs) // 2
    for source, target in zip(refs[:half], refs[half:]):
        target[...] = source[...]


def score_kernel(factor, nkey, width, heads, last, *refs):
    lat_refs, refs = refs[:nkey], refs[nkey:]
    tok = lat_refs[0].shape[1]
    rows = heads * tok
    if last:
        q_all_ref, near_ref, delta_ref, s_ref, k_ref, stat_ref, kt = refs
    else:
        q_refs, refs = refs[:GROUP], refs[GROUP:]
        s_ref, k_ref, stat_ref, q_all_ref, kt = refs
        for j in range(GROUP):
            for h in range(heads):
                cols = slice(j * rows + h * tok, j * rows + (h + 1) * tok)
                q_all_ref[:width, cols] = q_refs[j][h * width : (h + 1) * width, :]
                q_all_ref[width : width + EXTRA, cols] = q_refs[j][q_refs[j].shape[0] - EXTRA :, :]
        spare = q_all_ref.shape[0] - width - EXTRA
        q_all_ref[width + EXTRA :, :] = jnp.zeros((spare, GROUP * rows), BF16)
    wide = kt.shape[0]
    for a in range(nkey):
        kt[: width + EXTRA, a * tok : (a + 1) * tok] = lat_refs[a][...]
    kt[width + EXTRA :, :] = jnp.zeros((wide - width - EXTRA, nkey * tok), BF16)
    keys = kt[...].T
    pos = keys[:, wide - 128 :].astype(F32)
    at = width - (wide - 128)
    key_pos = pos[:, at : at + 1] * 64.0 + pos[:, at + 1 : at + 2]
    lane = lax.broadcasted_iota(jnp.int32, keys.shape, 1)
    k_ref[...] = jnp.where(lane < width, keys, jnp.zeros_like(keys))
    stat_ref[...] = jnp.zeros_like(stat_ref)
    if last:
        stat_ref[GROUP * heads : GROUP * heads + heads, :] = delta_ref[:heads, :]
    for j in range(GROUP):
        cols = slice(j * rows, (j + 1) * rows)
        qp = q_all_ref[width : width + EXTRA, cols].astype(F32)
        row_pos = qp[0:1, :] * 64.0 + qp[1:2, :]
        s = mm(k_ref[...], q_all_ref[:, cols]) * factor
        s = jnp.where(key_pos <= row_pos, s, -1e30)
        s_ref[:, cols] = s
        top = jnp.max(s, axis=0, keepdims=True)
        lse = top + jnp.log(jnp.sum(jnp.exp(s - top), axis=0, keepdims=True))
        for h in range(heads):
            at = j * heads + h
            part = lse[:, h * tok : (h + 1) * tok]
            if last:
                near = near_ref[at : at + 1, :]
                most = jnp.maximum(part, near)
                part = most + jnp.log(jnp.exp(part - most) + jnp.exp(near - most))
            stat_ref[at : at + 1, :] = part


def context_kernel(width, heads, *refs):
    q_refs = refs[:GROUP]
    wuv_ref, near_k_ref, last_k_ref, g_ref, near_gp_ref, last_gp_ref = refs[GROUP:]
    lat, all_rows = g_ref.shape
    tok = q_refs[0].shape[1]
    rows = heads * tok
    for j in range(GROUP):
        for h in range(heads):
            at = heads * width + h * HEAD_DIM
            og = q_refs[j][at : at + HEAD_DIM, :]
            col = j * rows + h * tok
            g_ref[:, col : col + tok] = mm(wuv_ref[h], og).astype(BF16)
        cols = slice(j * rows, (j + 1) * rows)
        near_gp_ref[:, cols] = mm(near_k_ref[:, :lat], g_ref[:, cols])
        last_gp_ref[:, cols] = mm(last_k_ref[:, :lat], g_ref[:, cols])


def pair_kernel(heads, keys, *refs):
    stats, (s_ref, gp_ref, gs_ref, p_ref) = refs[:GROUP], refs[GROUP : GROUP + 4]
    all_rows = s_ref.shape[1]
    rows = all_rows // GROUP
    for j in range(GROUP):
        cols = slice(j * rows, (j + 1) * rows)
        lse_parts = []
        for k in range(GROUP):
            at = (j ^ k) * heads
            lse_parts.append(
                jnp.concatenate([stats[k][at + h : at + h + 1, :] for h in range(heads)], axis=1)
            )
        top = functools.reduce(jnp.maximum, lse_parts)
        lse = top + jnp.log(sum(jnp.exp(part - top) for part in lse_parts))
        at = GROUP * heads
        delta = jnp.concatenate([stats[j][at + h : at + h + 1, :] for h in range(heads)], axis=1)
        p = jnp.exp(s_ref[keys, cols] - lse)
        gs_ref[:, cols] = (p * (gp_ref[keys, cols] - delta)).astype(BF16)
        p_ref[:, cols] = p.astype(BF16)


def partial_kernel(factor, places, width, g_ref, q_all_ref, gs_ref, p_ref, *part_refs):
    lat = g_ref.shape[0]
    for a, at in enumerate(places):
        along = mm_t(q_all_ref[:width, :], gs_ref[at, :]) * factor
        value = mm_t(g_ref[...], p_ref[at, :])
        part_refs[a][:lat, :] = (along[:lat] + value).astype(BF16)
        part_refs[a][lat:, :] = along[lat:].astype(BF16)


def block_kernel(factor, keys, width, heads, *refs):
    stats, refs = refs[:GROUP], refs[GROUP:]
    s_ref, gp_ref, g_ref, q_all_ref, part_ref, gs_ref, p_ref = refs
    pair_kernel(heads, keys, *stats, s_ref, gp_ref, gs_ref, p_ref)
    partial_kernel(factor, [slice(None)], width, g_ref, q_all_ref, gs_ref, p_ref, part_ref)


def query_kernel(factor, nkey, width, heads, *refs):
    stats, refs = refs[:GROUP], refs[GROUP:]
    (s_ref, gp_ref, last_gs_ref), refs = refs[:3], refs[3:]
    lat_refs, refs = refs[:nkey], refs[nkey:]
    gq_refs, far_refs, (gs_ref, p_ref, kt) = refs[: GROUP - 1], refs[GROUP - 1 : -3], refs[-3:]
    tok = lat_refs[0].shape[1]
    keys = s_ref.shape[0]
    rows = heads * tok
    for a in range(nkey):
        kt[:, a * tok : (a + 1) * tok] = lat_refs[a][:width, :]
    pair_kernel(heads, slice(None), *stats, s_ref, gp_ref, gs_ref, p_ref)
    for j in range(GROUP):
        cols = slice(j * rows, (j + 1) * rows)
        gq = mm(kt[:, :keys], gs_ref[:, cols]) + mm(kt[:, keys:], last_gs_ref[:, cols])
        gq = (gq * factor).astype(BF16)
        for h in range(heads):
            part = gq[:, h * tok : (h + 1) * tok]
            if j < GROUP - 1:
                gq_refs[j][h] = part
            else:
                for c, at, here in segments(h, width, far_refs):
                    far_refs[c][here, :] = part[at]


def segments(head, width, pieces):
    cut = pieces[0].shape[0]
    found = []
    for c in range(len(pieces)):
        low, high = max(head * width, c * cut), min((head + 1) * width, (c + 1) * cut)
        if low < high:
            at = slice(low - head * width, high - head * width)
            found.append((c, at, slice(low - c * cut, high - c * cut)))
    return found


def join_kernel(whole_ref, *refs):
    pieces, out_ref = refs[:-1], refs[-1]
    heads, width, _ = out_ref.shape
    for h in range(heads):
        for c, at, here in segments(h, width, pieces):
            both = whole_ref[h, at, :].astype(F32) + pieces[c][here, :].astype(F32)
            out_ref[h, at, :] = both.astype(BF16)


def sum_kernel(*refs):
    refs[-1][...] = sum(ref[...].astype(F32) for ref in refs[:-1])


def finish_kernel(lat_sum_ref, *refs):
    pieces, lat_out_ref, q_out_ref = refs[:-2], refs[-2], refs[-1]
    lat_out_ref[...] = lat_sum_ref[...].astype(BF16)
    q_out_ref[...] = sum(piece[...].astype(F32) for piece in pieces).astype(BF16)


def spread_kernel(scale, idx_ref, *refs):
    chunks, out_ref = refs[:GROUP], refs[GROUP]
    step = chunks[0].shape[1]
    me = lax.rem(idx_ref[0], GROUP)
    for k in range(GROUP):
        at = pl.multiple_of(jnp.bitwise_xor(me, k) * step, step)
        out_ref[:, pl.ds(at, step), :] = chunks[k][...].astype(F32) * scale


def body(n_ctx, n_dp, positions, queries, latent, out_grad, attn_out, wuv):
    tok, heads, width = queries.shape[1:]
    lat = attn_out.shape[3]
    lines = n_ctx // GROUP
    line_bits = (lines - 1).bit_length()
    rows = heads * tok
    all_rows = GROUP * rows
    keys = lines * tok
    wide = -(-(width + EXTRA) // 128) * 128
    factor = (HEAD_DIM + ROPE) ** (-0.5)

    def swap(x, mask, axis="ctx", size=n_ctx):
        return lax.ppermute(x, axis, [(i, i ^ mask) for i in range(size)])

    def after(x, *done):
        return lax.optimization_barrier((x, done))[0]

    idx = lax.axis_index("ctx").reshape(1)
    step = lat // GROUP
    lat_msg, q_msg, delta, keep, send = call(
        pack_kernel,
        "pack",
        [
            ((width + EXTRA, tok), BF16),
            ((heads * (width + HEAD_DIM) + EXTRA, tok), BF16),
            ((8, tok), F32),
            ((2 * heads, step, HEAD_DIM), BF16),
            ((2 * heads, step, HEAD_DIM), BF16),
        ],
        [
            idx,
            positions,
            jnp.transpose(queries[0], (1, 2, 0)),
            out_grad[0],
            latent[0].T,
            attn_out[0],
            wuv,
        ],
        [
            ((1, tok), jnp.int32),
            (out_grad.shape[1:], BF16),
            (attn_out.shape[1:], BF16),
            (wuv.shape, BF16),
            ((heads, lat, HEAD_DIM), F32),
            ((EXTRA, tok), BF16),
            ((heads, HEAD_DIM, tok), BF16),
            ((8, tok), F32),
            ((2 * heads, step, HEAD_DIM), BF16),
            ((2 * heads, step, HEAD_DIM), BF16),
            ((width, tok), BF16),
            ((heads, width, tok), BF16),
        ],
        smem=(0,),
        hbm=(1, 2, 3, 4, 5, 6),
        copies=11 + 3 * heads,
        out=pltpu.HBM,
        limit=PACK_LIMIT,
    )

    def add(a, b):
        return (a.astype(F32) + b.astype(F32)).astype(BF16)

    dp_hops = [(1 << bit, "dp", n_dp) for bit in range((n_dp - 1).bit_length())]
    line_hops = [(GROUP << bit,) for bit in range(line_bits)]

    q_across = swap(q_msg, 2)
    q_core = swap(q_msg, 1)
    pair = add(keep, swap(send, 1))
    got_pair = swap(pair, *dp_hops[0])
    firsts = [swap(after(lat_msg, q_core) if bit + 1 < line_bits else lat_msg, GROUP << bit) for bit in range(line_bits)]
    own = call(
        hold_kernel,
        "hold_own",
        [(lat_msg.shape, BF16), (q_msg.shape, BF16), (delta.shape, F32)],
        [lat_msg, q_msg, delta],
        share=0,
    )
    q_core, q_across, firsts, got_pair, own = lax.optimization_barrier(
        (q_core, q_across, firsts, got_pair, own)
    )
    held = {0: lat_msg}
    for bit in reversed(range(line_bits)):
        held.update({m | 1 << bit: swap(x, GROUP << bit) for m, x in held.items() if m})
        held[1 << bit] = firsts[bit]
    pair = add(pair, got_pair)
    for step_hop in dp_hops[1:]:
        pair = add(pair, swap(pair, *step_hop))
    lats = [held[m] for m in range(lines)]
    q_far = swap(q_across, 1)
    got_own = swap(pair[heads:], 2)
    lat_own, q_own, delta = own
    lats[0] = lat_own
    qs = [q_own, q_core, q_across, q_far]

    most = lines - 1
    keys = most * tok
    score_flops = 2 * tok * all_rows * wide
    near_s, near_k, near_stat, q_all = call(
        functools.partial(score_kernel, factor, most, width, heads, False),
        "near_scores",
        [((keys, all_rows), F32), ((keys, wide), BF16), ((EXTRA, tok), F32), ((wide, all_rows), BF16)],
        lats[:most] + qs,
        [((wide, keys), BF16)],
        flops=most * score_flops,
        share=0,
    )
    mine = add(pair[:heads], after(got_own, near_stat))
    near = swap(mine, *line_hops[0])
    last_s, last_k, stat = call(
        functools.partial(score_kernel, factor, 1, width, heads, True),
        "last_scores",
        [((tok, all_rows), F32), ((tok, wide), BF16), ((EXTRA, tok), F32)],
        [lats[most], q_all, near_stat, delta],
        [((wide, tok), BF16)],
        flops=score_flops,
    )
    stats = [stat] + [swap(stat, k) for k in range(1, GROUP)]
    g, near_gp, last_gp = call(
        functools.partial(context_kernel, width, heads),
        "context",
        [((lat, all_rows), BF16), ((keys, all_rows), F32), ((tok, all_rows), F32)],
        qs + [wuv, near_k, last_k],
        flops=2 * lines * tok * all_rows * lat + 2 * all_rows * lat * HEAD_DIM,
        share=3,
    )
    mine = add(mine, after(near, stat))
    for step_hop in line_hops[1:-1]:
        mine = add(mine, swap(mine, *step_hop))
    near = swap(mine, *line_hops[-1])
    def block(name, keys_at, s, gp, keep):
        part, pairs = ((width, tok), BF16), ((tok, all_rows), BF16)
        return call(
            functools.partial(block_kernel, factor, keys_at, width, heads),
            name,
            [part, pairs] if keep else [part],
            stats + [s, gp, g, q_all],
            [pairs] if keep else [pairs] * 2,
            flops=2 * tok * all_rows * (width + lat),
        )

    last_part, last_gs = block("last_gradients", slice(None), last_s, last_gp, True)
    last_got = swap(last_part, GROUP)
    (next_part,) = block("next_gradients", slice(tok, 2 * tok), near_s, after(near_gp, last_part), False)
    next_got = swap(next_part, GROUP)
    mine = add(mine, near)
    gq_shape, cut_shape = (heads, width, tok), (heads * width // CUTS, tok)
    gq_own, gq_core, gq_across, *far_cuts, near_gs, near_p = call(
        functools.partial(query_kernel, factor, lines, width, heads),
        "query_gradients",
        [(gq_shape, BF16)] * 3 + [(cut_shape, BF16)] * CUTS + [((keys, all_rows), BF16)] * 2,
        stats + [near_s, near_gp, after(last_gs, mine)] + lats,
        [((width, lines * tok), BF16)],
        flops=2 * lines * tok * all_rows * width,
        share=0,
    )
    across = swap(mine, 2)
    far_cuts = [swap(cut, 1) for cut in far_cuts]
    (gq_sum,) = call(join_kernel, "join", [(gq_shape, BF16)], [after(gq_across, across)] + far_cuts)
    gq_last = swap(gq_sum, 2)
    gq_core = swap(after(gq_core, gq_sum), 1)
    def partials(name, blocks, gs, p, share=1):
        rows = [slice(m * tok, (m + 1) * tok) for m in blocks]
        made = call(
            functools.partial(partial_kernel, factor, rows, width),
            name,
            [((width, tok), BF16)] * len(blocks),
            [g, q_all, gs, p],
            flops=2 * len(blocks) * tok * all_rows * (width + lat),
            share=share,
        )
        return dict(zip(blocks, made))

    middle = lines // 2
    made = partials("middle_gradients", [middle], near_gs, near_p, 3)
    made.update(partials("near_gradients", [m for m in range(most) if m not in (1, middle)], near_gs, after(near_p, *far_cuts)))
    made[1] = next_part
    near_parts = [made[m] for m in range(most)]
    parts = list(near_parts) + [last_part]
    kept = [parts[0]]
    for bit in range(line_bits):
        for m in range(3 << bit, lines, 2 << bit):
            got = last_got if m == most and bit == 0 else swap(parts[m], GROUP << bit)
            parts[m ^ 1 << bit] = add(parts[m ^ 1 << bit], got)
    mine_two = jnp.concatenate([mine, across], axis=0)
    other_two = swap(mine_two, 1)
    pieces = [mine_two[:heads], other_two[:heads], mine_two[heads:], other_two[heads:]]
    kept += [swap(parts[1 << bit], GROUP << bit) for bit in range(1, line_bits)] + [next_got]
    scale = 1.0 / math.sqrt(tok * n_ctx * n_dp)
    (grad_w,) = call(
        functools.partial(spread_kernel, scale),
        "spread",
        [((heads, lat, HEAD_DIM), F32)],
        [idx] + pieces,
        smem=(0,),
    )
    kept[0] = after(kept[0], grad_w)
    (lat_sum,) = call(sum_kernel, "latent_sum", [((width, tok), F32)], kept, flops=3 * 10**9)
    grad_lat, grad_q = call(
        finish_kernel,
        "finish",
        [((width, tok), BF16), ((heads, width, tok), BF16)],
        [lat_sum, gq_own, gq_core, gq_last],
    )
    return (jnp.transpose(grad_q, (2, 0, 1))[None], grad_lat.T[None], grad_w)


def solution(mesh):
    placed = (
        P("dp", "ctx"),
        P("dp", "ctx", None, None),
        P("dp", "ctx", None),
        P("dp", "ctx", None, None),
        P("dp", "ctx", None, None),
        P(),
    )
    return jax.shard_map(
        functools.partial(body, mesh.shape["ctx"], mesh.shape["dp"]),
        mesh=mesh,
        in_specs=placed,
        out_specs=(P("dp", "ctx", None, None), P("dp", "ctx", None), P()),
        check_vma=False,
    )
```

```python
import functools
import math

import jax
import jax.numpy as jnp
from jax import lax
from jax.experimental import pallas as pl
from jax.experimental.pallas import tpu as pltpu
from jax.sharding import PartitionSpec as P

ROPE = 64
HEAD_DIM = 128
GROUP = 4
EXTRA = 16
CUTS = 2
PACK_LIMIT = 63 << 20
F32 = jnp.float32
BF16 = jnp.bfloat16


def mm(a, b):
    return jnp.dot(a, b, preferred_element_type=F32)


def mm_t(a, b):
    return lax.dot_general(a, b, (((1,), (1,)), ((), ())), preferred_element_type=F32)


def size_of(shape, dtype):
    return math.prod(shape) * jnp.dtype(dtype).itemsize


def call(kernel, name, outs, args, scratch=(), flops=0, smem=(), hbm=(), copies=0, limit=None, share=1, out=pltpu.VMEM):
    def place(i):
        return pltpu.SMEM if i in smem else pltpu.HBM if i in hbm else pltpu.VMEM

    moved = sum(size_of(a.shape, a.dtype) for a in args) + sum(size_of(*o) for o in outs)
    held = moved + sum(size_of(*s) for s in scratch)
    semaphores = [pltpu.SemaphoreType.DMA((copies,))] if copies else []
    return pl.pallas_call(
        kernel,
        out_shape=[jax.ShapeDtypeStruct(s, d) for s, d in outs],
        in_specs=[pl.BlockSpec(memory_space=place(i)) for i in range(len(args))],
        out_specs=[pl.BlockSpec(memory_space=out) for _ in outs],
        scratch_shapes=[pltpu.VMEM(s, d) for s, d in scratch] + semaphores,
        compiler_params=pltpu.CompilerParams(vmem_limit_bytes=limit or int(1.2 * held) + (8 << 20)),
        cost_estimate=pl.CostEstimate(flops=flops * share, bytes_accessed=moved * share, transcendentals=0),
        name=name,
    )(*args)


def fetch(pairs, sems):
    copies = [pltpu.make_async_copy(src, dst, sems.at[i]) for i, (src, dst) in enumerate(pairs)]
    for copy in copies:
        copy.start()
    return copies


def pack_kernel(
    idx_ref, pos_hbm, q_hbm, og_hbm, lat_hbm, attn_hbm, wuv_hbm,
    lat_msg, q_msg, delta_hbm, keep_hbm, send_hbm,
    pos_ref, og_ref, attn_ref, wuv_ref, term, rows_ref, og_t_ref, delta_ref, keep_ref, send_ref,
    lat_ref, q_ref, sems,
):
    heads, width, tok = q_hbm.shape
    _, lat, _ = wuv_ref.shape
    started = []

    def send_off(src, dst):
        copy = pltpu.make_async_copy(src, dst, sems.at[len(started)])
        copy.start()
        started.append(copy)

    send_off(og_hbm, og_ref)
    send_off(pos_hbm, pos_ref)
    send_off(attn_hbm, attn_ref)
    send_off(wuv_hbm, wuv_ref)
    send_off(lat_hbm, lat_ref)
    for h in range(heads):
        send_off(q_hbm.at[h], q_ref.at[h])
    started[0].wait()
    for h in range(heads):
        og_t_ref[h] = og_ref[:, h, :].T
        send_off(og_t_ref.at[h], q_msg.at[pl.ds(heads * width + h * HEAD_DIM, HEAD_DIM), :])
    started[1].wait()
    pos = jnp.broadcast_to(pos_ref[...], (EXTRA, tok))
    row = lax.broadcasted_iota(jnp.int32, (EXTRA, tok), 0)
    high = lax.shift_right_logical(pos, 6)
    both = jnp.where(row == 0, high, jnp.where(row == 1, pos - high * 64, 0))
    rows_ref[...] = both.astype(F32).astype(BF16)
    send_off(rows_ref, lat_msg.at[pl.ds(width, EXTRA), :])
    send_off(rows_ref, q_msg.at[pl.ds(heads * (width + HEAD_DIM), EXTRA), :])
    delta_ref[...] = jnp.zeros_like(delta_ref)
    started[2].wait()
    attn = [attn_ref[:, h, :].T for h in range(heads)]
    for h in range(heads):
        term[h] = mm_t(attn[h], og_t_ref[h])
    step = lat // GROUP
    me = lax.rem(idx_ref[0], GROUP)
    for k in range(GROUP):
        at = pl.multiple_of(jnp.bitwise_xor(me, k) * step, step)
        target = send_ref if k % 2 else keep_ref
        target[k // 2 * heads : (k // 2 + 1) * heads] = term[:, pl.ds(at, step), :].astype(BF16)
    send_off(send_ref, send_hbm)
    send_off(keep_ref, keep_hbm)
    started[4].wait()
    send_off(lat_ref, lat_msg.at[pl.ds(0, width), :])
    for h in range(heads):
        started[5 + h].wait()
        send_off(q_ref.at[h], q_msg.at[pl.ds(h * width, width), :])
    started[3].wait()
    for h in range(heads):
        g = mm(wuv_ref[h], og_t_ref[h]).astype(BF16).astype(F32)
        delta_ref[h : h + 1, :] = jnp.sum(g * attn[h].astype(F32), axis=0, keepdims=True)
    send_off(delta_ref, delta_hbm)
    for copy in started[5 + heads :]:
        copy.wait()


def hold_kernel(*refs):
    half = len(refs) // 2
    for source, target in zip(refs[:half], refs[half:]):
        target[...] = source[...]


def score_kernel(factor, nkey, width, heads, last, *refs):
    lat_refs, refs = refs[:nkey], refs[nkey:]
    tok = lat_refs[0].shape[1]
    rows = heads * tok
    if last:
        q_all_ref, near_ref, delta_ref, s_ref, k_ref, stat_ref, kt = refs
    else:
        q_refs, refs = refs[:GROUP], refs[GROUP:]
        s_ref, k_ref, stat_ref, q_all_ref, kt = refs
        for j in range(GROUP):
            for h in range(heads):
                cols = slice(j * rows + h * tok, j * rows + (h + 1) * tok)
                q_all_ref[:width, cols] = q_refs[j][h * width : (h + 1) * width, :]
                q_all_ref[width : width + EXTRA, cols] = q_refs[j][q_refs[j].shape[0] - EXTRA :, :]
        spare = q_all_ref.shape[0] - width - EXTRA
        q_all_ref[width + EXTRA :, :] = jnp.zeros((spare, GROUP * rows), BF16)
    wide = kt.shape[0]
    for a in range(nkey):
        kt[: width + EXTRA, a * tok : (a + 1) * tok] = lat_refs[a][...]
    kt[width + EXTRA :, :] = jnp.zeros((wide - width - EXTRA, nkey * tok), BF16)
    keys = kt[...].T
    pos = keys[:, wide - 128 :].astype(F32)
    at = width - (wide - 128)
    key_pos = pos[:, at : at + 1] * 64.0 + pos[:, at + 1 : at + 2]
    lane = lax.broadcasted_iota(jnp.int32, keys.shape, 1)
    k_ref[...] = jnp.where(lane < width, keys, jnp.zeros_like(keys))
    stat_ref[...] = jnp.zeros_like(stat_ref)
    if last:
        stat_ref[GROUP * heads : GROUP * heads + heads, :] = delta_ref[:heads, :]
    for j in range(GROUP):
        cols = slice(j * rows, (j + 1) * rows)
        qp = q_all_ref[width : width + EXTRA, cols].astype(F32)
        row_pos = qp[0:1, :] * 64.0 + qp[1:2, :]
        s = mm(k_ref[...], q_all_ref[:, cols]) * factor
        s = jnp.where(key_pos <= row_pos, s, -1e30)
        s_ref[:, cols] = s
        top = jnp.max(s, axis=0, keepdims=True)
        lse = top + jnp.log(jnp.sum(jnp.exp(s - top), axis=0, keepdims=True))
        for h in range(heads):
            at = j * heads + h
            part = lse[:, h * tok : (h + 1) * tok]
            if last:
                near = near_ref[at : at + 1, :]
                most = jnp.maximum(part, near)
                part = most + jnp.log(jnp.exp(part - most) + jnp.exp(near - most))
            stat_ref[at : at + 1, :] = part


def context_kernel(width, heads, *refs):
    q_refs = refs[:GROUP]
    wuv_ref, k_ref, g_ref, gp_ref = refs[GROUP:]
    lat, all_rows = g_ref.shape
    tok = q_refs[0].shape[1]
    rows = heads * tok
    for j in range(GROUP):
        for h in range(heads):
            at = heads * width + h * HEAD_DIM
            og = q_refs[j][at : at + HEAD_DIM, :]
            col = j * rows + h * tok
            g_ref[:, col : col + tok] = mm(wuv_ref[h], og).astype(BF16)
        cols = slice(j * rows, (j + 1) * rows)
        gp_ref[:, cols] = mm(k_ref[:, :lat], g_ref[:, cols])


def prob_kernel(k_ref, g_ref, gp_ref):
    lat, all_rows = g_ref.shape
    rows = all_rows // GROUP
    for j in range(GROUP):
        cols = slice(j * rows, (j + 1) * rows)
        gp_ref[:, cols] = mm(k_ref[:, :lat], g_ref[:, cols])


def pair_kernel(heads, keys, *refs):
    stats, (s_ref, gp_ref, gs_ref, p_ref) = refs[:GROUP], refs[GROUP : GROUP + 4]
    all_rows = s_ref.shape[1]
    rows = all_rows // GROUP
    for j in range(GROUP):
        cols = slice(j * rows, (j + 1) * rows)
        lse_parts = []
        for k in range(GROUP):
            at = (j ^ k) * heads
            lse_parts.append(
                jnp.concatenate([stats[k][at + h : at + h + 1, :] for h in range(heads)], axis=1)
            )
        top = functools.reduce(jnp.maximum, lse_parts)
        lse = top + jnp.log(sum(jnp.exp(part - top) for part in lse_parts))
        at = GROUP * heads
        delta = jnp.concatenate([stats[j][at + h : at + h + 1, :] for h in range(heads)], axis=1)
        p = jnp.exp(s_ref[keys, cols] - lse)
        gs_ref[:, cols] = (p * (gp_ref[keys, cols] - delta)).astype(BF16)
        p_ref[:, cols] = p.astype(BF16)


def partial_kernel(factor, places, width, g_ref, q_all_ref, gs_ref, p_ref, *part_refs):
    lat = g_ref.shape[0]
    for a, at in enumerate(places):
        along = mm_t(q_all_ref[:width, :], gs_ref[at, :]) * factor
        value = mm_t(g_ref[...], p_ref[at, :])
        part_refs[a][:lat, :] = (along[:lat] + value).astype(BF16)
        part_refs[a][lat:, :] = along[lat:].astype(BF16)


def block_kernel(factor, keys, width, heads, *refs):
    stats, refs = refs[:GROUP], refs[GROUP:]
    s_ref, gp_ref, g_ref, q_all_ref, part_ref, gs_ref, p_ref = refs
    pair_kernel(heads, keys, *stats, s_ref, gp_ref, gs_ref, p_ref)
    partial_kernel(factor, [slice(None)], width, g_ref, q_all_ref, gs_ref, p_ref, part_ref)


def query_kernel(factor, nkey, width, heads, *refs):
    stats, refs = refs[:GROUP], refs[GROUP:]
    (s_ref, gp_ref, last_gs_ref), refs = refs[:3], refs[3:]
    lat_refs, refs = refs[:nkey], refs[nkey:]
    gq_refs, far_refs, (gs_ref, p_ref, kt) = refs[: GROUP - 1], refs[GROUP - 1 : -3], refs[-3:]
    tok = lat_refs[0].shape[1]
    keys = s_ref.shape[0]
    rows = heads * tok
    for a in range(nkey):
        kt[:, a * tok : (a + 1) * tok] = lat_refs[a][:width, :]
    pair_kernel(heads, slice(None), *stats, s_ref, gp_ref, gs_ref, p_ref)
    for j in range(GROUP):
        cols = slice(j * rows, (j + 1) * rows)
        gq = mm(kt[:, :keys], gs_ref[:, cols]) + mm(kt[:, keys:], last_gs_ref[:, cols])
        gq = (gq * factor).astype(BF16)
        for h in range(heads):
            part = gq[:, h * tok : (h + 1) * tok]
            if j < GROUP - 1:
                gq_refs[j][h] = part
            else:
                for c, at, here in segments(h, width, far_refs):
                    far_refs[c][here, :] = part[at]


def segments(head, width, pieces):
    cut = pieces[0].shape[0]
    found = []
    for c in range(len(pieces)):
        low, high = max(head * width, c * cut), min((head + 1) * width, (c + 1) * cut)
        if low < high:
            at = slice(low - head * width, high - head * width)
            found.append((c, at, slice(low - c * cut, high - c * cut)))
    return found


def join_kernel(whole_ref, *refs):
    pieces, out_ref = refs[:-1], refs[-1]
    heads, width, _ = out_ref.shape
    for h in range(heads):
        for c, at, here in segments(h, width, pieces):
            both = whole_ref[h, at, :].astype(F32) + pieces[c][here, :].astype(F32)
            out_ref[h, at, :] = both.astype(BF16)


def sum_kernel(*refs):
    refs[-1][...] = sum(ref[...].astype(F32) for ref in refs[:-1])


def finish_kernel(lat_sum_ref, *refs):
    pieces, lat_out_ref, q_out_ref = refs[:-2], refs[-2], refs[-1]
    lat_out_ref[...] = lat_sum_ref[...].astype(BF16)
    q_out_ref[...] = sum(piece[...].astype(F32) for piece in pieces).astype(BF16)


def spread_kernel(scale, idx_ref, *refs):
    chunks, out_ref = refs[:GROUP], refs[GROUP]
    step = chunks[0].shape[1]
    me = lax.rem(idx_ref[0], GROUP)
    for k in range(GROUP):
        at = pl.multiple_of(jnp.bitwise_xor(me, k) * step, step)
        out_ref[:, pl.ds(at, step), :] = chunks[k][...].astype(F32) * scale


def body(n_ctx, n_dp, positions, queries, latent, out_grad, attn_out, wuv):
    tok, heads, width = queries.shape[1:]
    lat = attn_out.shape[3]
    lines = n_ctx // GROUP
    line_bits = (lines - 1).bit_length()
    rows = heads * tok
    all_rows = GROUP * rows
    keys = lines * tok
    wide = -(-(width + EXTRA) // 128) * 128
    factor = (HEAD_DIM + ROPE) ** (-0.5)

    def swap(x, mask, axis="ctx", size=n_ctx):
        return lax.ppermute(x, axis, [(i, i ^ mask) for i in range(size)])

    def after(x, *done):
        return lax.optimization_barrier((x, done))[0]

    idx = lax.axis_index("ctx").reshape(1)
    step = lat // GROUP
    lat_msg, q_msg, delta, keep, send = call(
        pack_kernel,
        "pack",
        [
            ((width + EXTRA, tok), BF16),
            ((heads * (width + HEAD_DIM) + EXTRA, tok), BF16),
            ((8, tok), F32),
            ((2 * heads, step, HEAD_DIM), BF16),
            ((2 * heads, step, HEAD_DIM), BF16),
        ],
        [
            idx,
            positions,
            jnp.transpose(queries[0], (1, 2, 0)),
            out_grad[0],
            latent[0].T,
            attn_out[0],
            wuv,
        ],
        [
            ((1, tok), jnp.int32),
            (out_grad.shape[1:], BF16),
            (attn_out.shape[1:], BF16),
            (wuv.shape, BF16),
            ((heads, lat, HEAD_DIM), F32),
            ((EXTRA, tok), BF16),
            ((heads, HEAD_DIM, tok), BF16),
            ((8, tok), F32),
            ((2 * heads, step, HEAD_DIM), BF16),
            ((2 * heads, step, HEAD_DIM), BF16),
            ((width, tok), BF16),
            ((heads, width, tok), BF16),
        ],
        smem=(0,),
        hbm=(1, 2, 3, 4, 5, 6),
        copies=11 + 3 * heads,
        out=pltpu.HBM,
        limit=PACK_LIMIT,
    )

    def add(a, b):
        return (a.astype(F32) + b.astype(F32)).astype(BF16)

    dp_hops = [(1 << bit, "dp", n_dp) for bit in range((n_dp - 1).bit_length())]
    line_hops = [(GROUP << bit,) for bit in range(line_bits)]

    q_across = swap(q_msg, 2)
    q_core = swap(q_msg, 1)
    pair = add(keep, swap(send, 1))
    got_pair = swap(pair, *dp_hops[0])
    firsts = [swap(after(lat_msg, q_core) if bit + 1 < line_bits else lat_msg, GROUP << bit) for bit in range(line_bits)]
    own = call(
        hold_kernel,
        "hold_own",
        [(lat_msg.shape, BF16), (q_msg.shape, BF16), (delta.shape, F32)],
        [lat_msg, q_msg, delta],
        share=0,
    )
    q_core, q_across, firsts, got_pair, own = lax.optimization_barrier(
        (q_core, q_across, firsts, got_pair, own)
    )
    held = {0: lat_msg}
    for bit in reversed(range(line_bits)):
        held.update({m | 1 << bit: swap(x, GROUP << bit) for m, x in held.items() if m})
        held[1 << bit] = firsts[bit]
    pair = add(pair, got_pair)
    for step_hop in dp_hops[1:]:
        pair = add(pair, swap(pair, *step_hop))
    lats = [held[m] for m in range(lines)]
    q_far = swap(q_across, 1)
    got_own = swap(pair[heads:], 2)
    lat_own, q_own, delta = own
    lats[0] = lat_own
    qs = [q_own, q_core, q_across, q_far]

    most = lines - 1
    keys = most * tok
    score_flops = 2 * tok * all_rows * wide
    near_s, near_k, near_stat, q_all = call(
        functools.partial(score_kernel, factor, most, width, heads, False),
        "near_scores",
        [((keys, all_rows), F32), ((keys, wide), BF16), ((EXTRA, tok), F32), ((wide, all_rows), BF16)],
        lats[:most] + qs,
        [((wide, keys), BF16)],
        flops=most * score_flops,
        share=0,
    )
    g, near_gp = call(
        functools.partial(context_kernel, width, heads),
        "near_context",
        [((lat, all_rows), BF16), ((keys, all_rows), F32)],
        qs + [wuv, near_k],
        share=0,
    )
    mine = add(pair[:heads], after(got_own, near_gp))
    near = swap(mine, *line_hops[0])
    last_s, last_k, stat = call(
        functools.partial(score_kernel, factor, 1, width, heads, True),
        "last_scores",
        [((tok, all_rows), F32), ((tok, wide), BF16), ((EXTRA, tok), F32)],
        [lats[most], q_all, after(near_stat, near_gp), delta],
        [((wide, tok), BF16)],
        flops=score_flops,
    )
    stats = [stat] + [swap(stat, k) for k in range(1, GROUP)]
    (last_gp,) = call(
        prob_kernel,
        "last_context",
        [((tok, all_rows), F32)],
        [last_k, g],
        flops=2 * lines * tok * all_rows * lat + 2 * all_rows * lat * HEAD_DIM,
        share=3,
    )
    mine = add(mine, after(near, stat))
    for step_hop in line_hops[1:-1]:
        mine = add(mine, swap(mine, *step_hop))
    near = swap(mine, *line_hops[-1])
    def block(name, keys_at, s, gp, keep):
        part, pairs = ((width, tok), BF16), ((tok, all_rows), BF16)
        return call(
            functools.partial(block_kernel, factor, keys_at, width, heads),
            name,
            [part, pairs] if keep else [part],
            stats + [s, gp, g, q_all],
            [pairs] if keep else [pairs] * 2,
            flops=2 * tok * all_rows * (width + lat),
        )

    last_part, last_gs = block("last_gradients", slice(None), last_s, last_gp, True)
    last_got = swap(last_part, GROUP)
    (next_part,) = block("next_gradients", slice(tok, 2 * tok), near_s, after(near_gp, last_part), False)
    next_got = swap(next_part, GROUP)
    mine = add(mine, near)
    gq_shape, cut_shape = (heads, width, tok), (heads * width // CUTS, tok)
    gq_own, gq_core, gq_across, *far_cuts, near_gs, near_p = call(
        functools.partial(query_kernel, factor, lines, width, heads),
        "query_gradients",
        [(gq_shape, BF16)] * 3 + [(cut_shape, BF16)] * CUTS + [((keys, all_rows), BF16)] * 2,
        stats + [near_s, near_gp, after(last_gs, mine)] + lats,
        [((width, lines * tok), BF16)],
        flops=2 * lines * tok * all_rows * width,
        share=0,
    )
    across = swap(mine, 2)
    far_cuts = [swap(cut, 1) for cut in far_cuts]
    (gq_sum,) = call(join_kernel, "join", [(gq_shape, BF16)], [after(gq_across, across)] + far_cuts)
    gq_last = swap(gq_sum, 2)
    gq_core = swap(after(gq_core, gq_sum), 1)
    def partials(name, blocks, gs, p, share=1):
        rows = [slice(m * tok, (m + 1) * tok) for m in blocks]
        made = call(
            functools.partial(partial_kernel, factor, rows, width),
            name,
            [((width, tok), BF16)] * len(blocks),
            [g, q_all, gs, p],
            flops=2 * len(blocks) * tok * all_rows * (width + lat),
            share=share,
        )
        return dict(zip(blocks, made))

    middle = lines // 2
    made = partials("middle_gradients", [middle], near_gs, near_p, 3)
    made.update(partials("near_gradients", [m for m in range(most) if m not in (1, middle)], near_gs, after(near_p, *far_cuts)))
    made[1] = next_part
    near_parts = [made[m] for m in range(most)]
    parts = list(near_parts) + [last_part]
    kept = [parts[0]]
    for bit in range(line_bits):
        for m in range(3 << bit, lines, 2 << bit):
            got = last_got if m == most and bit == 0 else swap(parts[m], GROUP << bit)
            parts[m ^ 1 << bit] = add(parts[m ^ 1 << bit], got)
    mine_two = jnp.concatenate([mine, across], axis=0)
    other_two = swap(mine_two, 1)
    pieces = [mine_two[:heads], other_two[:heads], mine_two[heads:], other_two[heads:]]
    kept += [swap(parts[1 << bit], GROUP << bit) for bit in range(1, line_bits)] + [next_got]
    scale = 1.0 / math.sqrt(tok * n_ctx * n_dp)
    (grad_w,) = call(
        functools.partial(spread_kernel, scale),
        "spread",
        [((heads, lat, HEAD_DIM), F32)],
        [idx] + pieces,
        smem=(0,),
    )
    kept[0] = after(kept[0], grad_w)
    (lat_sum,) = call(sum_kernel, "latent_sum", [((width, tok), F32)], kept, flops=3 * 10**9)
    grad_lat, grad_q = call(
        finish_kernel,
        "finish",
        [((width, tok), BF16), ((heads, width, tok), BF16)],
        [lat_sum, gq_own, gq_core, gq_last],
    )
    return (jnp.transpose(grad_q, (2, 0, 1))[None], grad_lat.T[None], grad_w)


def solution(mesh):
    placed = (
        P("dp", "ctx"),
        P("dp", "ctx", None, None),
        P("dp", "ctx", None),
        P("dp", "ctx", None, None),
        P("dp", "ctx", None, None),
        P(),
    )
    return jax.shard_map(
        functools.partial(body, mesh.shape["ctx"], mesh.shape["dp"]),
        mesh=mesh,
        in_specs=placed,
        out_specs=(P("dp", "ctx", None, None), P("dp", "ctx", None), P()),
        check_vma=False,
    )
```

```python
import functools
import math

import jax
import jax.numpy as jnp
from jax import lax
from jax.experimental import pallas as pl
from jax.experimental.pallas import tpu as pltpu
from jax.sharding import PartitionSpec as P

ROPE = 64
HEAD_DIM = 128
GROUP = 4
EXTRA = 16
CUTS = 2
PACK_LIMIT = 63 << 20
F32 = jnp.float32
BF16 = jnp.bfloat16


def mm(a, b):
    return jnp.dot(a, b, preferred_element_type=F32)


def mm_t(a, b):
    return lax.dot_general(a, b, (((1,), (1,)), ((), ())), preferred_element_type=F32)


def size_of(shape, dtype):
    return math.prod(shape) * jnp.dtype(dtype).itemsize


def call(kernel, name, outs, args, scratch=(), flops=0, smem=(), hbm=(), copies=0, limit=None, share=1, out=pltpu.VMEM):
    def place(i):
        return pltpu.SMEM if i in smem else pltpu.HBM if i in hbm else pltpu.VMEM

    moved = sum(size_of(a.shape, a.dtype) for a in args) + sum(size_of(*o) for o in outs)
    held = moved + sum(size_of(*s) for s in scratch)
    semaphores = [pltpu.SemaphoreType.DMA((copies,))] if copies else []
    return pl.pallas_call(
        kernel,
        out_shape=[jax.ShapeDtypeStruct(s, d) for s, d in outs],
        in_specs=[pl.BlockSpec(memory_space=place(i)) for i in range(len(args))],
        out_specs=[pl.BlockSpec(memory_space=out) for _ in outs],
        scratch_shapes=[pltpu.VMEM(s, d) for s, d in scratch] + semaphores,
        compiler_params=pltpu.CompilerParams(vmem_limit_bytes=limit or int(1.2 * held) + (8 << 20)),
        cost_estimate=pl.CostEstimate(flops=flops * share, bytes_accessed=moved * share, transcendentals=0),
        name=name,
    )(*args)


def fetch(pairs, sems):
    copies = [pltpu.make_async_copy(src, dst, sems.at[i]) for i, (src, dst) in enumerate(pairs)]
    for copy in copies:
        copy.start()
    return copies


def pack_kernel(
    idx_ref, pos_hbm, q_hbm, og_hbm, lat_hbm, attn_hbm, wuv_hbm,
    lat_msg, q_msg, delta_hbm, keep_hbm, send_hbm,
    pos_ref, og_ref, attn_ref, wuv_ref, term, rows_ref, og_t_ref, delta_ref, keep_ref, send_ref,
    lat_ref, q_ref, sems,
):
    heads, width, tok = q_hbm.shape
    _, lat, _ = wuv_ref.shape
    started = []

    def send_off(src, dst):
        copy = pltpu.make_async_copy(src, dst, sems.at[len(started)])
        copy.start()
        started.append(copy)

    send_off(og_hbm, og_ref)
    send_off(pos_hbm, pos_ref)
    send_off(attn_hbm, attn_ref)
    send_off(wuv_hbm, wuv_ref)
    send_off(lat_hbm, lat_ref)
    for h in range(heads):
        send_off(q_hbm.at[h], q_ref.at[h])
    started[0].wait()
    for h in range(heads):
        og_t_ref[h] = og_ref[:, h, :].T
        send_off(og_t_ref.at[h], q_msg.at[pl.ds(heads * width + h * HEAD_DIM, HEAD_DIM), :])
    started[1].wait()
    pos = jnp.broadcast_to(pos_ref[...], (EXTRA, tok))
    row = lax.broadcasted_iota(jnp.int32, (EXTRA, tok), 0)
    high = lax.shift_right_logical(pos, 6)
    both = jnp.where(row == 0, high, jnp.where(row == 1, pos - high * 64, 0))
    rows_ref[...] = both.astype(F32).astype(BF16)
    send_off(rows_ref, lat_msg.at[pl.ds(width, EXTRA), :])
    send_off(rows_ref, q_msg.at[pl.ds(heads * (width + HEAD_DIM), EXTRA), :])
    delta_ref[...] = jnp.zeros_like(delta_ref)
    started[2].wait()
    attn = [attn_ref[:, h, :].T for h in range(heads)]
    for h in range(heads):
        term[h] = mm_t(attn[h], og_t_ref[h])
    step = lat // GROUP
    me = lax.rem(idx_ref[0], GROUP)
    for k in range(GROUP):
        at = pl.multiple_of(jnp.bitwise_xor(me, k) * step, step)
        target = send_ref if k % 2 else keep_ref
        target[k // 2 * heads : (k // 2 + 1) * heads] = term[:, pl.ds(at, step), :].astype(BF16)
    send_off(send_ref, send_hbm)
    send_off(keep_ref, keep_hbm)
    started[4].wait()
    send_off(lat_ref, lat_msg.at[pl.ds(0, width), :])
    for h in range(heads):
        started[5 + h].wait()
        send_off(q_ref.at[h], q_msg.at[pl.ds(h * width, width), :])
    started[3].wait()
    for h in range(heads):
        g = mm(wuv_ref[h], og_t_ref[h]).astype(BF16).astype(F32)
        delta_ref[h : h + 1, :] = jnp.sum(g * attn[h].astype(F32), axis=0, keepdims=True)
    send_off(delta_ref, delta_hbm)
    for copy in started[5 + heads :]:
        copy.wait()


def hold_kernel(*refs):
    half = len(refs) // 2
    for source, target in zip(refs[:half], refs[half:]):
        target[...] = source[...]


def score_kernel(factor, nkey, width, heads, last, *refs):
    lat_refs, refs = refs[:nkey], refs[nkey:]
    tok = lat_refs[0].shape[1]
    rows = heads * tok
    if last:
        q_all_ref, near_ref, delta_ref, s_ref, k_ref, stat_ref, kt = refs
    else:
        q_refs, refs = refs[:GROUP], refs[GROUP:]
        s_ref, k_ref, stat_ref, q_all_ref, kt = refs
        for j in range(GROUP):
            for h in range(heads):
                cols = slice(j * rows + h * tok, j * rows + (h + 1) * tok)
                q_all_ref[:width, cols] = q_refs[j][h * width : (h + 1) * width, :]
                q_all_ref[width : width + EXTRA, cols] = q_refs[j][q_refs[j].shape[0] - EXTRA :, :]
        spare = q_all_ref.shape[0] - width - EXTRA
        q_all_ref[width + EXTRA :, :] = jnp.zeros((spare, GROUP * rows), BF16)
    wide = kt.shape[0]
    for a in range(nkey):
        kt[: width + EXTRA, a * tok : (a + 1) * tok] = lat_refs[a][...]
    kt[width + EXTRA :, :] = jnp.zeros((wide - width - EXTRA, nkey * tok), BF16)
    keys = kt[...].T
    pos = keys[:, wide - 128 :].astype(F32)
    at = width - (wide - 128)
    key_pos = pos[:, at : at + 1] * 64.0 + pos[:, at + 1 : at + 2]
    lane = lax.broadcasted_iota(jnp.int32, keys.shape, 1)
    k_ref[...] = jnp.where(lane < width, keys, jnp.zeros_like(keys))
    stat_ref[...] = jnp.zeros_like(stat_ref)
    if last:
        stat_ref[GROUP * heads : GROUP * heads + heads, :] = delta_ref[:heads, :]
    for j in range(GROUP):
        cols = slice(j * rows, (j + 1) * rows)
        qp = q_all_ref[width : width + EXTRA, cols].astype(F32)
        row_pos = qp[0:1, :] * 64.0 + qp[1:2, :]
        s = mm(k_ref[...], q_all_ref[:, cols]) * factor
        s = jnp.where(key_pos <= row_pos, s, -1e30)
        s_ref[:, cols] = s
        top = jnp.max(s, axis=0, keepdims=True)
        lse = top + jnp.log(jnp.sum(jnp.exp(s - top), axis=0, keepdims=True))
        for h in range(heads):
            at = j * heads + h
            part = lse[:, h * tok : (h + 1) * tok]
            if last:
                near = near_ref[at : at + 1, :]
                most = jnp.maximum(part, near)
                part = most + jnp.log(jnp.exp(part - most) + jnp.exp(near - most))
            stat_ref[at : at + 1, :] = part


def context_kernel(width, heads, *refs):
    q_refs = refs[:GROUP]
    wuv_ref, k_ref, g_ref, gp_ref = refs[GROUP:]
    lat, all_rows = g_ref.shape
    tok = q_refs[0].shape[1]
    rows = heads * tok
    for j in range(GROUP):
        for h in range(heads):
            at = heads * width + h * HEAD_DIM
            og = q_refs[j][at : at + HEAD_DIM, :]
            col = j * rows + h * tok
            g_ref[:, col : col + tok] = mm(wuv_ref[h], og).astype(BF16)
        cols = slice(j * rows, (j + 1) * rows)
        gp_ref[:, cols] = mm(k_ref[:, :lat], g_ref[:, cols])


def prob_kernel(k_ref, g_ref, gp_ref):
    lat, all_rows = g_ref.shape
    rows = all_rows // GROUP
    for j in range(GROUP):
        cols = slice(j * rows, (j + 1) * rows)
        gp_ref[:, cols] = mm(k_ref[:, :lat], g_ref[:, cols])


def pair_kernel(heads, keys, *refs):
    stats, (s_ref, gp_ref, gs_ref, p_ref) = refs[:GROUP], refs[GROUP : GROUP + 4]
    all_rows = s_ref.shape[1]
    rows = all_rows // GROUP
    for j in range(GROUP):
        cols = slice(j * rows, (j + 1) * rows)
        lse_parts = []
        for k in range(GROUP):
            at = (j ^ k) * heads
            lse_parts.append(
                jnp.concatenate([stats[k][at + h : at + h + 1, :] for h in range(heads)], axis=1)
            )
        top = functools.reduce(jnp.maximum, lse_parts)
        lse = top + jnp.log(sum(jnp.exp(part - top) for part in lse_parts))
        at = GROUP * heads
        delta = jnp.concatenate([stats[j][at + h : at + h + 1, :] for h in range(heads)], axis=1)
        p = jnp.exp(s_ref[keys, cols] - lse)
        gs_ref[:, cols] = (p * (gp_ref[keys, cols] - delta)).astype(BF16)
        p_ref[:, cols] = p.astype(BF16)


def partial_kernel(factor, places, width, g_ref, q_all_ref, gs_ref, p_ref, *part_refs):
    lat = g_ref.shape[0]
    for a, at in enumerate(places):
        along = mm_t(q_all_ref[:width, :], gs_ref[at, :]) * factor
        value = mm_t(g_ref[...], p_ref[at, :])
        part_refs[a][:lat, :] = (along[:lat] + value).astype(BF16)
        part_refs[a][lat:, :] = along[lat:].astype(BF16)


def block_kernel(factor, keys, width, heads, *refs):
    stats, refs = refs[:GROUP], refs[GROUP:]
    s_ref, gp_ref, g_ref, q_all_ref, part_ref, gs_ref, p_ref = refs
    pair_kernel(heads, keys, *stats, s_ref, gp_ref, gs_ref, p_ref)
    partial_kernel(factor, [slice(None)], width, g_ref, q_all_ref, gs_ref, p_ref, part_ref)


def query_kernel(factor, nkey, width, heads, *refs):
    stats, refs = refs[:GROUP], refs[GROUP:]
    (s_ref, gp_ref, last_gs_ref), refs = refs[:3], refs[3:]
    lat_refs, refs = refs[:nkey], refs[nkey:]
    gq_refs, far_refs, (gs_ref, p_ref, kt) = refs[: GROUP - 1], refs[GROUP - 1 : -3], refs[-3:]
    tok = lat_refs[0].shape[1]
    keys = s_ref.shape[0]
    rows = heads * tok
    for a in range(nkey):
        kt[:, a * tok : (a + 1) * tok] = lat_refs[a][:width, :]
    pair_kernel(heads, slice(None), *stats, s_ref, gp_ref, gs_ref, p_ref)
    for j in range(GROUP):
        cols = slice(j * rows, (j + 1) * rows)
        gq = mm(kt[:, :keys], gs_ref[:, cols]) + mm(kt[:, keys:], last_gs_ref[:, cols])
        gq = (gq * factor).astype(BF16)
        for h in range(heads):
            part = gq[:, h * tok : (h + 1) * tok]
            if j < GROUP - 1:
                gq_refs[j][h] = part
            else:
                for c, at, here in segments(h, width, far_refs):
                    far_refs[c][here, :] = part[at]


def segments(head, width, pieces):
    cut = pieces[0].shape[0]
    found = []
    for c in range(len(pieces)):
        low, high = max(head * width, c * cut), min((head + 1) * width, (c + 1) * cut)
        if low < high:
            at = slice(low - head * width, high - head * width)
            found.append((c, at, slice(low - c * cut, high - c * cut)))
    return found


def join_kernel(whole_ref, *refs):
    pieces, out_ref = refs[:-1], refs[-1]
    heads, width, _ = out_ref.shape
    for h in range(heads):
        for c, at, here in segments(h, width, pieces):
            both = whole_ref[h, at, :].astype(F32) + pieces[c][here, :].astype(F32)
            out_ref[h, at, :] = both.astype(BF16)


def sum_kernel(*refs):
    refs[-1][...] = sum(ref[...].astype(F32) for ref in refs[:-1])


def finish_kernel(lat_sum_ref, *refs):
    pieces, (lat_hbm, q_hbm, lat_ref, q_ref, sems) = refs[:-5], refs[-5:]
    lat_ref[...] = lat_sum_ref[...].astype(BF16)
    copies = [pltpu.make_async_copy(lat_ref, lat_hbm, sems.at[0])]
    copies[0].start()
    for h in range(q_ref.shape[0]):
        q_ref[h] = sum(piece[h].astype(F32) for piece in pieces).astype(BF16)
        copies.append(pltpu.make_async_copy(q_ref.at[h], q_hbm.at[h], sems.at[1 + h]))
        copies[-1].start()
    for copy in copies:
        copy.wait()


def spread_kernel(scale, idx_ref, *refs):
    chunks, out_ref = refs[:GROUP], refs[GROUP]
    step = chunks[0].shape[1]
    me = lax.rem(idx_ref[0], GROUP)
    for k in range(GROUP):
        at = pl.multiple_of(jnp.bitwise_xor(me, k) * step, step)
        out_ref[:, pl.ds(at, step), :] = chunks[k][...].astype(F32) * scale


def body(n_ctx, n_dp, positions, queries, latent, out_grad, attn_out, wuv):
    tok, heads, width = queries.shape[1:]
    lat = attn_out.shape[3]
    lines = n_ctx // GROUP
    line_bits = (lines - 1).bit_length()
    rows = heads * tok
    all_rows = GROUP * rows
    keys = lines * tok
    wide = -(-(width + EXTRA) // 128) * 128
    factor = (HEAD_DIM + ROPE) ** (-0.5)

    def swap(x, mask, axis="ctx", size=n_ctx):
        return lax.ppermute(x, axis, [(i, i ^ mask) for i in range(size)])

    def after(x, *done):
        return lax.optimization_barrier((x, done))[0]

    idx = lax.axis_index("ctx").reshape(1)
    step = lat // GROUP
    lat_msg, q_msg, delta, keep, send = call(
        pack_kernel,
        "pack",
        [
            ((width + EXTRA, tok), BF16),
            ((heads * (width + HEAD_DIM) + EXTRA, tok), BF16),
            ((8, tok), F32),
            ((2 * heads, step, HEAD_DIM), BF16),
            ((2 * heads, step, HEAD_DIM), BF16),
        ],
        [
            idx,
            positions,
            jnp.transpose(queries[0], (1, 2, 0)),
            out_grad[0],
            latent[0].T,
            attn_out[0],
            wuv,
        ],
        [
            ((1, tok), jnp.int32),
            (out_grad.shape[1:], BF16),
            (attn_out.shape[1:], BF16),
            (wuv.shape, BF16),
            ((heads, lat, HEAD_DIM), F32),
            ((EXTRA, tok), BF16),
            ((heads, HEAD_DIM, tok), BF16),
            ((8, tok), F32),
            ((2 * heads, step, HEAD_DIM), BF16),
            ((2 * heads, step, HEAD_DIM), BF16),
            ((width, tok), BF16),
            ((heads, width, tok), BF16),
        ],
        smem=(0,),
        hbm=(1, 2, 3, 4, 5, 6),
        copies=11 + 3 * heads,
        out=pltpu.HBM,
        limit=PACK_LIMIT,
    )

    def add(a, b):
        return (a.astype(F32) + b.astype(F32)).astype(BF16)

    dp_hops = [(1 << bit, "dp", n_dp) for bit in range((n_dp - 1).bit_length())]
    line_hops = [(GROUP << bit,) for bit in range(line_bits)]

    q_across = swap(q_msg, 2)
    q_core = swap(q_msg, 1)
    pair = add(keep, swap(send, 1))
    got_pair = swap(pair, *dp_hops[0])
    firsts = [swap(after(lat_msg, q_core) if bit + 1 < line_bits else lat_msg, GROUP << bit) for bit in range(line_bits)]
    own = call(
        hold_kernel,
        "hold_own",
        [(lat_msg.shape, BF16), (q_msg.shape, BF16), (delta.shape, F32)],
        [lat_msg, q_msg, delta],
        share=0,
    )
    q_core, q_across, firsts, got_pair, own = lax.optimization_barrier(
        (q_core, q_across, firsts, got_pair, own)
    )
    held = {0: lat_msg}
    for bit in reversed(range(line_bits)):
        held.update({m | 1 << bit: swap(x, GROUP << bit) for m, x in held.items() if m})
        held[1 << bit] = firsts[bit]
    pair = add(pair, got_pair)
    for step_hop in dp_hops[1:]:
        pair = add(pair, swap(pair, *step_hop))
    lats = [held[m] for m in range(lines)]
    q_far = swap(q_across, 1)
    got_own = swap(pair[heads:], 2)
    lat_own, q_own, delta = own
    lats[0] = lat_own
    qs = [q_own, q_core, q_across, q_far]

    most = lines - 1
    keys = most * tok
    score_flops = 2 * tok * all_rows * wide
    near_s, near_k, near_stat, q_all = call(
        functools.partial(score_kernel, factor, most, width, heads, False),
        "near_scores",
        [((keys, all_rows), F32), ((keys, wide), BF16), ((EXTRA, tok), F32), ((wide, all_rows), BF16)],
        lats[:most] + qs,
        [((wide, keys), BF16)],
        flops=most * score_flops,
        share=0,
    )
    g, near_gp = call(
        functools.partial(context_kernel, width, heads),
        "near_context",
        [((lat, all_rows), BF16), ((keys, all_rows), F32)],
        qs + [wuv, near_k],
        share=0,
    )
    mine = add(pair[:heads], after(got_own, near_gp))
    near = swap(mine, *line_hops[0])
    last_s, last_k, stat = call(
        functools.partial(score_kernel, factor, 1, width, heads, True),
        "last_scores",
        [((tok, all_rows), F32), ((tok, wide), BF16), ((EXTRA, tok), F32)],
        [lats[most], q_all, after(near_stat, near_gp), delta],
        [((wide, tok), BF16)],
        flops=score_flops,
    )
    stats = [stat] + [swap(stat, k) for k in range(1, GROUP)]
    (last_gp,) = call(
        prob_kernel,
        "last_context",
        [((tok, all_rows), F32)],
        [last_k, g],
        flops=2 * lines * tok * all_rows * lat + 2 * all_rows * lat * HEAD_DIM,
        share=3,
    )
    mine = add(mine, after(near, stat))
    for step_hop in line_hops[1:-1]:
        mine = add(mine, swap(mine, *step_hop))
    near = swap(mine, *line_hops[-1])
    def block(name, keys_at, s, gp, keep):
        part, pairs = ((width, tok), BF16), ((tok, all_rows), BF16)
        return call(
            functools.partial(block_kernel, factor, keys_at, width, heads),
            name,
            [part, pairs] if keep else [part],
            stats + [s, gp, g, q_all],
            [pairs] if keep else [pairs] * 2,
            flops=2 * tok * all_rows * (width + lat),
        )

    last_part, last_gs = block("last_gradients", slice(None), last_s, last_gp, True)
    last_got = swap(last_part, GROUP)
    (next_part,) = block("next_gradients", slice(tok, 2 * tok), near_s, after(near_gp, last_part), False)
    next_got = swap(next_part, GROUP)
    mine = add(mine, near)
    gq_shape, cut_shape = (heads, width, tok), (heads * width // CUTS, tok)
    gq_own, gq_core, gq_across, *far_cuts, near_gs, near_p = call(
        functools.partial(query_kernel, factor, lines, width, heads),
        "query_gradients",
        [(gq_shape, BF16)] * 3 + [(cut_shape, BF16)] * CUTS + [((keys, all_rows), BF16)] * 2,
        stats + [near_s, near_gp, after(last_gs, mine)] + lats,
        [((width, lines * tok), BF16)],
        flops=2 * lines * tok * all_rows * width,
        share=0,
    )
    across = swap(mine, 2)
    far_cuts = [swap(cut, 1) for cut in far_cuts]
    (gq_sum,) = call(join_kernel, "join", [(gq_shape, BF16)], [after(gq_across, across)] + far_cuts)
    gq_last = swap(gq_sum, 2)
    gq_core = swap(after(gq_core, gq_sum), 1)
    def partials(name, blocks, gs, p, share=1):
        rows = [slice(m * tok, (m + 1) * tok) for m in blocks]
        made = call(
            functools.partial(partial_kernel, factor, rows, width),
            name,
            [((width, tok), BF16)] * len(blocks),
            [g, q_all, gs, p],
            flops=2 * len(blocks) * tok * all_rows * (width + lat),
            share=share,
        )
        return dict(zip(blocks, made))

    middle = lines // 2
    made = partials("middle_gradients", [middle], near_gs, near_p, 3)
    made.update(partials("near_gradients", [m for m in range(most) if m not in (1, middle)], near_gs, after(near_p, *far_cuts)))
    made[1] = next_part
    near_parts = [made[m] for m in range(most)]
    parts = list(near_parts) + [last_part]
    kept = [parts[0]]
    for bit in range(line_bits):
        for m in range(3 << bit, lines, 2 << bit):
            got = last_got if m == most and bit == 0 else swap(parts[m], GROUP << bit)
            parts[m ^ 1 << bit] = add(parts[m ^ 1 << bit], got)
    mine_two = jnp.concatenate([mine, across], axis=0)
    other_two = swap(mine_two, 1)
    pieces = [mine_two[:heads], other_two[:heads], mine_two[heads:], other_two[heads:]]
    kept += [swap(parts[1 << bit], GROUP << bit) for bit in range(1, line_bits)] + [next_got]
    scale = 1.0 / math.sqrt(tok * n_ctx * n_dp)
    (grad_w,) = call(
        functools.partial(spread_kernel, scale),
        "spread",
        [((heads, lat, HEAD_DIM), F32)],
        [idx] + pieces,
        smem=(0,),
    )
    kept[0] = after(kept[0], grad_w)
    (lat_sum,) = call(sum_kernel, "latent_sum", [((width, tok), F32)], kept, flops=3 * 10**9)
    grad_lat, grad_q = call(
        finish_kernel,
        "finish",
        [((width, tok), BF16), ((heads, width, tok), BF16)],
        [lat_sum, gq_own, gq_core, gq_last],
        [((width, tok), BF16), ((heads, width, tok), BF16)],
        copies=1 + heads,
        out=pltpu.HBM,
    )
    return (jnp.transpose(grad_q, (2, 0, 1))[None], grad_lat.T[None], grad_w)


def solution(mesh):
    placed = (
        P("dp", "ctx"),
        P("dp", "ctx", None, None),
        P("dp", "ctx", None),
        P("dp", "ctx", None, None),
        P("dp", "ctx", None, None),
        P(),
    )
    return jax.shard_map(
        functools.partial(body, mesh.shape["ctx"], mesh.shape["dp"]),
        mesh=mesh,
        in_specs=placed,
        out_specs=(P("dp", "ctx", None, None), P("dp", "ctx", None), P()),
        check_vma=False,
    )
```
